32 devices in a mesh: sec: 8 (over y, x, core), term: 4 (over z).
Axes of the slice: x: 2, y: 2, z: 4, core: 2. Of those that a mesh axis runs over, the one named last changes fastest.
Arguments:
- vectors: bfloat16 [2, 8, 4, 256, 256], P(None, 'sec'), may hold values from -6 to 6
- left_ops: bfloat16 [12, 8, 256, 256], P('term', 'sec'), may hold values from -0.375 to 0.375
- right_ops: bfloat16 [12, 8, 256, 256], P('term', 'sec'), may hold values from -0.109375 to 0.109375
- offsets: int32 [12, 4], P('term'), may hold values from 0 to 7, as said below
Outputs:
- products: bfloat16 [2, 8, 4, 256, 256], P(None, 'sec', None, 'term')
- rayleigh: float32 [2, 2], replicated
The draws below stay inside these ranges and needn't reach their ends.
Inputs may be any that keep to these rules, and one draw needn't show every extreme that they name: Each term's 4 offsets are distinct, and every shift from 0 to 7 occurs for some term and pair.
All inputs are finite; a program needn't handle non-finite values.
Results may differ from the reference program's by a relative error of at most 0.015.
Values may be sent and summed in bfloat16 or wider, within the bound.
No kernel may reach another device: no remote copies, remote signals or barrier semaphores. Data moves between devices by JAX's collectives and lax.ppermute only.
A program may use at most 64 MiB of HBM per device.

```python
import jax
import jax.numpy as jnp
from jax import lax

B = 256
P_SIZE = 4
S = 8
TERMS = 12


def draw_offsets(key, part):
    order = jax.random.permutation(key, S).astype(jnp.int32)
    first = jax.random.randint(jax.random.fold_in(key, 3), (), 0, S).astype(jnp.int32)
    positions = ((first + jnp.arange(TERMS * P_SIZE, dtype=jnp.int32)) % S).astype(jnp.int32)
    table = order[positions].reshape(TERMS, P_SIZE)
    row_order = jax.random.permutation(jax.random.fold_in(key, 5), TERMS).astype(jnp.int32)
    return table[row_order].astype(jnp.int32)


def block_scale(rng, extent, shards, low, high):
    loudness = 1.0
    for position, parts in shards:
        steps = jax.random.uniform(jax.random.fold_in(jax.random.fold_in(rng, 6), position), (parts,), jnp.float32, low / len(shards), high / len(shards))
        loudness = loudness * jnp.repeat(jnp.exp(steps), extent[position] // parts).reshape((-1,) + (1,) * (len(extent) - 1 - position))
    return loudness


def gaussian(own_key, shape, deviation, reach, split=(), kind=jnp.bfloat16):
    level = block_scale(own_key, shape, split, -0.22, 0.18) if split else 1.0
    result = jax.random.normal(own_key, shape, jnp.float32) * deviation * level
    return jnp.minimum(jnp.maximum(result, -reach), reach).astype(kind)


def setup_inputs(seed: int = 0) -> dict:
    arg_keys = jax.random.split(jax.random.key(seed), 5)
    vectors = gaussian(arg_keys[0], (2, S, P_SIZE, B, B), 1.0, 6.0, ((1, 8),))
    left_ops = gaussian(arg_keys[1], (TERMS, S, B, B), B ** -0.5, 0.375, ((0, 4), (1, 8)))
    right_ops = gaussian(arg_keys[2], (TERMS, S, B, B), (B * TERMS) ** -0.5, 0.109375, ((0, 4), (1, 8)))
    offsets = draw_offsets(jax.random.fold_in(arg_keys[4], 71), 0)
    return {"vectors": vectors, "left_ops": left_ops, "right_ops": right_ops, "offsets": offsets}


def reference(vectors, left_ops, right_ops, offsets):
    sector_ids = jnp.arange(S, dtype=jnp.int32)
    right_sector = ((sector_ids[None, :, None] + offsets[:, None, :]) % S).astype(jnp.int32)
    wave = vectors.astype(jnp.float32)

    def one_term(running, operands):
        left_block, right_block, sector_table = operands
        inner_part = jnp.einsum('lab,ilpbc->ilpac', left_block.astype(jnp.float32), wave).astype(jnp.bfloat16)
        chosen = right_block[sector_table]
        added = jnp.einsum('ilpac,lpcd->ilpad', inner_part.astype(jnp.float32), chosen.astype(jnp.float32))
        return (running + added, None)
    start_value = jnp.zeros(vectors.shape, jnp.float32)
    products_full, _ = lax.scan(one_term, start_value, (left_ops, right_ops, right_sector))
    gram_matrix = jnp.einsum('ilpab,jlpab->ij', wave, products_full)
    squares = lax.optimization_barrier(jnp.sum(wave * wave, axis=(1, 2, 3, 4)))
    rayleigh = gram_matrix / jnp.sqrt(squares[:, None] * squares[None, :])
    return (products_full.astype(jnp.bfloat16), rayleigh)
```

```python
import functools

import jax
import jax.numpy as jnp
from jax import lax
from jax.experimental import pallas as pl
from jax.experimental.pallas import tpu as pltpu
from jax.sharding import PartitionSpec as P

MIB = 1 << 20
TILE = (8, 128)


def swap(value, axis, mask):
    count = lax.axis_size(axis)
    return lax.ppermute(value, axis, [(place, place ^ mask) for place in range(count)])


def gather_by_mask(own, axis, high_last):
    held = [own]
    for mask in range(1, lax.axis_size(axis)):
        if mask & 1:
            step = 1
        elif high_last:
            step = 1 << (mask.bit_length() - 1)
        else:
            step = mask & -mask
        held.append(swap(held[mask ^ step], axis, step))
    return held


def place_rows(values):
    row = lax.broadcasted_iota(jnp.int32, TILE, 0)
    tile = jnp.zeros(TILE, jnp.float32)
    for position, value in values:
        tile = jnp.where(row == position, value, tile)
    return tile


def total(value):
    return jnp.sum(jnp.sum(value, axis=0, keepdims=True), axis=1, keepdims=True)


def inner_kernel(square_scale, vectors, left, inner, squares):
    terms, states = left.shape[0], left.shape[1]
    stacked = left[...].reshape(terms * states, states)
    sums = []
    for trial in range(vectors.shape[0]):
        square = jnp.zeros((8, states), jnp.float32)
        for pair in range(vectors.shape[1]):
            block = vectors[trial, pair]
            product = jnp.dot(stacked, block, preferred_element_type=jnp.float32)
            inner[:, trial, pair] = product.astype(jnp.bfloat16).reshape(terms, states, states)
            wide = block.astype(jnp.float32)
            square += jnp.sum((wide * wide).reshape(-1, 8, states), axis=0)
        sums.append(total(square) * square_scale)
    trials = len(sums)
    squares[...] = place_rows([(trials * trials + k, value) for k, value in enumerate(sums)])


def sum_kernel(sectors, shares, offsets, vectors, inner, squares, *rest):
    pieces = rest[: 2 * sectors]
    own, *others, tile, rights, partial, sems = rest[2 * sectors :]
    terms, trials, pairs, states, _ = inner.shape
    half = states // 2
    copies = []
    for mask in range(sectors):
        for part in range(2):
            copies.append(
                pltpu.make_async_copy(
                    pieces[2 * mask + part],
                    rights.at[mask, :, pl.ds(part * half, half)],
                    sems.at[2 * mask + part],
                )
            )
    for copy in copies:
        copy.start()
    for copy in copies:
        copy.wait()
    sector = lax.axis_index("sec")
    place = lax.axis_index("term")
    rows = states // shares
    grams = [jnp.zeros((8, states), jnp.float32) for _ in range(trials * trials)]
    for pair in range(pairs):
        result = None
        for term in range(terms):
            wanted = (sector + offsets[term, pair]) & (sectors - 1)
            added = jnp.dot(
                inner[term, :, pair].reshape(trials * states, states),
                rights[sector ^ wanted, term],
                preferred_element_type=jnp.float32,
            )
            result = added if result is None else result + added
        partial[...] = result.reshape(trials, states, states)
        for j in range(trials):
            product = partial[j]
            for i in range(trials):
                spread = vectors[i, pair].astype(jnp.float32) * product
                grams[i * trials + j] += jnp.sum(spread.reshape(-1, 8, states), axis=0)
        for mask in range(shares):
            start = pl.multiple_of((place ^ mask) * rows, rows)
            share = partial[:, pl.ds(start, rows)]
            if mask == 0:
                own[:, pair] = share
            else:
                others[mask - 1][:, pair] = share.astype(jnp.bfloat16)
    tile[...] = squares[...] + place_rows([(k, total(value)) for k, value in enumerate(grams)])


def in_vmem(count):
    return [pl.BlockSpec(memory_space=pltpu.VMEM)] * count


def local(vectors, left_ops, right_ops, offsets):
    sectors = lax.axis_size("sec")
    shares = lax.axis_size("term")
    trials, _, pairs, states, _ = vectors.shape
    terms = left_ops.shape[0]
    vectors, left, right = vectors[:, 0], left_ops[:, 0], right_ops[:, 0]
    half, rows = states // 2, states // shares

    first = gather_by_mask(right[:, :half], "sec", True)
    second = gather_by_mask(right[:, half:], "sec", False)
    pieces = [piece for both in zip(first, second) for piece in both]

    flops = 2 * terms * trials * pairs * states**3
    inner, squares = pl.pallas_call(
        functools.partial(inner_kernel, 1.0 / shares),
        out_shape=(
            jax.ShapeDtypeStruct((terms, trials, pairs, states, states), jnp.bfloat16),
            jax.ShapeDtypeStruct(TILE, jnp.float32),
        ),
        in_specs=in_vmem(2),
        out_specs=tuple(in_vmem(2)),
        compiler_params=pltpu.CompilerParams(vmem_limit_bytes=12 * MIB),
        cost_estimate=pl.CostEstimate(flops=flops, bytes_accessed=5 * MIB, transcendentals=0),
        name="inner_products",
    )(vectors, left)

    share_shape = (trials, pairs, rows, states)
    own, *others, tile = pl.pallas_call(
        functools.partial(sum_kernel, sectors, shares),
        out_shape=(
            jax.ShapeDtypeStruct(share_shape, jnp.float32),
            *[jax.ShapeDtypeStruct(share_shape, jnp.bfloat16)] * (shares - 1),
            jax.ShapeDtypeStruct(TILE, jnp.float32),
        ),
        in_specs=[pl.BlockSpec(memory_space=pltpu.SMEM)]
        + in_vmem(3)
        + [pl.BlockSpec(memory_space=pl.ANY)] * len(pieces),
        out_specs=tuple(in_vmem(shares + 1)),
        scratch_shapes=[
            pltpu.VMEM((sectors, terms, states, states), jnp.bfloat16),
            pltpu.VMEM((trials, states, states), jnp.float32),
            pltpu.SemaphoreType.DMA((2 * sectors,)),
        ],
        compiler_params=pltpu.CompilerParams(
            vmem_limit_bytes=sectors * terms * states * states * 2 + 12 * MIB
        ),
        cost_estimate=pl.CostEstimate(flops=flops, bytes_accessed=8 * MIB, transcendentals=0),
        name="sum_over_terms",
    )(offsets, vectors, inner, squares, *pieces)

    received = [swap(share, "term", mask + 1) for mask, share in enumerate(others)]
    for axis in ("sec", "term"):
        step = 1
        while step < lax.axis_size(axis):
            tile = tile + swap(tile, axis, step)
            step *= 2
    products = own
    for share in received:
        products = products + share.astype(jnp.float32)
    column = tile[:, 0]
    gram = column[: trials * trials].reshape(trials, trials)
    squares = column[trials * trials : trials * trials + trials]
    rayleigh = gram / jnp.sqrt(squares[:, None] * squares[None, :])
    return (products.astype(jnp.bfloat16)[:, None], rayleigh)


def solution(mesh):
    in_specs = (
        P(None, "sec", None, None, None),
        P("term", "sec", None, None),
        P("term", "sec", None, None),
        P("term", None),
    )
    out_specs = (P(None, "sec", None, "term", None), P())
    return jax.shard_map(local, mesh=mesh, in_specs=in_specs, out_specs=out_specs, check_vma=False)
```

```python
import functools

import jax
import jax.numpy as jnp
from jax import lax
from jax.experimental import pallas as pl
from jax.experimental.pallas import tpu as pltpu
from jax.sharding import PartitionSpec as P

MIB = 1 << 20
TILE = (8, 128)
CHUNKS = 2
VMEM = pl.BlockSpec(memory_space=pltpu.VMEM)
SMEM = pl.BlockSpec(memory_space=pltpu.SMEM)
ANY = pl.BlockSpec(memory_space=pl.ANY)


def swap(value, axis, mask):
    count = lax.axis_size(axis)
    return lax.ppermute(value, axis, [(place, place ^ mask) for place in range(count)])


def place_rows(values):
    row = lax.broadcasted_iota(jnp.int32, TILE, 0)
    tile = jnp.zeros(TILE, jnp.float32)
    for position, value in values:
        tile = jnp.where(row == position, value, tile)
    return tile


def total(value):
    return jnp.sum(jnp.sum(value, axis=0, keepdims=True), axis=1, keepdims=True)


def inner_kernel(square_scale, vectors, left, inner, squares):
    terms, states = left.shape[0], left.shape[1]
    stacked = left[...].reshape(terms * states, states)
    sums = []
    for trial in range(vectors.shape[0]):
        square = jnp.zeros((8, states), jnp.float32)
        for pair in range(vectors.shape[1]):
            block = vectors[trial, pair]
            product = jnp.dot(stacked, block, preferred_element_type=jnp.float32)
            inner[:, trial, pair] = product.astype(jnp.bfloat16).reshape(terms, states, states)
            wide = block.astype(jnp.float32)
            square += jnp.sum((wide * wide).reshape(-1, 8, states), axis=0)
        sums.append(total(square) * square_scale)
    trials = len(sums)
    squares[...] = place_rows([(trials * trials + k, value) for k, value in enumerate(sums)])


def sum_kernel(sectors, chunk, offsets, vectors, inner, before, *rest):
    pieces = rest[:sectors]
    keep, send, tile, rights, partial = rest[-5:]
    terms, trials, pairs, states, _ = inner.shape
    width = partial.shape[2]
    shares = 2 * keep.shape[0]
    rows = states // shares
    for mask in range(sectors):
        rights[mask] = pieces[mask][...]
    sector = lax.axis_index("sec")
    place = lax.axis_index("term")
    columns = slice(chunk * width, (chunk + 1) * width)
    grams = [jnp.zeros((8, width), jnp.float32) for _ in range(trials * trials)]
    for pair in range(pairs):
        result = None
        for term in range(terms):
            wanted = (sector + offsets[term, pair]) & (sectors - 1)
            added = jnp.dot(
                inner[term, :, pair].reshape(trials * states, states),
                rights[sector ^ wanted, term],
                preferred_element_type=jnp.float32,
            )
            result = added if result is None else result + added
        partial[...] = result.reshape(trials, states, width)
        for j in range(trials):
            product = partial[j]
            for i in range(trials):
                spread = vectors[i, pair, :, columns].astype(jnp.float32) * product
                grams[i * trials + j] += jnp.sum(spread.reshape(-1, 8, width), axis=0)
        for mask in range(shares):
            start = pl.multiple_of((place ^ mask) * rows, rows)
            share = partial[:, pl.ds(start, rows)]
            if mask & 1:
                send[mask // 2, :, pair] = share.astype(jnp.bfloat16)
            else:
                keep[mask // 2, :, pair] = share
    tile[...] = before[...] + place_rows([(k, total(value)) for k, value in enumerate(grams)])


def halve_kernel(kept, received, keep, send):
    for k in range(kept.shape[0]):
        both = kept[k] + received[k].astype(jnp.float32)
        if k & 1:
            send[k // 2] = both.astype(jnp.bfloat16)
        else:
            keep[k // 2] = both


def finish_kernel(*refs):
    *parts, products = refs
    width = products.shape[-1] // (len(parts) // 2)
    for chunk in range(len(parts) // 2):
        kept, received = parts[2 * chunk : 2 * chunk + 2]
        both = kept[0] + received[0].astype(jnp.float32)
        products[:, :, :, chunk * width : (chunk + 1) * width] = both.astype(jnp.bfloat16)


def rayleigh_kernel(tiles, rayleigh):
    tile = jnp.sum(tiles[...], axis=0)
    trials = rayleigh.shape[0]
    row = lax.broadcasted_iota(jnp.int32, rayleigh.shape, 0)
    column = lax.broadcasted_iota(jnp.int32, rayleigh.shape, 1)

    def entry(position):
        return tile[position : position + 1, :trials]

    result = jnp.zeros(rayleigh.shape, jnp.float32)
    for i in range(trials):
        for j in range(trials):
            squares = entry(trials * trials + i) * entry(trials * trials + j)
            value = entry(i * trials + j) / jnp.sqrt(squares)
            result = jnp.where((row == i) & (column == j), value, result)
    rayleigh[...] = result


def call(kernel, name, flops, moved, limit, **kwargs):
    return pl.pallas_call(
        kernel,
        name=name,
        cost_estimate=pl.CostEstimate(flops=flops, bytes_accessed=moved, transcendentals=0),
        compiler_params=pltpu.CompilerParams(vmem_limit_bytes=limit),
        **kwargs,
    )


def local(vectors, left_ops, right_ops, offsets):
    sectors = lax.axis_size("sec")
    shares = lax.axis_size("term")
    trials, _, pairs, states, _ = vectors.shape
    terms = left_ops.shape[0]
    vectors, left, right = vectors[:, 0], left_ops[:, 0], right_ops[:, 0]
    width, rows = states // CHUNKS, states // shares

    inner, tile = call(
        functools.partial(inner_kernel, 1.0 / shares),
        "inner_products",
        2 * terms * trials * pairs * states**3,
        5 * MIB,
        12 * MIB,
        out_shape=(
            jax.ShapeDtypeStruct((terms, trials, pairs, states, states), jnp.bfloat16),
            jax.ShapeDtypeStruct(TILE, jnp.float32),
        ),
        in_specs=[VMEM, VMEM],
        out_specs=(VMEM, VMEM),
    )(vectors, left)

    gathered = []
    for chunk in range(CHUNKS):
        own = right[:, :, chunk * width : (chunk + 1) * width]
        held = [own] + [swap(own, "sec", mask) for mask in range(2, sectors, 2)]
        if chunk == 0:
            held[1], inner = lax.optimization_barrier((held[1], inner))
        both = []
        for block in held:
            both += [block, swap(block, "sec", 1)]
        gathered.append(both)

    def share_of(count, dtype):
        return jax.ShapeDtypeStruct((count, trials, pairs, rows, width), dtype)

    parts, waited = [], None
    for chunk in range(CHUNKS):
        after = [] if waited is None else [waited]
        keep, send, tile = call(
            functools.partial(sum_kernel, sectors, chunk),
            "sum_over_terms",
            2 * terms * trials * pairs * states * states * width,
            4 * MIB,
            sectors * terms * states * width * 2 + 12 * MIB,
            out_shape=(
                share_of(shares // 2, jnp.float32),
                share_of(shares // 2, jnp.bfloat16),
                jax.ShapeDtypeStruct(TILE, jnp.float32),
            ),
            in_specs=[SMEM, VMEM, VMEM, VMEM] + [VMEM] * sectors + [ANY] * len(after),
            out_specs=(VMEM, VMEM, VMEM),
            scratch_shapes=[
                pltpu.VMEM((sectors, terms, states, width), jnp.bfloat16),
                pltpu.VMEM((trials, states, width), jnp.float32),
            ],
        )(offsets, vectors, inner, tile, *gathered[chunk], *after)
        step = 1
        waited = received = swap(send, "term", step)
        while 2 * step < shares:
            step *= 2
            count = shares // (2 * step)
            keep, send = call(
                halve_kernel,
                "halve_rows",
                1,
                1,
                8 * MIB,
                out_shape=(share_of(count, jnp.float32), share_of(count, jnp.bfloat16)),
                in_specs=[VMEM, VMEM],
                out_specs=(VMEM, VMEM),
            )(keep, received)
            received = swap(send, "term", step)
        parts += [keep, received]

    tiles = jnp.broadcast_to(tile[None], (sectors * shares, *TILE))
    tiles = lax.all_to_all(tiles, ("sec", "term"), 0, 0, tiled=True)
    rayleigh = call(
        rayleigh_kernel,
        "rayleigh",
        1,
        1,
        8 * MIB,
        out_shape=jax.ShapeDtypeStruct((trials, trials), jnp.float32),
        in_specs=[VMEM],
        out_specs=VMEM,
    )(tiles)
    products = call(
        finish_kernel,
        "add_last_share",
        1,
        1,
        8 * MIB,
        out_shape=jax.ShapeDtypeStruct((trials, pairs, rows, states), jnp.bfloat16),
        in_specs=[VMEM] * len(parts),
        out_specs=VMEM,
    )(*parts)
    return (products[:, None], rayleigh)


def solution(mesh):
    in_specs = (
        P(None, "sec", None, None, None),
        P("term", "sec", None, None),
        P("term", "sec", None, None),
        P("term", None),
    )
    out_specs = (P(None, "sec", None, "term", None), P())
    return jax.shard_map(local, mesh=mesh, in_specs=in_specs, out_specs=out_specs, check_vma=False)
```

```python
import functools

import jax
import jax.numpy as jnp
from jax import lax
from jax.experimental import pallas as pl
from jax.experimental.pallas import tpu as pltpu
from jax.sharding import PartitionSpec as P

MIB = 1 << 20
TILE = (8, 128)
CHUNKS = 2
VMEM = pl.BlockSpec(memory_space=pltpu.VMEM)
SMEM = pl.BlockSpec(memory_space=pltpu.SMEM)
HBM = pl.BlockSpec(memory_space=pltpu.HBM)


def swap(value, axis, mask, count=None):
    masks = [mask, mask] if count is None else [turned(mask, parity, count) for parity in range(2)]
    places = range(lax.axis_size(axis))
    return lax.ppermute(value, axis, [(place, place ^ masks[place & 1]) for place in places])


def turned(mask, parity, count):
    bits = count.bit_length() - 1
    if not parity:
        return mask
    return sum(1 << (bits - bit) for bit in range(1, bits) if mask >> bit & 1) | mask & 1


def gather_sectors(own, sectors, after):
    held = {0: own}
    for mask in range(2, sectors, 2):
        step = 1 << (mask.bit_length() - 1)
        held[mask] = swap(held[mask ^ step], "sec", step, sectors)
    blocks = []
    for mask, block in held.items():
        sent = block
        if mask == 2:
            sent = after(block)
        blocks += [block, swap(sent, "sec", 1)]
    return blocks


def place_rows(values):
    row = lax.broadcasted_iota(jnp.int32, TILE, 0)
    tile = jnp.zeros(TILE, jnp.float32)
    for position, value in values:
        tile = jnp.where(row == position, value, tile)
    return tile


def total(value):
    return jnp.sum(jnp.sum(value, axis=0, keepdims=True), axis=1, keepdims=True)


def inner_kernel(square_scale, vectors_hbm, left_hbm, inner, squares, vectors, left, sems):
    terms, states = left.shape[0], left.shape[1]
    pairs = vectors.shape[1]
    fetch_left = pltpu.make_async_copy(left_hbm, left, sems.at[vectors.shape[0] * pairs])
    fetch_left.start()
    fetches = []
    for trial in range(vectors.shape[0]):
        for pair in range(pairs):
            fetch = pltpu.make_async_copy(
                vectors_hbm.at[trial, pair], vectors.at[trial, pair], sems.at[trial * pairs + pair]
            )
            fetch.start()
            fetches.append(fetch)
    fetch_left.wait()
    stacked = left[...].reshape(terms * states, states)
    sums = []
    for trial in range(vectors.shape[0]):
        square = jnp.zeros((8, states), jnp.float32)
        for pair in range(vectors.shape[1]):
            fetches[trial * pairs + pair].wait()
            block = vectors[trial, pair]
            product = jnp.dot(stacked, block, preferred_element_type=jnp.float32)
            inner[:, trial, pair] = product.astype(jnp.bfloat16).reshape(terms, states, states)
            wide = block.astype(jnp.float32)
            square += jnp.sum((wide * wide).reshape(-1, 8, states), axis=0)
        sums.append(total(square) * square_scale)
    trials = len(sums)
    squares[...] = place_rows([(trials * trials + k, value) for k, value in enumerate(sums)])


def sum_kernel(sectors, chunk, offsets, vectors, inner, before, *rest):
    pieces = rest[:sectors]
    keep, send, tile, rights, partial = rest[sectors:]
    terms, trials, pairs, states, _ = inner.shape
    width = partial.shape[2]
    shares = 2 * keep.shape[0]
    rows = states // shares
    sector = lax.axis_index("sec")
    odd = sector & 1
    for mask in range(0, sectors, 2):
        even_place, odd_place = turned(mask, 0, sectors), turned(mask, 1, sectors)
        rights[jnp.where(odd == 1, odd_place, even_place)] = pieces[mask][...]
        rights[jnp.where(odd == 1, even_place, odd_place) ^ 1] = pieces[mask + 1][...]
    place = lax.axis_index("term")
    columns = slice(chunk * width, (chunk + 1) * width)
    grams = [jnp.zeros((8, width), jnp.float32) for _ in range(trials * trials)]
    for pair in range(pairs):
        result = None
        for term in range(terms):
            wanted = (sector + offsets[term, pair]) & (sectors - 1)
            added = jnp.dot(
                inner[term, :, pair].reshape(trials * states, states),
                rights[sector ^ wanted, term],
                preferred_element_type=jnp.float32,
            )
            result = added if result is None else result + added
        partial[...] = result.reshape(trials, states, width)
        for j in range(trials):
            product = partial[j]
            for i in range(trials):
                spread = vectors[i, pair, :, columns].astype(jnp.float32) * product
                grams[i * trials + j] += jnp.sum(spread.reshape(-1, 8, width), axis=0)
        for mask in range(shares):
            start = pl.multiple_of((place ^ mask) * rows, rows)
            share = partial[:, pl.ds(start, rows)]
            if mask & 1:
                send[mask // 2, :, pair] = share.astype(jnp.bfloat16)
            else:
                keep[mask // 2, :, pair] = share
    tile[...] = before[...] + place_rows([(k, total(value)) for k, value in enumerate(grams)])


def halve_kernel(kept, received, keep, send):
    for k in range(kept.shape[0]):
        both = kept[k] + received[k].astype(jnp.float32)
        if k & 1:
            send[k // 2] = both.astype(jnp.bfloat16)
        else:
            keep[k // 2] = both


def finish_kernel(*refs):
    *parts, products = refs
    width = products.shape[-1] // (len(parts) // 2)
    for chunk in range(len(parts) // 2):
        kept, received = parts[2 * chunk : 2 * chunk + 2]
        both = kept[0] + received[0].astype(jnp.float32)
        products[:, :, :, chunk * width : (chunk + 1) * width] = both.astype(jnp.bfloat16)


def rayleigh_kernel(*refs):
    *tiles, rayleigh = refs
    tile = sum(part[...] for part in tiles)
    trials = rayleigh.shape[0]
    row = lax.broadcasted_iota(jnp.int32, rayleigh.shape, 0)
    column = lax.broadcasted_iota(jnp.int32, rayleigh.shape, 1)

    def entry(position):
        return tile[position : position + 1, :trials]

    result = jnp.zeros(rayleigh.shape, jnp.float32)
    for i in range(trials):
        for j in range(trials):
            squares = entry(trials * trials + i) * entry(trials * trials + j)
            value = entry(i * trials + j) / jnp.sqrt(squares)
            result = jnp.where((row == i) & (column == j), value, result)
    rayleigh[...] = result


def in_hbm(value):
    return pltpu.with_memory_space_constraint(value, pltpu.HBM)


def add_places(tile, axis):
    step, other = 1, None
    while step < lax.axis_size(axis):
        tile = tile if other is None else tile + other
        other = swap(tile, axis, step)
        step *= 2
    return tile, other


def call(kernel, name, flops, moved, limit, **kwargs):
    return pl.pallas_call(
        kernel,
        name=name,
        cost_estimate=pl.CostEstimate(flops=flops, bytes_accessed=moved, transcendentals=0),
        compiler_params=pltpu.CompilerParams(vmem_limit_bytes=limit),
        **kwargs,
    )


def local(vectors, left_ops, right_ops, offsets):
    sectors = lax.axis_size("sec")
    shares = lax.axis_size("term")
    trials, _, pairs, states, _ = vectors.shape
    terms = left_ops.shape[0]
    vectors, left, right = vectors[:, 0], left_ops[:, 0], right_ops[:, 0]
    width, rows = states // CHUNKS, states // shares

    inner, tile = call(
        functools.partial(inner_kernel, 1.0 / shares),
        "inner_products",
        2 * terms * trials * pairs * states**3,
        5 * MIB,
        12 * MIB,
        out_shape=(
            jax.ShapeDtypeStruct((terms, trials, pairs, states, states), jnp.bfloat16),
            jax.ShapeDtypeStruct(TILE, jnp.float32),
        ),
        in_specs=[HBM, HBM],
        out_specs=(VMEM, VMEM),
        scratch_shapes=[
            pltpu.VMEM(vectors.shape, jnp.bfloat16),
            pltpu.VMEM(left.shape, jnp.bfloat16),
            pltpu.SemaphoreType.DMA((trials * pairs + 1,)),
        ],
    )(in_hbm(vectors), in_hbm(left))

    def behind_inner(block):
        return lax.optimization_barrier((block, inner))[0]

    gathered = []
    for chunk in range(CHUNKS):
        own = right[:, :, chunk * width : (chunk + 1) * width]
        after = behind_inner if chunk == 0 else lambda block: block
        gathered.append(gather_sectors(own, sectors, after))

    def share_of(count, dtype):
        return jax.ShapeDtypeStruct((count, trials, pairs, rows, width), dtype)

    parts, arrived = [], None
    for chunk in range(CHUNKS):
        keep, send, tile = call(
            functools.partial(sum_kernel, sectors, chunk),
            "sum_over_terms",
            2 * terms * trials * pairs * states * states * width,
            4 * MIB,
            sectors * terms * states * width * 2 + 12 * MIB,
            out_shape=(
                share_of(shares // 2, jnp.float32),
                share_of(shares // 2, jnp.bfloat16),
                jax.ShapeDtypeStruct(TILE, jnp.float32),
            ),
            in_specs=[SMEM, VMEM, VMEM, VMEM] + [VMEM] * sectors,
            out_specs=(VMEM, VMEM, VMEM),
            scratch_shapes=[
                pltpu.VMEM((sectors, terms, states, width), jnp.bfloat16),
                pltpu.VMEM((trials, states, width), jnp.float32),
            ],
        )(offsets, vectors, inner, tile, *gathered[chunk])
        if arrived is not None:
            send, arrived = lax.optimization_barrier((send, arrived))
        step = 1
        arrived = received = swap(send, "term", step)
        if chunk == CHUNKS - 1:
            tile, other = add_places(tile, "sec")
            tile = tile + other
            received, tile = lax.optimization_barrier((received, tile))
        while 2 * step < shares:
            step *= 2
            count = shares // (2 * step)
            keep, send = call(
                halve_kernel,
                "halve_rows",
                1,
                1,
                8 * MIB,
                out_shape=(share_of(count, jnp.float32), share_of(count, jnp.bfloat16)),
                in_specs=[VMEM, VMEM],
                out_specs=(VMEM, VMEM),
            )(keep, received)
            received = swap(send, "term", step)
        parts += [keep, received]

    tiles = add_places(tile, "term")
    rayleigh = call(
        rayleigh_kernel,
        "rayleigh",
        1,
        1,
        8 * MIB,
        out_shape=jax.ShapeDtypeStruct((trials, trials), jnp.float32),
        in_specs=[VMEM] * len(tiles),
        out_specs=VMEM,
    )(*tiles)
    products = call(
        finish_kernel,
        "add_last_share",
        1,
        1,
        8 * MIB,
        out_shape=jax.ShapeDtypeStruct((trials, pairs, rows, states), jnp.bfloat16),
        in_specs=[VMEM] * len(parts),
        out_specs=VMEM,
    )(*parts)
    return (products[:, None], rayleigh)


def solution(mesh):
    in_specs = (
        P(None, "sec", None, None, None),
        P("term", "sec", None, None),
        P("term", "sec", None, None),
        P("term", None),
    )
    out_specs = (P(None, "sec", None, "term", None), P())
    return jax.shard_map(local, mesh=mesh, in_specs=in_specs, out_specs=out_specs, check_vma=False)
```

```python
import functools

import jax
import jax.numpy as jnp
from jax import lax
from jax.experimental import pallas as pl
from jax.experimental.pallas import tpu as pltpu
from jax.sharding import PartitionSpec as P

MIB = 1 << 20
TILE = (8, 128)
CHUNKS = 2
VMEM = pl.BlockSpec(memory_space=pltpu.VMEM)
SMEM = pl.BlockSpec(memory_space=pltpu.SMEM)
HBM = pl.BlockSpec(memory_space=pltpu.HBM)


def swap(value, axis, mask, count=None):
    masks = [mask, mask] if count is None else [turned(mask, parity, count) for parity in range(2)]
    places = range(lax.axis_size(axis))
    return lax.ppermute(value, axis, [(place, place ^ masks[place & 1]) for place in places])


def turned(mask, parity, count):
    bits = count.bit_length() - 1
    if not parity:
        return mask
    return sum(1 << (bits - bit) for bit in range(1, bits) if mask >> bit & 1) | mask & 1


def gather_sectors(own, sectors, after):
    held = {0: own}
    for mask in range(2, sectors, 2):
        step = 1 << (mask.bit_length() - 1)
        held[mask] = swap(held[mask ^ step], "sec", step, sectors)
        if mask == 2:
            held[mask] = after(held[mask])
    return [block for mine in held.values() for block in (mine, swap(mine, "sec", 1))]


def place_rows(values):
    row = lax.broadcasted_iota(jnp.int32, TILE, 0)
    tile = jnp.zeros(TILE, jnp.float32)
    for position, value in values:
        tile = jnp.where(row == position, value, tile)
    return tile


def total(value):
    return jnp.sum(jnp.sum(value, axis=0, keepdims=True), axis=1, keepdims=True)


def split_kernel(right, *rest):
    *chunks, sems = rest
    width = chunks[0].shape[2]
    copies = []
    for place, chunk in enumerate(chunks):
        columns = pl.ds(place * width, width)
        copies.append(pltpu.make_async_copy(right.at[:, :, columns], chunk, sems.at[place]))
    for copy in copies:
        copy.start()
    for copy in copies:
        copy.wait()


def inner_kernel(square_scale, vectors, left, inner, squares):
    terms, states = left.shape[0], left.shape[1]
    stacked = left[...].reshape(terms * states, states)
    sums = []
    for trial in range(vectors.shape[0]):
        square = jnp.zeros((8, states), jnp.float32)
        for pair in range(vectors.shape[1]):
            block = vectors[trial, pair]
            product = jnp.dot(stacked, block, preferred_element_type=jnp.float32)
            inner[:, trial, pair] = product.astype(jnp.bfloat16).reshape(terms, states, states)
            wide = block.astype(jnp.float32)
            square += jnp.sum((wide * wide).reshape(-1, 8, states), axis=0)
        sums.append(total(square) * square_scale)
    trials = len(sums)
    squares[...] = place_rows([(trials * trials + k, value) for k, value in enumerate(sums)])


def sum_kernel(sectors, chunk, offsets, vectors, inner, before, *rest):
    pieces = rest[:sectors]
    keep, send, tile, rights, partial = rest[sectors:]
    terms, trials, pairs, states, _ = inner.shape
    width = partial.shape[2]
    shares = 2 * keep.shape[0]
    rows = states // shares
    sector = lax.axis_index("sec")
    odd = sector & 1
    for mask in range(0, sectors, 2):
        even_place, odd_place = turned(mask, 0, sectors), turned(mask, 1, sectors)
        rights[jnp.where(odd == 1, odd_place, even_place)] = pieces[mask][...]
        rights[jnp.where(odd == 1, even_place, odd_place) ^ 1] = pieces[mask + 1][...]
    place = lax.axis_index("term")
    columns = slice(chunk * width, (chunk + 1) * width)
    grams = [jnp.zeros((8, width), jnp.float32) for _ in range(trials * trials)]
    for pair in range(pairs):
        result = None
        for term in range(terms):
            wanted = (sector + offsets[term, pair]) & (sectors - 1)
            added = jnp.dot(
                inner[term, :, pair].reshape(trials * states, states),
                rights[sector ^ wanted, term],
                preferred_element_type=jnp.float32,
            )
            result = added if result is None else result + added
        partial[...] = result.reshape(trials, states, width)
        for j in range(trials):
            product = partial[j]
            for i in range(trials):
                spread = vectors[i, pair, :, columns].astype(jnp.float32) * product
                grams[i * trials + j] += jnp.sum(spread.reshape(-1, 8, width), axis=0)
        for mask in range(shares):
            start = pl.multiple_of((place ^ mask) * rows, rows)
            share = partial[:, pl.ds(start, rows)]
            if mask & 1:
                send[mask // 2, :, pair] = share.astype(jnp.bfloat16)
            else:
                keep[mask // 2, :, pair] = share
    tile[...] = before[...] + place_rows([(k, total(value)) for k, value in enumerate(grams)])


def halve_kernel(kept, received, keep, send):
    for k in range(kept.shape[0]):
        both = kept[k] + received[k].astype(jnp.float32)
        if k & 1:
            send[k // 2] = both.astype(jnp.bfloat16)
        else:
            keep[k // 2] = both


def finish_kernel(*refs):
    *parts, products = refs
    width = products.shape[-1] // (len(parts) // 2)
    for chunk in range(len(parts) // 2):
        kept, received = parts[2 * chunk : 2 * chunk + 2]
        both = kept[0] + received[0].astype(jnp.float32)
        products[:, :, :, chunk * width : (chunk + 1) * width] = both.astype(jnp.bfloat16)


def rayleigh_kernel(*refs):
    *tiles, rayleigh = refs
    tile = sum(part[...] for part in tiles)
    trials = rayleigh.shape[0]
    row = lax.broadcasted_iota(jnp.int32, rayleigh.shape, 0)
    column = lax.broadcasted_iota(jnp.int32, rayleigh.shape, 1)

    def entry(position):
        return tile[position : position + 1, :trials]

    result = jnp.zeros(rayleigh.shape, jnp.float32)
    for i in range(trials):
        for j in range(trials):
            squares = entry(trials * trials + i) * entry(trials * trials + j)
            value = entry(i * trials + j) / jnp.sqrt(squares)
            result = jnp.where((row == i) & (column == j), value, result)
    rayleigh[...] = result


def in_hbm(value):
    return pltpu.with_memory_space_constraint(value, pltpu.HBM)


def add_places(tile, axis, masks):
    parts = [tile] + [swap(tile, axis, mask) for mask in masks]
    return sum(parts[1:], parts[0])


def steps_of(count, low):
    steps = []
    while 1 << low < count:
        unit = 1 << low
        steps.append([unit, 2 * unit, 3 * unit] if 2 * unit < count else [unit])
        low += 2
    return steps


def call(kernel, name, flops, moved, limit, **kwargs):
    return pl.pallas_call(
        kernel,
        name=name,
        cost_estimate=pl.CostEstimate(flops=flops, bytes_accessed=moved, transcendentals=0),
        compiler_params=pltpu.CompilerParams(vmem_limit_bytes=limit),
        **kwargs,
    )


def local(vectors, left_ops, right_ops, offsets):
    sectors = lax.axis_size("sec")
    shares = lax.axis_size("term")
    trials, _, pairs, states, _ = vectors.shape
    terms = left_ops.shape[0]
    vectors, left, right = vectors[:, 0], left_ops[:, 0], right_ops[:, 0]
    width, rows = states // CHUNKS, states // shares

    chunks = call(
        split_kernel,
        "split_columns",
        2 * terms * trials * pairs * states**3,
        2 * MIB,
        4 * MIB,
        out_shape=[jax.ShapeDtypeStruct((terms, states, width), jnp.bfloat16)] * CHUNKS,
        in_specs=[HBM],
        out_specs=[VMEM] * CHUNKS,
        scratch_shapes=[pltpu.SemaphoreType.DMA((CHUNKS,))],
    )(in_hbm(right))

    inner, tile = call(
        functools.partial(inner_kernel, 1.0 / shares),
        "inner_products",
        2 * terms * trials * pairs * states**3,
        5 * MIB,
        12 * MIB,
        out_shape=(
            jax.ShapeDtypeStruct((terms, trials, pairs, states, states), jnp.bfloat16),
            jax.ShapeDtypeStruct(TILE, jnp.float32),
        ),
        in_specs=[VMEM, VMEM],
        out_specs=(VMEM, VMEM),
    )(vectors, left)

    def behind_inner(block):
        return lax.optimization_barrier((block, inner))[0]

    gathered = []
    for chunk in range(CHUNKS):
        after = behind_inner if chunk == 0 else lambda block: block
        gathered.append(gather_sectors(chunks[chunk], sectors, after))

    def share_of(count, dtype):
        return jax.ShapeDtypeStruct((count, trials, pairs, rows, width), dtype)

    parts, arrived = [], None
    for chunk in range(CHUNKS):
        keep, send, tile = call(
            functools.partial(sum_kernel, sectors, chunk),
            "sum_over_terms",
            2 * terms * trials * pairs * states * states * width,
            4 * MIB,
            sectors * terms * states * width * 2 + 12 * MIB,
            out_shape=(
                share_of(shares // 2, jnp.float32),
                share_of(shares // 2, jnp.bfloat16),
                jax.ShapeDtypeStruct(TILE, jnp.float32),
            ),
            in_specs=[SMEM, VMEM, VMEM, VMEM] + [VMEM] * sectors,
            out_specs=(VMEM, VMEM, VMEM),
            scratch_shapes=[
                pltpu.VMEM((sectors, terms, states, width), jnp.bfloat16),
                pltpu.VMEM((trials, states, width), jnp.float32),
            ],
        )(offsets, vectors, inner, tile, *gathered[chunk])
        if arrived is not None:
            send, arrived = lax.optimization_barrier((send, arrived))
        step = 1
        arrived = received = swap(send, "term", step)
        if chunk == CHUNKS - 1:
            for masks in [[1]] + steps_of(sectors, 1):
                tile = add_places(tile, "sec", masks)
            others = tuple(parts[1::2])
            received, tile, others = lax.optimization_barrier((received, tile, others))
            parts[1::2] = others
        while 2 * step < shares:
            step *= 2
            count = shares // (2 * step)
            keep, send = call(
                halve_kernel,
                "halve_rows",
                1,
                1,
                8 * MIB,
                out_shape=(share_of(count, jnp.float32), share_of(count, jnp.bfloat16)),
                in_specs=[VMEM, VMEM],
                out_specs=(VMEM, VMEM),
            )(keep, received)
            received = swap(send, "term", step)
        parts += [keep, received]

    *steps, last = steps_of(shares, 0)
    for masks in steps:
        tile = add_places(tile, "term", masks)
    tiles = [tile] + [swap(tile, "term", mask) for mask in last]
    rayleigh = call(
        rayleigh_kernel,
        "rayleigh",
        1,
        1,
        8 * MIB,
        out_shape=jax.ShapeDtypeStruct((trials, trials), jnp.float32),
        in_specs=[VMEM] * len(tiles),
        out_specs=VMEM,
    )(*tiles)
    products = call(
        finish_kernel,
        "add_last_share",
        1,
        1,
        8 * MIB,
        out_shape=jax.ShapeDtypeStruct((trials, pairs, rows, states), jnp.bfloat16),
        in_specs=[VMEM] * len(parts),
        out_specs=VMEM,
    )(*parts)
    return (products[:, None], rayleigh)


def solution(mesh):
    in_specs = (
        P(None, "sec", None, None, None),
        P("term", "sec", None, None),
        P("term", "sec", None, None),
        P("term", None),
    )
    out_specs = (P(None, "sec", None, "term", None), P())
    return jax.shard_map(local, mesh=mesh, in_specs=in_specs, out_specs=out_specs, check_vma=False)
```

```python
import functools

import jax
import jax.numpy as jnp
from jax import lax
from jax.experimental import pallas as pl
from jax.experimental.pallas import tpu as pltpu
from jax.sharding import PartitionSpec as P

MIB = 1 << 20
TILE = (8, 128)
CHUNKS = 2
VMEM = pl.BlockSpec(memory_space=pltpu.VMEM)
SMEM = pl.BlockSpec(memory_space=pltpu.SMEM)
HBM = pl.BlockSpec(memory_space=pltpu.HBM)


def swap(value, axis, mask, count=None):
    masks = [mask, mask] if count is None else [turned(mask, parity, count) for parity in range(2)]
    places = range(lax.axis_size(axis))
    return lax.ppermute(value, axis, [(place, place ^ masks[place & 1]) for place in places])


def turned(mask, parity, count):
    bits = count.bit_length() - 1
    if not parity:
        return mask
    return sum(1 << (bits - bit) for bit in range(1, bits) if mask >> bit & 1) | mask & 1


def gather_sectors(own, sectors, after):
    held = {0: own}
    for mask in range(2, sectors, 2):
        step = 1 << (mask.bit_length() - 1)
        held[mask] = swap(held[mask ^ step], "sec", step, sectors)
        if mask == 2:
            held[mask] = after(held[mask])
    return [block for mine in held.values() for block in (mine, swap(mine, "sec", 1))]


def place_rows(values):
    row = lax.broadcasted_iota(jnp.int32, TILE, 0)
    tile = jnp.zeros(TILE, jnp.float32)
    for position, value in values:
        tile = jnp.where(row == position, value, tile)
    return tile


def total(value):
    return jnp.sum(jnp.sum(value, axis=0, keepdims=True), axis=1, keepdims=True)


def split_kernel(right, *rest):
    *chunks, sems = rest
    width = chunks[0].shape[2]
    copies = []
    for place, chunk in enumerate(chunks):
        columns = pl.ds(place * width, width)
        copies.append(pltpu.make_async_copy(right.at[:, :, columns], chunk, sems.at[place]))
    for copy in copies:
        copy.start()
    for copy in copies:
        copy.wait()


def inner_kernel(square_scale, vectors, left, inner, squares):
    terms, states = left.shape[0], left.shape[1]
    stacked = left[...].reshape(terms * states, states)
    sums = []
    for trial in range(vectors.shape[0]):
        square = jnp.zeros((8, states), jnp.float32)
        for pair in range(vectors.shape[1]):
            block = vectors[trial, pair]
            product = jnp.dot(stacked, block, preferred_element_type=jnp.float32)
            inner[:, trial, pair] = product.astype(jnp.bfloat16).reshape(terms, states, states)
            wide = block.astype(jnp.float32)
            square += jnp.sum((wide * wide).reshape(-1, 8, states), axis=0)
        sums.append(total(square) * square_scale)
    trials = len(sums)
    squares[...] = place_rows([(trials * trials + k, value) for k, value in enumerate(sums)])


def sum_kernel(sectors, chunk, offsets, vectors, inner, before, *rest):
    pieces = rest[:sectors]
    shares, tile, rights, partial = rest[sectors:]
    terms, trials, pairs, states, _ = inner.shape
    width = partial.shape[2]
    rows = shares.shape[3]
    sector = lax.axis_index("sec")
    odd = sector & 1
    for mask in range(0, sectors, 2):
        even_place, odd_place = turned(mask, 0, sectors), turned(mask, 1, sectors)
        rights[jnp.where(odd == 1, odd_place, even_place)] = pieces[mask][...]
        rights[jnp.where(odd == 1, even_place, odd_place) ^ 1] = pieces[mask + 1][...]
    columns = slice(chunk * width, (chunk + 1) * width)
    grams = [jnp.zeros((8, width), jnp.float32) for _ in range(trials * trials)]
    for pair in range(pairs):
        result = None
        for term in range(terms):
            wanted = (sector + offsets[term, pair]) & (sectors - 1)
            added = jnp.dot(
                inner[term, :, pair].reshape(trials * states, states),
                rights[sector ^ wanted, term],
                preferred_element_type=jnp.float32,
            )
            result = added if result is None else result + added
        partial[...] = result.reshape(trials, states, width)
        for j in range(trials):
            product = partial[j]
            for i in range(trials):
                spread = vectors[i, pair, :, columns].astype(jnp.float32) * product
                grams[i * trials + j] += jnp.sum(spread.reshape(-1, 8, width), axis=0)
        for place in range(shares.shape[0]):
            share = partial[:, place * rows : (place + 1) * rows]
            shares[place, :, pair] = share.astype(jnp.bfloat16)
    tile[...] = before[...] + place_rows([(k, total(value)) for k, value in enumerate(grams)])


def add_kernel(*refs):
    *parts, products = refs
    width = products.shape[-1] // len(parts)
    for chunk, part in enumerate(parts):
        both = part[0].astype(jnp.float32)
        for place in range(1, part.shape[0]):
            both = both + part[place].astype(jnp.float32)
        products[:, :, :, chunk * width : (chunk + 1) * width] = both.astype(jnp.bfloat16)


def rayleigh_kernel(*refs):
    *tiles, rayleigh = refs
    tile = sum(part[...] for part in tiles)
    trials = rayleigh.shape[0]
    row = lax.broadcasted_iota(jnp.int32, rayleigh.shape, 0)
    column = lax.broadcasted_iota(jnp.int32, rayleigh.shape, 1)

    def entry(position):
        return tile[position : position + 1, :trials]

    result = jnp.zeros(rayleigh.shape, jnp.float32)
    for i in range(trials):
        for j in range(trials):
            squares = entry(trials * trials + i) * entry(trials * trials + j)
            value = entry(i * trials + j) / jnp.sqrt(squares)
            result = jnp.where((row == i) & (column == j), value, result)
    rayleigh[...] = result


def in_hbm(value):
    return pltpu.with_memory_space_constraint(value, pltpu.HBM)


def add_places(tile, axis, masks):
    parts = [tile] + [swap(tile, axis, mask) for mask in masks]
    return sum(parts[1:], parts[0])


def steps_of(count, low):
    steps = []
    while 1 << low < count:
        unit = 1 << low
        steps.append([unit, 2 * unit, 3 * unit] if 2 * unit < count else [unit])
        low += 2
    return steps


def call(kernel, name, flops, moved, limit, **kwargs):
    return pl.pallas_call(
        kernel,
        name=name,
        cost_estimate=pl.CostEstimate(flops=flops, bytes_accessed=moved, transcendentals=0),
        compiler_params=pltpu.CompilerParams(vmem_limit_bytes=limit),
        **kwargs,
    )


def local(vectors, left_ops, right_ops, offsets):
    sectors = lax.axis_size("sec")
    shares = lax.axis_size("term")
    trials, _, pairs, states, _ = vectors.shape
    terms = left_ops.shape[0]
    vectors, left, right = vectors[:, 0], left_ops[:, 0], right_ops[:, 0]
    width, rows = states // CHUNKS, states // shares

    chunks = call(
        split_kernel,
        "split_columns",
        2 * terms * trials * pairs * states**3,
        2 * MIB,
        4 * MIB,
        out_shape=[jax.ShapeDtypeStruct((terms, states, width), jnp.bfloat16)] * CHUNKS,
        in_specs=[HBM],
        out_specs=[VMEM] * CHUNKS,
        scratch_shapes=[pltpu.SemaphoreType.DMA((CHUNKS,))],
    )(in_hbm(right))

    inner, tile = call(
        functools.partial(inner_kernel, 1.0 / shares),
        "inner_products",
        2 * terms * trials * pairs * states**3,
        5 * MIB,
        12 * MIB,
        out_shape=(
            jax.ShapeDtypeStruct((terms, trials, pairs, states, states), jnp.bfloat16),
            jax.ShapeDtypeStruct(TILE, jnp.float32),
        ),
        in_specs=[VMEM, VMEM],
        out_specs=(VMEM, VMEM),
    )(vectors, left)

    def behind_inner(block):
        return lax.optimization_barrier((block, inner))[0]

    gathered = []
    for chunk in range(CHUNKS):
        after = behind_inner if chunk == 0 else lambda block: block
        gathered.append(gather_sectors(chunks[chunk], sectors, after))

    parts = []
    for chunk in range(CHUNKS):
        sent, tile = call(
            functools.partial(sum_kernel, sectors, chunk),
            "sum_over_terms",
            2 * terms * trials * pairs * states * states * width,
            4 * MIB,
            sectors * terms * states * width * 2 + 12 * MIB,
            out_shape=(
                jax.ShapeDtypeStruct((shares, trials, pairs, rows, width), jnp.bfloat16),
                jax.ShapeDtypeStruct(TILE, jnp.float32),
            ),
            in_specs=[SMEM, VMEM, VMEM, VMEM] + [VMEM] * sectors,
            out_specs=(VMEM, VMEM),
            scratch_shapes=[
                pltpu.VMEM((sectors, terms, states, width), jnp.bfloat16),
                pltpu.VMEM((trials, states, width), jnp.float32),
            ],
        )(offsets, vectors, inner, tile, *gathered[chunk])
        parts.append(lax.all_to_all(sent, "term", 0, 0, tiled=True))

    for masks in [[1]] + steps_of(sectors, 1):
        tile = add_places(tile, "sec", masks)
    *steps, last = steps_of(shares, 0)
    for masks in steps:
        tile = add_places(tile, "term", masks)
    tiles = [tile] + [swap(tile, "term", mask) for mask in last]
    rayleigh = call(
        rayleigh_kernel,
        "rayleigh",
        1,
        1,
        8 * MIB,
        out_shape=jax.ShapeDtypeStruct((trials, trials), jnp.float32),
        in_specs=[VMEM] * len(tiles),
        out_specs=VMEM,
    )(*tiles)
    products = call(
        add_kernel,
        "add_shares",
        1,
        1,
        8 * MIB,
        out_shape=jax.ShapeDtypeStruct((trials, pairs, rows, states), jnp.bfloat16),
        in_specs=[VMEM] * len(parts),
        out_specs=VMEM,
    )(*parts)
    return (products[:, None], rayleigh)


def solution(mesh):
    in_specs = (
        P(None, "sec", None, None, None),
        P("term", "sec", None, None),
        P("term", "sec", None, None),
        P("term", None),
    )
    out_specs = (P(None, "sec", None, "term", None), P())
    return jax.shard_map(local, mesh=mesh, in_specs=in_specs, out_specs=out_specs, check_vma=False)
```

```python
import functools

import jax
import jax.numpy as jnp
from jax import lax
from jax.experimental import pallas as pl
from jax.experimental.pallas import tpu as pltpu
from jax.sharding import PartitionSpec as P

MIB = 1 << 20
TILE = (8, 128)
CHUNKS = 2
VMEM = pl.BlockSpec(memory_space=pltpu.VMEM)
SMEM = pl.BlockSpec(memory_space=pltpu.SMEM)
HBM = pl.BlockSpec(memory_space=pltpu.HBM)


def swap(value, axis, mask, count=None):
    masks = [mask, mask] if count is None else [turned(mask, parity, count) for parity in range(2)]
    places = range(lax.axis_size(axis))
    return lax.ppermute(value, axis, [(place, place ^ masks[place & 1]) for place in places])


def turned(mask, parity, count):
    bits = count.bit_length() - 1
    if not parity:
        return mask
    return sum(1 << (bits - bit) for bit in range(1, bits) if mask >> bit & 1) | mask & 1


def gather_sectors(own, sectors, after):
    held = {0: own}
    for mask in range(2, sectors, 2):
        step = 1 << (mask.bit_length() - 1)
        held[mask] = swap(held[mask ^ step], "sec", step, sectors)
        if mask == 2:
            held[mask] = after(held[mask])
    return [block for mine in held.values() for block in (mine, swap(mine, "sec", 1))]


def place_rows(values):
    row = lax.broadcasted_iota(jnp.int32, TILE, 0)
    tile = jnp.zeros(TILE, jnp.float32)
    for position, value in values:
        tile = jnp.where(row == position, value, tile)
    return tile


def total(value):
    return jnp.sum(jnp.sum(value, axis=0, keepdims=True), axis=1, keepdims=True)


def inner_kernel(square_scale, vectors, left, right_hbm, inner, squares, right, sem):
    fetch = pltpu.make_async_copy(right_hbm, right, sem)
    fetch.start()
    terms, states = left.shape[0], left.shape[1]
    stacked = left[...].reshape(terms * states, states)
    sums = []
    for trial in range(vectors.shape[0]):
        square = jnp.zeros((8, states), jnp.float32)
        for pair in range(vectors.shape[1]):
            block = vectors[trial, pair]
            product = jnp.dot(stacked, block, preferred_element_type=jnp.float32)
            inner[:, trial, pair] = product.astype(jnp.bfloat16).reshape(terms, states, states)
            wide = block.astype(jnp.float32)
            square += jnp.sum((wide * wide).reshape(-1, 8, states), axis=0)
        sums.append(total(square) * square_scale)
    trials = len(sums)
    squares[...] = place_rows([(trials * trials + k, value) for k, value in enumerate(sums)])
    fetch.wait()


def sum_kernel(sectors, chunk, offsets, vectors, inner, before, *rest):
    pieces = rest[:sectors]
    keep, send, tile, rights, partial = rest[sectors:]
    terms, trials, pairs, states, _ = inner.shape
    width = partial.shape[2]
    shares = 2 * keep.shape[0]
    rows = states // shares
    sector = lax.axis_index("sec")
    odd = sector & 1
    columns = slice(chunk * width, (chunk + 1) * width)
    for mask in range(0, sectors, 2):
        even_place, odd_place = turned(mask, 0, sectors), turned(mask, 1, sectors)
        rights[jnp.where(odd == 1, odd_place, even_place)] = pieces[mask][:, :, columns]
        rights[jnp.where(odd == 1, even_place, odd_place) ^ 1] = pieces[mask + 1][:, :, columns]
    place = lax.axis_index("term")
    grams = [jnp.zeros((8, width), jnp.float32) for _ in range(trials * trials)]
    for pair in range(pairs):
        result = None
        for term in range(terms):
            wanted = (sector + offsets[term, pair]) & (sectors - 1)
            added = jnp.dot(
                inner[term, :, pair].reshape(trials * states, states),
                rights[sector ^ wanted, term],
                preferred_element_type=jnp.float32,
            )
            result = added if result is None else result + added
        partial[...] = result.reshape(trials, states, width)
        for j in range(trials):
            product = partial[j]
            for i in range(trials):
                spread = vectors[i, pair, :, columns].astype(jnp.float32) * product
                grams[i * trials + j] += jnp.sum(spread.reshape(-1, 8, width), axis=0)
        for mask in range(shares):
            start = pl.multiple_of((place ^ mask) * rows, rows)
            share = partial[:, pl.ds(start, rows)]
            if mask & 1:
                send[mask // 2, :, pair] = share.astype(jnp.bfloat16)
            else:
                keep[mask // 2, :, pair] = share
    tile[...] = before[...] + place_rows([(k, total(value)) for k, value in enumerate(grams)])


def halve_kernel(kept, received, keep, send):
    for k in range(kept.shape[0]):
        both = kept[k] + received[k].astype(jnp.float32)
        if k & 1:
            send[k // 2] = both.astype(jnp.bfloat16)
        else:
            keep[k // 2] = both


def finish_kernel(*refs):
    *parts, products = refs
    width = products.shape[-1] // (len(parts) // 2)
    for chunk in range(len(parts) // 2):
        kept, received = parts[2 * chunk : 2 * chunk + 2]
        both = kept[0] + received[0].astype(jnp.float32)
        products[:, :, :, chunk * width : (chunk + 1) * width] = both.astype(jnp.bfloat16)


def rayleigh_kernel(*refs):
    *tiles, rayleigh = refs
    tile = sum(part[...] for part in tiles)
    trials = rayleigh.shape[0]
    row = lax.broadcasted_iota(jnp.int32, rayleigh.shape, 0)
    column = lax.broadcasted_iota(jnp.int32, rayleigh.shape, 1)

    def entry(position):
        return tile[position : position + 1, :trials]

    result = jnp.zeros(rayleigh.shape, jnp.float32)
    for i in range(trials):
        for j in range(trials):
            squares = entry(trials * trials + i) * entry(trials * trials + j)
            value = entry(i * trials + j) / jnp.sqrt(squares)
            result = jnp.where((row == i) & (column == j), value, result)
    rayleigh[...] = result


def in_hbm(value):
    return pltpu.with_memory_space_constraint(value, pltpu.HBM)


def add_places(tile, axis, masks):
    parts = [tile] + [swap(tile, axis, mask) for mask in masks]
    return sum(parts[1:], parts[0])


def steps_of(count, low):
    steps = []
    while 1 << low < count:
        unit = 1 << low
        steps.append([unit, 2 * unit, 3 * unit] if 2 * unit < count else [unit])
        low += 2
    return steps


def call(kernel, name, flops, moved, limit, **kwargs):
    return pl.pallas_call(
        kernel,
        name=name,
        cost_estimate=pl.CostEstimate(flops=flops, bytes_accessed=moved, transcendentals=0),
        compiler_params=pltpu.CompilerParams(vmem_limit_bytes=limit),
        **kwargs,
    )


def local(vectors, left_ops, right_ops, offsets):
    sectors = lax.axis_size("sec")
    shares = lax.axis_size("term")
    trials, _, pairs, states, _ = vectors.shape
    terms = left_ops.shape[0]
    vectors, left, right = vectors[:, 0], left_ops[:, 0], right_ops[:, 0]
    width, rows = states // CHUNKS, states // shares

    inner, tile, own = call(
        functools.partial(inner_kernel, 1.0 / shares),
        "inner_products",
        2 * terms * trials * pairs * states**3,
        5 * MIB,
        12 * MIB,
        out_shape=(
            jax.ShapeDtypeStruct((terms, trials, pairs, states, states), jnp.bfloat16),
            jax.ShapeDtypeStruct(TILE, jnp.float32),
            jax.ShapeDtypeStruct(right.shape, jnp.bfloat16),
        ),
        in_specs=[VMEM, VMEM, HBM],
        out_specs=(VMEM, VMEM, VMEM),
        scratch_shapes=[pltpu.SemaphoreType.DMA],
    )(vectors, left, in_hbm(right))

    def behind_inner(block):
        return lax.optimization_barrier((block, inner))[0]

    gathered = gather_sectors(right, sectors, behind_inner)
    gathered[0] = own

    def share_of(count, dtype):
        return jax.ShapeDtypeStruct((count, trials, pairs, rows, width), dtype)

    parts, arrived = [], None
    for chunk in range(CHUNKS):
        keep, send, tile = call(
            functools.partial(sum_kernel, sectors, chunk),
            "sum_over_terms",
            2 * terms * trials * pairs * states * states * width,
            4 * MIB,
            sectors * terms * states * width * 2 + 12 * MIB,
            out_shape=(
                share_of(shares // 2, jnp.float32),
                share_of(shares // 2, jnp.bfloat16),
                jax.ShapeDtypeStruct(TILE, jnp.float32),
            ),
            in_specs=[SMEM, VMEM, VMEM, VMEM] + [VMEM] * sectors,
            out_specs=(VMEM, VMEM, VMEM),
            scratch_shapes=[
                pltpu.VMEM((sectors, terms, states, width), jnp.bfloat16),
                pltpu.VMEM((trials, states, width), jnp.float32),
            ],
        )(in_hbm(offsets), vectors, inner, tile, *gathered)
        step = 1
        arrived = received = swap(send, "term", step)
        if chunk == CHUNKS - 1:
            for masks in [[1]] + steps_of(sectors, 1):
                tile = add_places(tile, "sec", masks)
            others = tuple(parts[1::2])
            tile, others = lax.optimization_barrier((tile, others))
            parts[1::2] = others
        while 2 * step < shares:
            step *= 2
            count = shares // (2 * step)
            keep, send = call(
                halve_kernel,
                "halve_rows",
                1,
                1,
                8 * MIB,
                out_shape=(share_of(count, jnp.float32), share_of(count, jnp.bfloat16)),
                in_specs=[VMEM, VMEM],
                out_specs=(VMEM, VMEM),
            )(keep, received)
            received = swap(send, "term", step)
        parts += [keep, received]

    *steps, last = steps_of(shares, 0)
    for masks in steps:
        tile = add_places(tile, "term", masks)
    tiles = [tile] + [swap(tile, "term", mask) for mask in last]
    rayleigh = call(
        rayleigh_kernel,
        "rayleigh",
        1,
        1,
        8 * MIB,
        out_shape=jax.ShapeDtypeStruct((trials, trials), jnp.float32),
        in_specs=[VMEM] * len(tiles),
        out_specs=VMEM,
    )(*tiles)
    products = call(
        finish_kernel,
        "add_last_share",
        1,
        1,
        8 * MIB,
        out_shape=jax.ShapeDtypeStruct((trials, pairs, rows, states), jnp.bfloat16),
        in_specs=[VMEM] * len(parts),
        out_specs=VMEM,
    )(*parts)
    return (products[:, None], rayleigh)


def solution(mesh):
    in_specs = (
        P(None, "sec", None, None, None),
        P("term", "sec", None, None),
        P("term", "sec", None, None),
        P("term", None),
    )
    out_specs = (P(None, "sec", None, "term", None), P())
    return jax.shard_map(local, mesh=mesh, in_specs=in_specs, out_specs=out_specs, check_vma=False)
```

```python
import functools

import jax
import jax.numpy as jnp
from jax import lax
from jax.experimental import pallas as pl
from jax.experimental.pallas import tpu as pltpu
from jax.sharding import PartitionSpec as P

MIB = 1 << 20
TILE = (8, 128)
VMEM = pl.BlockSpec(memory_space=pltpu.VMEM)
SMEM = pl.BlockSpec(memory_space=pltpu.SMEM)
HBM = pl.BlockSpec(memory_space=pltpu.HBM)


def swap(value, axis, mask, count=None):
    masks = [mask, mask] if count is None else [turned(mask, parity, count) for parity in range(2)]
    places = range(lax.axis_size(axis))
    return lax.ppermute(value, axis, [(place, place ^ masks[place & 1]) for place in places])


def turned(mask, parity, count):
    bits = count.bit_length() - 1
    if not parity:
        return mask
    return sum(1 << (bits - bit) for bit in range(1, bits) if mask >> bit & 1) | mask & 1


def gather_sectors(own, sectors, after):
    held = {0: own}
    for mask in range(2, sectors, 2):
        step = 1 << (mask.bit_length() - 1)
        sent = after(own) if mask == 4 else held[mask ^ step]
        held[mask] = swap(sent, "sec", step, sectors)
    return [block for mine in held.values() for block in (mine, swap(mine, "sec", 1))]


def place_rows(values):
    row = lax.broadcasted_iota(jnp.int32, TILE, 0)
    tile = jnp.zeros(TILE, jnp.float32)
    for position, value in values:
        tile = jnp.where(row == position, value, tile)
    return tile


def total(value):
    return jnp.sum(jnp.sum(value, axis=0, keepdims=True), axis=1, keepdims=True)


def inner_kernel(square_scale, vectors, left, right_hbm, inner, squares, right, sem):
    fetch = pltpu.make_async_copy(right_hbm, right, sem)
    fetch.start()
    terms, states = left.shape[0], left.shape[1]
    stacked = left[...].reshape(terms * states, states)
    sums = []
    for trial in range(vectors.shape[0]):
        square = jnp.zeros((8, states), jnp.float32)
        for pair in range(vectors.shape[1]):
            block = vectors[trial, pair]
            product = jnp.dot(stacked, block, preferred_element_type=jnp.float32)
            inner[:, trial, pair] = product.astype(jnp.bfloat16).reshape(terms, states, states)
            wide = block.astype(jnp.float32)
            square += jnp.sum((wide * wide).reshape(-1, 8, states), axis=0)
        sums.append(total(square) * square_scale)
    trials = len(sums)
    squares[...] = place_rows([(trials * trials + k, value) for k, value in enumerate(sums)])
    fetch.wait()


def place_blocks(sectors, pieces, rights):
    odd = lax.axis_index("sec") & 1
    for mask in range(0, sectors, 2):
        even_place, odd_place = turned(mask, 0, sectors), turned(mask, 1, sectors)
        rights[jnp.where(odd == 1, odd_place, even_place)] = pieces[mask][...]
        rights[jnp.where(odd == 1, even_place, odd_place) ^ 1] = pieces[mask + 1][...]


def sum_kernel(sectors, first, offsets, vectors, inner, before, *rest):
    if first == 0:
        *pieces, keep, send, tile, rights, partial = rest
        place_blocks(sectors, pieces, rights)
    else:
        rights, keep, send, tile, partial = rest
    terms, trials, _, states, _ = inner.shape
    shares = 2 * keep.shape[0]
    rows = states // shares
    sector = lax.axis_index("sec")
    place = lax.axis_index("term")
    grams = [jnp.zeros((8, states), jnp.float32) for _ in range(trials * trials)]
    for local_pair in range(keep.shape[2]):
        pair = first + local_pair
        result = None
        for term in range(terms):
            wanted = (sector + offsets[term, pair]) & (sectors - 1)
            added = jnp.dot(
                inner[term, :, pair].reshape(trials * states, states),
                rights[sector ^ wanted, term],
                preferred_element_type=jnp.float32,
            )
            result = added if result is None else result + added
        partial[...] = result.reshape(trials, states, states)
        for j in range(trials):
            product = partial[j]
            for i in range(trials):
                spread = vectors[i, pair].astype(jnp.float32) * product
                grams[i * trials + j] += jnp.sum(spread.reshape(-1, 8, states), axis=0)
        for mask in range(shares):
            start = pl.multiple_of((place ^ mask) * rows, rows)
            share = partial[:, pl.ds(start, rows)]
            if mask & 1:
                send[mask // 2, :, local_pair] = share.astype(jnp.bfloat16)
            else:
                keep[mask // 2, :, local_pair] = share
    tile[...] = before[...] + place_rows([(k, total(value)) for k, value in enumerate(grams)])


def halve_kernel(kept, received, keep, send):
    for k in range(kept.shape[0]):
        both = kept[k] + received[k].astype(jnp.float32)
        if k & 1:
            send[k // 2] = both.astype(jnp.bfloat16)
        else:
            keep[k // 2] = both


def finish_kernel(*refs):
    *parts, products = refs
    first = 0
    for kept, received in zip(parts[::2], parts[1::2]):
        both = kept[0] + received[0].astype(jnp.float32)
        products[:, first : first + both.shape[1]] = both.astype(jnp.bfloat16)
        first += both.shape[1]


def rayleigh_kernel(*refs):
    *tiles, rayleigh = refs
    tile = sum(part[...] for part in tiles)
    trials = rayleigh.shape[0]
    row = lax.broadcasted_iota(jnp.int32, rayleigh.shape, 0)
    column = lax.broadcasted_iota(jnp.int32, rayleigh.shape, 1)

    def entry(position):
        return tile[position : position + 1, :trials]

    result = jnp.zeros(rayleigh.shape, jnp.float32)
    for i in range(trials):
        for j in range(trials):
            squares = entry(trials * trials + i) * entry(trials * trials + j)
            value = entry(i * trials + j) / jnp.sqrt(squares)
            result = jnp.where((row == i) & (column == j), value, result)
    rayleigh[...] = result


def in_hbm(value):
    return pltpu.with_memory_space_constraint(value, pltpu.HBM)


def add_places(tile, axis, masks):
    parts = [tile] + [swap(tile, axis, mask) for mask in masks]
    return sum(parts[1:], parts[0])


def steps_of(count, low):
    steps = []
    while 1 << low < count:
        unit = 1 << low
        steps.append([unit, 2 * unit, 3 * unit] if 2 * unit < count else [unit])
        low += 2
    return steps


def chunk_sizes(pairs):
    return [pairs // 2, pairs - pairs // 2]


def call(kernel, name, flops, moved, limit, **kwargs):
    return pl.pallas_call(
        kernel,
        name=name,
        cost_estimate=pl.CostEstimate(flops=flops, bytes_accessed=moved, transcendentals=0),
        compiler_params=pltpu.CompilerParams(vmem_limit_bytes=limit),
        **kwargs,
    )


def local(vectors, left_ops, right_ops, offsets):
    sectors = lax.axis_size("sec")
    shares = lax.axis_size("term")
    trials, _, pairs, states, _ = vectors.shape
    terms = left_ops.shape[0]
    vectors, left, right = vectors[:, 0], left_ops[:, 0], right_ops[:, 0]
    rows = states // shares

    inner, tile, own = call(
        functools.partial(inner_kernel, 1.0 / shares),
        "inner_products",
        2 * terms * trials * pairs * states**3,
        5 * MIB,
        12 * MIB,
        out_shape=(
            jax.ShapeDtypeStruct((terms, trials, pairs, states, states), jnp.bfloat16),
            jax.ShapeDtypeStruct(TILE, jnp.float32),
            jax.ShapeDtypeStruct(right.shape, jnp.bfloat16),
        ),
        in_specs=[VMEM, VMEM, HBM],
        out_specs=(VMEM, VMEM, VMEM),
        scratch_shapes=[pltpu.SemaphoreType.DMA],
    )(vectors, left, in_hbm(right))

    def behind_inner(block):
        return lax.optimization_barrier((block, inner))[0]

    gathered = gather_sectors(right, sectors, behind_inner)
    gathered[0] = own

    def share_of(count, size, dtype):
        return jax.ShapeDtypeStruct((count, trials, size, rows, states), dtype)

    rights_shape = (sectors, terms, states, states)
    sizes = chunk_sizes(pairs)
    parts, rights, first = [], None, 0
    for size in sizes:
        outs = [
            share_of(shares // 2, size, jnp.float32),
            share_of(shares // 2, size, jnp.bfloat16),
            jax.ShapeDtypeStruct(TILE, jnp.float32),
        ]
        blocks = gathered if first == 0 else [rights]
        if first == 0:
            outs.append(jax.ShapeDtypeStruct(rights_shape, jnp.bfloat16))
        keep, send, tile, *placed = call(
            functools.partial(sum_kernel, sectors, first),
            "sum_over_terms",
            2 * terms * trials * size * states**3,
            4 * MIB,
            12 * MIB,
            out_shape=outs,
            in_specs=[SMEM, VMEM, VMEM, VMEM] + [VMEM] * len(blocks),
            out_specs=[VMEM] * len(outs),
            scratch_shapes=[pltpu.VMEM((trials, states, states), jnp.float32)],
        )(in_hbm(offsets), vectors, inner, tile, *blocks)
        rights = placed[0] if placed else rights
        first += size
        step = 1
        received = swap(send, "term", step)
        if first == pairs:
            for masks in [[1]] + steps_of(sectors, 1):
                tile = add_places(tile, "sec", masks)
            others = tuple(parts[1::2])
            tile, others = lax.optimization_barrier((tile, others))
            parts[1::2] = others
        while 2 * step < shares:
            step *= 2
            count = shares // (2 * step)
            keep, send = call(
                halve_kernel,
                "halve_rows",
                1,
                1,
                8 * MIB,
                out_shape=(share_of(count, size, jnp.float32), share_of(count, size, jnp.bfloat16)),
                in_specs=[VMEM, VMEM],
                out_specs=(VMEM, VMEM),
            )(keep, received)
            received = swap(send, "term", step)
        parts += [keep, received]

    *steps, last = steps_of(shares, 0)
    for masks in steps:
        tile = add_places(tile, "term", masks)
    tiles = [tile] + [swap(tile, "term", mask) for mask in last]
    rayleigh = call(
        rayleigh_kernel,
        "rayleigh",
        1,
        1,
        8 * MIB,
        out_shape=jax.ShapeDtypeStruct((trials, trials), jnp.float32),
        in_specs=[VMEM] * len(tiles),
        out_specs=VMEM,
    )(*tiles)
    products = call(
        finish_kernel,
        "add_last_share",
        1,
        1,
        8 * MIB,
        out_shape=jax.ShapeDtypeStruct((trials, pairs, rows, states), jnp.bfloat16),
        in_specs=[VMEM] * len(parts),
        out_specs=VMEM,
    )(*parts)
    return (products[:, None], rayleigh)


def solution(mesh):
    in_specs = (
        P(None, "sec", None, None, None),
        P("term", "sec", None, None),
        P("term", "sec", None, None),
        P("term", None),
    )
    out_specs = (P(None, "sec", None, "term", None), P())
    return jax.shard_map(local, mesh=mesh, in_specs=in_specs, out_specs=out_specs, check_vma=False)
```

```python
import functools

import jax
import jax.numpy as jnp
from jax import lax
from jax.experimental import pallas as pl
from jax.experimental.pallas import tpu as pltpu
from jax.sharding import PartitionSpec as P

MIB = 1 << 20
TILE = (8, 128)
VMEM = pl.BlockSpec(memory_space=pltpu.VMEM)
SMEM = pl.BlockSpec(memory_space=pltpu.SMEM)
HBM = pl.BlockSpec(memory_space=pltpu.HBM)


def swap(value, axis, mask, count=None):
    masks = [mask, mask] if count is None else [turned(mask, parity, count) for parity in range(2)]
    places = range(lax.axis_size(axis))
    return lax.ppermute(value, axis, [(place, place ^ masks[place & 1]) for place in places])


def turned(mask, parity, count):
    bits = count.bit_length() - 1
    if not parity:
        return mask
    return sum(1 << (bits - bit) for bit in range(1, bits) if mask >> bit & 1) | mask & 1


def gather_sectors(own, sectors, after):
    held = {0: own}
    for mask in range(2, sectors, 2):
        step = 1 << (mask.bit_length() - 1)
        sent = after(own) if mask == 4 else held[mask ^ step]
        held[mask] = swap(sent, "sec", step, sectors)
    return [block for mine in held.values() for block in (mine, swap(mine, "sec", 1))]


def place_rows(values):
    row = lax.broadcasted_iota(jnp.int32, TILE, 0)
    tile = jnp.zeros(TILE, jnp.float32)
    for position, value in values:
        tile = jnp.where(row == position, value, tile)
    return tile


def total(value):
    return jnp.sum(jnp.sum(value, axis=0, keepdims=True), axis=1, keepdims=True)


def inner_kernel(square_scale, vectors, left, right_hbm, inner, squares, right, sem):
    fetch = pltpu.make_async_copy(right_hbm, right, sem)
    fetch.start()
    terms, states = left.shape[0], left.shape[1]
    stacked = left[...].reshape(terms * states, states)
    sums = []
    for trial in range(vectors.shape[0]):
        square = jnp.zeros((8, states), jnp.float32)
        for pair in range(vectors.shape[1]):
            block = vectors[trial, pair]
            product = jnp.dot(stacked, block, preferred_element_type=jnp.float32)
            for term in range(terms):
                part = product[term * states : (term + 1) * states].astype(jnp.bfloat16)
                inner[trial, pair, :, term * states : (term + 1) * states] = part
            wide = block.astype(jnp.float32)
            square += jnp.sum((wide * wide).reshape(-1, 8, states), axis=0)
        sums.append(total(square) * square_scale)
    trials = len(sums)
    squares[...] = place_rows([(trials * trials + k, value) for k, value in enumerate(sums)])
    fetch.wait()


def place_kernel(sectors, *refs):
    *pieces, rights = refs
    odd = lax.axis_index("sec") & 1
    for mask in range(0, sectors - 2, 2):
        even_place, odd_place = turned(mask, 0, sectors), turned(mask, 1, sectors)
        rights[jnp.where(odd == 1, odd_place, even_place)] = pieces[mask][...]
        rights[jnp.where(odd == 1, even_place, odd_place) ^ 1] = pieces[mask + 1][...]


def sum_kernel(sectors, first, offsets, vectors, inner, before, early, mine, theirs, *rest):
    keep, send, tile, blocks, partial = rest
    trials, _, states, _ = inner.shape
    terms = early.shape[1]
    shares = 2 * keep.shape[0]
    rows = states // shares
    late = sectors - 2
    sector = lax.axis_index("sec")
    place = lax.axis_index("term")
    grams = [jnp.zeros((8, states), jnp.float32) for _ in range(trials * trials)]
    for local_pair in range(keep.shape[2]):
        pair = first + local_pair
        slot = local_pair % 2
        for term in range(terms):
            mask = sector ^ ((sector + offsets[term, pair]) & (sectors - 1))
            span = pl.ds(term * states, states)

            @pl.when(mask < late)
            def _():
                blocks[slot, span] = early[mask, term]

            @pl.when(mask == late)
            def _():
                blocks[slot, span] = mine[term]

            @pl.when(mask == late + 1)
            def _():
                blocks[slot, span] = theirs[term]

        result = jnp.dot(
            inner[:, pair].reshape(trials * states, terms * states),
            blocks[slot],
            preferred_element_type=jnp.float32,
        )
        partial[slot] = result.reshape(trials, states, states)
        for j in range(trials):
            product = partial[slot, j]
            for i in range(trials):
                spread = vectors[i, pair].astype(jnp.float32) * product
                grams[i * trials + j] += jnp.sum(spread.reshape(-1, 8, states), axis=0)
        for mask in range(shares):
            start = pl.multiple_of((place ^ mask) * rows, rows)
            share = partial[slot, :, pl.ds(start, rows)]
            if mask & 1:
                send[mask // 2, :, local_pair] = share.astype(jnp.bfloat16)
            else:
                keep[mask // 2, :, local_pair] = share
    tile[...] = before[...] + place_rows([(k, total(value)) for k, value in enumerate(grams)])


def halve_kernel(kept, received, keep, send):
    for k in range(kept.shape[0]):
        both = kept[k] + received[k].astype(jnp.float32)
        if k & 1:
            send[k // 2] = both.astype(jnp.bfloat16)
        else:
            keep[k // 2] = both


def finish_kernel(count, *refs):
    *parts, products, rayleigh = refs
    parts, tiles = parts[:count], parts[count:]
    first = 0
    for kept, received in zip(parts[::2], parts[1::2]):
        both = kept[0] + received[0].astype(jnp.float32)
        products[:, first : first + both.shape[1]] = both.astype(jnp.bfloat16)
        first += both.shape[1]

    tile = sum(part[...] for part in tiles)
    trials = rayleigh.shape[0]
    row = lax.broadcasted_iota(jnp.int32, rayleigh.shape, 0)
    column = lax.broadcasted_iota(jnp.int32, rayleigh.shape, 1)

    def entry(position):
        return tile[position : position + 1, :trials]

    result = jnp.zeros(rayleigh.shape, jnp.float32)
    for i in range(trials):
        for j in range(trials):
            squares = entry(trials * trials + i) * entry(trials * trials + j)
            value = entry(i * trials + j) / jnp.sqrt(squares)
            result = jnp.where((row == i) & (column == j), value, result)
    rayleigh[...] = result


def in_hbm(value):
    return pltpu.with_memory_space_constraint(value, pltpu.HBM)


def add_places(tile, axis, masks):
    parts = [tile] + [swap(tile, axis, mask) for mask in masks]
    return sum(parts[1:], parts[0])


def steps_of(count, low):
    steps = []
    while 1 << low < count:
        unit = 1 << low
        steps.append([unit, 2 * unit, 3 * unit] if 2 * unit < count else [unit])
        low += 2
    return steps


def call(kernel, name, flops, moved, limit, **kwargs):
    return pl.pallas_call(
        kernel,
        name=name,
        cost_estimate=pl.CostEstimate(flops=flops, bytes_accessed=moved, transcendentals=0),
        compiler_params=pltpu.CompilerParams(vmem_limit_bytes=limit),
        **kwargs,
    )


def local(vectors, left_ops, right_ops, offsets):
    sectors = lax.axis_size("sec")
    shares = lax.axis_size("term")
    trials, _, pairs, states, _ = vectors.shape
    terms = left_ops.shape[0]
    vectors, left, right = vectors[:, 0], left_ops[:, 0], right_ops[:, 0]
    rows = states // shares

    inner, tile, own = call(
        functools.partial(inner_kernel, 1.0 / shares),
        "inner_products",
        2 * terms * trials * pairs * states**3,
        5 * MIB,
        12 * MIB,
        out_shape=(
            jax.ShapeDtypeStruct((trials, pairs, states, terms * states), jnp.bfloat16),
            jax.ShapeDtypeStruct(TILE, jnp.float32),
            jax.ShapeDtypeStruct(right.shape, jnp.bfloat16),
        ),
        in_specs=[VMEM, VMEM, HBM],
        out_specs=(VMEM, VMEM, VMEM),
        scratch_shapes=[pltpu.SemaphoreType.DMA],
    )(vectors, left, in_hbm(right))

    def behind_inner(block):
        return lax.optimization_barrier((block, inner))[0]

    gathered = gather_sectors(right, sectors, behind_inner)
    gathered[0] = own

    def share_of(count, size, dtype):
        return jax.ShapeDtypeStruct((count, trials, size, rows, states), dtype)

    *early, mine, theirs = gathered
    early = call(
        functools.partial(place_kernel, sectors),
        "place_blocks",
        1,
        1,
        8 * MIB,
        out_shape=jax.ShapeDtypeStruct((sectors - 2, terms, states, states), jnp.bfloat16),
        in_specs=[VMEM] * len(early),
        out_specs=VMEM,
    )(*early)

    parts, first = [], 0
    for size in (pairs // 2, pairs - pairs // 2):
        keep, send, tile = call(
            functools.partial(sum_kernel, sectors, first),
            "sum_over_terms",
            2 * terms * trials * size * states**3,
            4 * MIB,
            12 * MIB,
            out_shape=(
                share_of(shares // 2, size, jnp.float32),
                share_of(shares // 2, size, jnp.bfloat16),
                jax.ShapeDtypeStruct(TILE, jnp.float32),
            ),
            in_specs=[SMEM] + [VMEM] * 6,
            out_specs=(VMEM, VMEM, VMEM),
            scratch_shapes=[
                pltpu.VMEM((2, terms * states, states), jnp.bfloat16),
                pltpu.VMEM((2, trials, states, states), jnp.float32),
            ],
        )(in_hbm(offsets), vectors, inner, tile, early, mine, theirs)
        first += size
        step = 1
        received = swap(send, "term", step)
        if first == pairs:
            for masks in [[1]] + steps_of(sectors, 1):
                tile = add_places(tile, "sec", masks)
            others = tuple(parts[1::2])
            tile, others = lax.optimization_barrier((tile, others))
            parts[1::2] = others
        while 2 * step < shares:
            step *= 2
            count = shares // (2 * step)
            keep, send = call(
                halve_kernel,
                "halve_rows",
                1,
                1,
                8 * MIB,
                out_shape=(share_of(count, size, jnp.float32), share_of(count, size, jnp.bfloat16)),
                in_specs=[VMEM, VMEM],
                out_specs=(VMEM, VMEM),
            )(keep, received)
            received = swap(send, "term", step)
        parts += [keep, received]

    *steps, last = steps_of(shares, 0)
    for masks in steps:
        tile = add_places(tile, "term", masks)
    tiles = [tile] + [swap(tile, "term", mask) for mask in last]
    products, rayleigh = call(
        functools.partial(finish_kernel, len(parts)),
        "finish",
        1,
        1,
        8 * MIB,
        out_shape=(
            jax.ShapeDtypeStruct((trials, pairs, rows, states), jnp.bfloat16),
            jax.ShapeDtypeStruct((trials, trials), jnp.float32),
        ),
        in_specs=[VMEM] * (len(parts) + len(tiles)),
        out_specs=(VMEM, VMEM),
    )(*parts, *tiles)
    return (products[:, None], rayleigh)


def solution(mesh):
    in_specs = (
        P(None, "sec", None, None, None),
        P("term", "sec", None, None),
        P("term", "sec", None, None),
        P("term", None),
    )
    out_specs = (P(None, "sec", None, "term", None), P())
    return jax.shard_map(local, mesh=mesh, in_specs=in_specs, out_specs=out_specs, check_vma=False)
```

```python
import functools

import jax
import jax.numpy as jnp
from jax import lax
from jax.experimental import pallas as pl
from jax.experimental.pallas import tpu as pltpu
from jax.sharding import PartitionSpec as P

MIB = 1 << 20
TILE = (8, 128)
TILE_ROWS = 16
VMEM = pl.BlockSpec(memory_space=pltpu.VMEM)
SMEM = pl.BlockSpec(memory_space=pltpu.SMEM)
HBM = pl.BlockSpec(memory_space=pltpu.HBM)


def swap(value, axis, mask, count=None):
    masks = [mask, mask] if count is None else [turned(mask, parity, count) for parity in range(2)]
    places = range(lax.axis_size(axis))
    return lax.ppermute(value, axis, [(place, place ^ masks[place & 1]) for place in places])


def turned(mask, parity, count):
    bits = count.bit_length() - 1
    if not parity:
        return mask
    return sum(1 << (bits - bit) for bit in range(1, bits) if mask >> bit & 1) | mask & 1


def gather_sectors(own, sectors, after):
    held = {0: own}
    for mask in range(2, sectors, 2):
        step = 1 << (mask.bit_length() - 1)
        sent = after(own) if mask == 4 else held[mask ^ step]
        held[mask] = swap(sent, "sec", step, sectors)
    return [block for mine in held.values() for block in (mine, swap(mine, "sec", 1))]


def place_rows(values):
    row = lax.broadcasted_iota(jnp.int32, TILE, 0)
    tile = jnp.zeros(TILE, jnp.float32)
    for position, value in values:
        tile = jnp.where(row == position, value, tile)
    return tile


def total(value):
    return jnp.sum(jnp.sum(value, axis=0, keepdims=True), axis=1, keepdims=True)


def inner_kernel(square_scale, vectors, left, right_hbm, inner, squares, right, sem):
    fetch = pltpu.make_async_copy(right_hbm, right, sem)
    fetch.start()
    terms, states = left.shape[0], left.shape[1]
    stacked = left[...].reshape(terms * states, states)
    sums = []
    for trial in range(vectors.shape[0]):
        square = jnp.zeros((8, states), jnp.float32)
        for pair in range(vectors.shape[1]):
            block = vectors[trial, pair]
            product = jnp.dot(stacked, block, preferred_element_type=jnp.float32)
            for term in range(terms):
                part = product[term * states : (term + 1) * states].astype(jnp.bfloat16)
                inner[trial, pair, :, term * states : (term + 1) * states] = part
            wide = block.astype(jnp.float32)
            square += jnp.sum((wide * wide).reshape(-1, 8, states), axis=0)
        sums.append(total(square) * square_scale)
    trials = len(sums)
    squares[...] = place_rows([(trials * trials + k, value) for k, value in enumerate(sums)])
    fetch.wait()


def place_blocks(sectors, pieces, rights):
    odd = lax.axis_index("sec") & 1
    for mask in range(0, sectors, 2):
        even_place, odd_place = turned(mask, 0, sectors), turned(mask, 1, sectors)
        rights[jnp.where(odd == 1, odd_place, even_place)] = pieces[mask][...]
        rights[jnp.where(odd == 1, even_place, odd_place) ^ 1] = pieces[mask + 1][...]


def sum_kernel(sectors, first, offsets, vectors, inner, before, *rest):
    if first == 0:
        *pieces, keep, send, tile, rights, partial = rest
        place_blocks(sectors, pieces, rights)
    else:
        rights, keep, send, tile, partial = rest
    trials, _, states, _ = inner.shape
    terms = rights.shape[1]
    shares = 2 * keep.shape[0]
    rows = states // shares
    sector = lax.axis_index("sec")
    place = lax.axis_index("term")
    grams = [jnp.zeros((8, states), jnp.float32) for _ in range(trials * trials)]
    for local_pair in range(keep.shape[2]):
        pair = first + local_pair
        blocks = []
        for term in range(terms):
            wanted = (sector + offsets[term, pair]) & (sectors - 1)
            blocks.append(rights[sector ^ wanted, term])
        result = jnp.dot(
            inner[:, pair].reshape(trials * states, terms * states),
            jnp.concatenate(blocks, axis=0),
            preferred_element_type=jnp.float32,
        )
        partial[...] = result.reshape(trials, states, states)
        for j in range(trials):
            product = partial[j]
            for i in range(trials):
                spread = vectors[i, pair].astype(jnp.float32) * product
                grams[i * trials + j] += jnp.sum(spread.reshape(-1, 8, states), axis=0)
        for mask in range(shares):
            start = pl.multiple_of((place ^ mask) * rows, rows)
            share = partial[:, pl.ds(start, rows)]
            if mask & 1:
                send[mask // 2, :, local_pair] = share.astype(jnp.bfloat16)
            else:
                keep[mask // 2, :, local_pair] = share
    tile[...] = before[...] + place_rows([(k, total(value)) for k, value in enumerate(grams)])


def halve_last_kernel(kept, received, tile, keep, send):
    keep[0] = kept[0] + received[0].astype(jnp.float32)
    both = kept[1] + received[1].astype(jnp.float32)
    lines = send.shape[0] - 3 * TILE_ROWS
    send[:lines] = both.astype(jnp.bfloat16).reshape(lines, send.shape[1])
    left = tile[...]
    for part in range(3):
        rounded = left.astype(jnp.bfloat16)
        left = left - rounded.astype(jnp.float32)
        block = jnp.concatenate([rounded, jnp.zeros_like(rounded)], axis=0)
        start = lines + part * TILE_ROWS
        send[start : start + TILE_ROWS] = jnp.concatenate([block, block], axis=1)


def halve_kernel(kept, received, keep, send):
    for k in range(kept.shape[0]):
        both = kept[k] + received[k].astype(jnp.float32)
        if k & 1:
            send[k // 2] = both.astype(jnp.bfloat16)
        else:
            keep[k // 2] = both


def ridden_tile(received):
    lines = received.shape[0] - 3 * TILE_ROWS
    parts = []
    for part in range(3):
        start = lines + part * TILE_ROWS
        block = received[start : start + TILE_ROWS, : TILE[1]].astype(jnp.float32)
        parts.append(block[: TILE[0]])
    return parts[0] + parts[1] + parts[2]


def add_ridden_kernel(tile, received, result):
    result[...] = tile[...] + ridden_tile(received)


def finish_kernel(first_kept, first_received, kept, received, *rest):
    *tiles, products, rayleigh = rest
    split = first_kept.shape[2]
    lines = first_received.shape[0] - 3 * TILE_ROWS
    both = first_received[:lines].astype(jnp.float32).reshape(first_kept.shape[1:])
    products[:, :split] = (first_kept[0] + both).astype(jnp.bfloat16)
    products[:, split:] = (kept[0] + received[0].astype(jnp.float32)).astype(jnp.bfloat16)

    tile = sum(part[...] for part in tiles)
    trials = rayleigh.shape[0]
    row = lax.broadcasted_iota(jnp.int32, rayleigh.shape, 0)
    column = lax.broadcasted_iota(jnp.int32, rayleigh.shape, 1)

    def entry(position):
        return tile[position : position + 1, :trials]

    result = jnp.zeros(rayleigh.shape, jnp.float32)
    for i in range(trials):
        for j in range(trials):
            squares = entry(trials * trials + i) * entry(trials * trials + j)
            value = entry(i * trials + j) / jnp.sqrt(squares)
            result = jnp.where((row == i) & (column == j), value, result)
    rayleigh[...] = result


def in_hbm(value):
    return pltpu.with_memory_space_constraint(value, pltpu.HBM)


def add_places(tile, axis, masks):
    parts = [tile] + [swap(tile, axis, mask) for mask in masks]
    return sum(parts[1:], parts[0])


def steps_of(count, low):
    steps = []
    while 1 << low < count:
        unit = 1 << low
        steps.append([unit, 2 * unit, 3 * unit] if 2 * unit < count else [unit])
        low += 2
    return steps


def call(kernel, name, flops, moved, limit, **kwargs):
    return pl.pallas_call(
        kernel,
        name=name,
        cost_estimate=pl.CostEstimate(flops=flops, bytes_accessed=moved, transcendentals=0),
        compiler_params=pltpu.CompilerParams(vmem_limit_bytes=limit),
        **kwargs,
    )


def local(vectors, left_ops, right_ops, offsets):
    sectors = lax.axis_size("sec")
    shares = lax.axis_size("term")
    trials, _, pairs, states, _ = vectors.shape
    terms = left_ops.shape[0]
    vectors, left, right = vectors[:, 0], left_ops[:, 0], right_ops[:, 0]
    rows = states // shares

    inner, tile, own = call(
        functools.partial(inner_kernel, 1.0 / shares),
        "inner_products",
        2 * terms * trials * pairs * states**3,
        5 * MIB,
        12 * MIB,
        out_shape=(
            jax.ShapeDtypeStruct((trials, pairs, states, terms * states), jnp.bfloat16),
            jax.ShapeDtypeStruct(TILE, jnp.float32),
            jax.ShapeDtypeStruct(right.shape, jnp.bfloat16),
        ),
        in_specs=[VMEM, VMEM, HBM],
        out_specs=(VMEM, VMEM, VMEM),
        scratch_shapes=[pltpu.SemaphoreType.DMA],
    )(vectors, left, in_hbm(right))

    def behind_inner(block):
        return lax.optimization_barrier((block, inner))[0]

    gathered = gather_sectors(right, sectors, behind_inner)
    gathered[0] = own

    def share_of(count, size, dtype):
        return jax.ShapeDtypeStruct((count, trials, size, rows, states), dtype)

    rights_shape = (sectors, terms, states, states)
    sizes = [pairs // 2, pairs - pairs // 2]
    sums, rights, first = [], None, 0
    for size in sizes:
        outs = [
            share_of(shares // 2, size, jnp.float32),
            share_of(shares // 2, size, jnp.bfloat16),
            jax.ShapeDtypeStruct(TILE, jnp.float32),
        ]
        blocks = gathered if first == 0 else [rights]
        if first == 0:
            outs.append(jax.ShapeDtypeStruct(rights_shape, jnp.bfloat16))
        keep, send, tile, *placed = call(
            functools.partial(sum_kernel, sectors, first),
            "sum_over_terms",
            2 * terms * trials * size * states**3,
            4 * MIB,
            12 * MIB,
            out_shape=outs,
            in_specs=[SMEM, VMEM, VMEM, VMEM] + [VMEM] * len(blocks),
            out_specs=[VMEM] * len(outs),
            scratch_shapes=[pltpu.VMEM((trials, states, states), jnp.float32)],
        )(in_hbm(offsets), vectors, inner, tile, *blocks)
        rights = placed[0] if placed else rights
        first += size
        sums.append((keep, swap(send, "term", 1)))

    for masks in [[1]] + steps_of(sectors, 1):
        tile = add_places(tile, "sec", masks)

    parts = []
    for chunk, size in enumerate(sizes):
        keep, received = sums[chunk]
        step = 1
        while 2 * step < shares:
            step *= 2
            count = shares // (2 * step)
            last = count == 1 and chunk == 0
            operands = (keep, received, tile) if last else (keep, received)
            lines = trials * size * rows + 3 * TILE_ROWS
            keep, send = call(
                halve_last_kernel if last else halve_kernel,
                "halve_rows",
                1,
                1,
                8 * MIB,
                out_shape=(
                    share_of(count, size, jnp.float32),
                    jax.ShapeDtypeStruct((lines, states), jnp.bfloat16)
                    if last
                    else share_of(count, size, jnp.bfloat16),
                ),
                in_specs=[VMEM] * len(operands),
                out_specs=(VMEM, VMEM),
            )(*operands)
            received = swap(send, "term", step)
        parts += [keep, received]

    tile = call(
        add_ridden_kernel,
        "add_ridden_tile",
        1,
        1,
        8 * MIB,
        out_shape=jax.ShapeDtypeStruct(TILE, jnp.float32),
        in_specs=[VMEM, VMEM],
        out_specs=VMEM,
    )(tile, parts[1])
    tiles, step = [tile], 1
    while 2 * step < shares:
        tile = tiles[0] if len(tiles) == 1 else tiles[0] + tiles[1]
        tiles = [tile, swap(tile, "term", step)]
        step *= 2
    products, rayleigh = call(
        finish_kernel,
        "finish",
        1,
        1,
        8 * MIB,
        out_shape=(
            jax.ShapeDtypeStruct((trials, pairs, rows, states), jnp.bfloat16),
            jax.ShapeDtypeStruct((trials, trials), jnp.float32),
        ),
        in_specs=[VMEM] * (len(parts) + len(tiles)),
        out_specs=(VMEM, VMEM),
    )(*parts, *tiles)
    return (products[:, None], rayleigh)


def solution(mesh):
    in_specs = (
        P(None, "sec", None, None, None),
        P("term", "sec", None, None),
        P("term", "sec", None, None),
        P("term", None),
    )
    out_specs = (P(None, "sec", None, "term", None), P())
    return jax.shard_map(local, mesh=mesh, in_specs=in_specs, out_specs=out_specs, check_vma=False)
```

```python
import functools

import jax
import jax.numpy as jnp
from jax import lax
from jax.experimental import pallas as pl
from jax.experimental.pallas import tpu as pltpu
from jax.sharding import PartitionSpec as P

MIB = 1 << 20
TILE = (8, 128)
TILE_ROWS = 16
VMEM = pl.BlockSpec(memory_space=pltpu.VMEM)
SMEM = pl.BlockSpec(memory_space=pltpu.SMEM)
HBM = pl.BlockSpec(memory_space=pltpu.HBM)


def swap(value, axis, mask, count=None):
    masks = [mask, mask] if count is None else [turned(mask, parity, count) for parity in range(2)]
    places = range(lax.axis_size(axis))
    return lax.ppermute(value, axis, [(place, place ^ masks[place & 1]) for place in places])


def turned(mask, parity, count):
    bits = count.bit_length() - 1
    if not parity:
        return mask
    return sum(1 << (bits - bit) for bit in range(1, bits) if mask >> bit & 1) | mask & 1


def gather_sectors(own, sectors, after):
    held = {0: own}
    for mask in range(2, sectors, 2):
        step = 1 << (mask.bit_length() - 1)
        sent = after(own) if mask == 4 else held[mask ^ step]
        held[mask] = swap(sent, "sec", step, sectors)
    return [block for mine in held.values() for block in (mine, swap(mine, "sec", 1))]


def place_rows(values):
    row = lax.broadcasted_iota(jnp.int32, TILE, 0)
    tile = jnp.zeros(TILE, jnp.float32)
    for position, value in values:
        tile = jnp.where(row == position, value, tile)
    return tile


def total(value):
    return jnp.sum(jnp.sum(value, axis=0, keepdims=True), axis=1, keepdims=True)


def inner_kernel(square_scale, vectors, left, right_hbm, inner, squares, right, sem):
    fetch = pltpu.make_async_copy(right_hbm, right, sem)
    fetch.start()
    terms, states = left.shape[0], left.shape[1]
    stacked = left[...].reshape(terms * states, states)
    sums = []
    for trial in range(vectors.shape[0]):
        square = jnp.zeros((8, states), jnp.float32)
        for pair in range(vectors.shape[1]):
            block = vectors[trial, pair]
            product = jnp.dot(stacked, block, preferred_element_type=jnp.float32)
            for term in range(terms):
                part = product[term * states : (term + 1) * states].astype(jnp.bfloat16)
                inner[trial, pair, :, term * states : (term + 1) * states] = part
            wide = block.astype(jnp.float32)
            square += jnp.sum((wide * wide).reshape(-1, 8, states), axis=0)
        sums.append(total(square) * square_scale)
    trials = len(sums)
    squares[...] = place_rows([(trials * trials + k, value) for k, value in enumerate(sums)])
    fetch.wait()


def place_blocks(sectors, pieces, rights):
    odd = lax.axis_index("sec") & 1
    for mask in range(0, sectors, 2):
        even_place, odd_place = turned(mask, 0, sectors), turned(mask, 1, sectors)
        rights[jnp.where(odd == 1, odd_place, even_place)] = pieces[mask][...]
        rights[jnp.where(odd == 1, even_place, odd_place) ^ 1] = pieces[mask + 1][...]


def sum_kernel(sectors, first, offsets, vectors, inner, before, *rest):
    if first == 0:
        *pieces, keep, send, tile, rights, partial = rest
        place_blocks(sectors, pieces, rights)
    else:
        rights, keep, send, tile, partial = rest
    trials, _, states, _ = inner.shape
    terms = rights.shape[1]
    shares = 2 * keep.shape[0]
    rows = states // shares
    sector = lax.axis_index("sec")
    place = lax.axis_index("term")
    grams = [jnp.zeros((8, states), jnp.float32) for _ in range(trials * trials)]
    for local_pair in range(keep.shape[2]):
        pair = first + local_pair
        blocks = []
        for term in range(terms):
            wanted = (sector + offsets[term, pair]) & (sectors - 1)
            blocks.append(rights[sector ^ wanted, term])
        result = jnp.dot(
            inner[:, pair].reshape(trials * states, terms * states),
            jnp.concatenate(blocks, axis=0),
            preferred_element_type=jnp.float32,
        )
        partial[...] = result.reshape(trials, states, states)
        for j in range(trials):
            product = partial[j]
            for i in range(trials):
                spread = vectors[i, pair].astype(jnp.float32) * product
                grams[i * trials + j] += jnp.sum(spread.reshape(-1, 8, states), axis=0)
        for mask in range(shares):
            start = pl.multiple_of((place ^ mask) * rows, rows)
            share = partial[:, pl.ds(start, rows)]
            if mask & 1:
                send[mask // 2, :, local_pair] = share.astype(jnp.bfloat16)
            else:
                keep[mask // 2, :, local_pair] = share
    tile[...] = before[...] + place_rows([(k, total(value)) for k, value in enumerate(grams)])


def halve_last_kernel(kept, received, tile, keep, send):
    keep[0] = kept[0] + received[0].astype(jnp.float32)
    both = kept[1] + received[1].astype(jnp.float32)
    lines = send.shape[0] - 3 * TILE_ROWS
    send[:lines] = both.astype(jnp.bfloat16).reshape(lines, send.shape[1])
    left = tile[...]
    for part in range(3):
        rounded = left.astype(jnp.bfloat16)
        left = left - rounded.astype(jnp.float32)
        block = jnp.concatenate([rounded, jnp.zeros_like(rounded)], axis=0)
        start = lines + part * TILE_ROWS
        send[start : start + TILE_ROWS] = jnp.concatenate([block, block], axis=1)


def halve_kernel(kept, received, keep, send):
    for k in range(kept.shape[0]):
        both = kept[k] + received[k].astype(jnp.float32)
        if k & 1:
            send[k // 2] = both.astype(jnp.bfloat16)
        else:
            keep[k // 2] = both


def ridden_tile(received):
    lines = received.shape[0] - 3 * TILE_ROWS
    parts = []
    for part in range(3):
        start = lines + part * TILE_ROWS
        block = received[start : start + TILE_ROWS, : TILE[1]].astype(jnp.float32)
        parts.append(block[: TILE[0]])
    return parts[0] + parts[1] + parts[2]


def add_last_kernel(kept, received, result):
    result[...] = (kept[0] + received[0].astype(jnp.float32)).astype(jnp.bfloat16)


def finish_kernel(done, kept, received, tile, products, rayleigh):
    first = done.shape[1]
    lines = received.shape[0] - 3 * TILE_ROWS
    both = received[:lines].astype(jnp.float32).reshape(kept.shape[1:])
    products[:, :first] = done[...]
    products[:, first:] = (kept[0] + both).astype(jnp.bfloat16)

    tile = tile[...] + ridden_tile(received)
    trials = rayleigh.shape[0]
    row = lax.broadcasted_iota(jnp.int32, rayleigh.shape, 0)
    column = lax.broadcasted_iota(jnp.int32, rayleigh.shape, 1)

    def entry(position):
        return tile[position : position + 1, :trials]

    result = jnp.zeros(rayleigh.shape, jnp.float32)
    for i in range(trials):
        for j in range(trials):
            squares = entry(trials * trials + i) * entry(trials * trials + j)
            value = entry(i * trials + j) / jnp.sqrt(squares)
            result = jnp.where((row == i) & (column == j), value, result)
    rayleigh[...] = result


def in_hbm(value):
    return pltpu.with_memory_space_constraint(value, pltpu.HBM)


def add_places(tile, axis, masks):
    parts = [tile] + [swap(tile, axis, mask) for mask in masks]
    return sum(parts[1:], parts[0])


def steps_of(count, low):
    steps = []
    while 1 << low < count:
        unit = 1 << low
        steps.append([unit, 2 * unit, 3 * unit] if 2 * unit < count else [unit])
        low += 2
    return steps


def call(kernel, name, flops, moved, limit, **kwargs):
    return pl.pallas_call(
        kernel,
        name=name,
        cost_estimate=pl.CostEstimate(flops=flops, bytes_accessed=moved, transcendentals=0),
        compiler_params=pltpu.CompilerParams(vmem_limit_bytes=limit),
        **kwargs,
    )


def local(vectors, left_ops, right_ops, offsets):
    sectors = lax.axis_size("sec")
    shares = lax.axis_size("term")
    trials, _, pairs, states, _ = vectors.shape
    terms = left_ops.shape[0]
    vectors, left, right = vectors[:, 0], left_ops[:, 0], right_ops[:, 0]
    rows = states // shares

    inner, tile, own = call(
        functools.partial(inner_kernel, 1.0 / shares),
        "inner_products",
        2 * terms * trials * pairs * states**3,
        5 * MIB,
        12 * MIB,
        out_shape=(
            jax.ShapeDtypeStruct((trials, pairs, states, terms * states), jnp.bfloat16),
            jax.ShapeDtypeStruct(TILE, jnp.float32),
            jax.ShapeDtypeStruct(right.shape, jnp.bfloat16),
        ),
        in_specs=[VMEM, VMEM, HBM],
        out_specs=(VMEM, VMEM, VMEM),
        scratch_shapes=[pltpu.SemaphoreType.DMA],
    )(vectors, left, in_hbm(right))

    def behind_inner(block):
        return lax.optimization_barrier((block, inner))[0]

    gathered = gather_sectors(right, sectors, behind_inner)
    gathered[0] = own

    def share_of(count, size, dtype):
        return jax.ShapeDtypeStruct((count, trials, size, rows, states), dtype)

    rights_shape = (sectors, terms, states, states)
    sizes = [pairs // 2, pairs - pairs // 2]
    sums, rights, first = [], None, 0
    for size in sizes:
        outs = [
            share_of(shares // 2, size, jnp.float32),
            share_of(shares // 2, size, jnp.bfloat16),
            jax.ShapeDtypeStruct(TILE, jnp.float32),
        ]
        blocks = gathered if first == 0 else [rights]
        if first == 0:
            outs.append(jax.ShapeDtypeStruct(rights_shape, jnp.bfloat16))
        keep, send, tile, *placed = call(
            functools.partial(sum_kernel, sectors, first),
            "sum_over_terms",
            2 * terms * trials * size * states**3,
            4 * MIB,
            12 * MIB,
            out_shape=outs,
            in_specs=[SMEM, VMEM, VMEM, VMEM] + [VMEM] * len(blocks),
            out_specs=[VMEM] * len(outs),
            scratch_shapes=[pltpu.VMEM((trials, states, states), jnp.float32)],
        )(in_hbm(offsets), vectors, inner, tile, *blocks)
        rights = placed[0] if placed else rights
        first += size
        sums.append((keep, swap(send, "term", 1)))

    for masks in [[1]] + steps_of(sectors, 1):
        tile = add_places(tile, "sec", masks)

    step = 1
    while 2 * step < shares:
        tile = add_places(tile, "term", [step])
        step *= 2

    parts = []
    for chunk, size in enumerate(sizes):
        keep, received = sums[chunk]
        step = 1
        while 2 * step < shares:
            step *= 2
            count = shares // (2 * step)
            last = count == 1 and chunk == len(sizes) - 1
            operands = (keep, received, tile) if last else (keep, received)
            lines = trials * size * rows + 3 * TILE_ROWS
            keep, send = call(
                halve_last_kernel if last else halve_kernel,
                "halve_rows",
                1,
                1,
                8 * MIB,
                out_shape=(
                    share_of(count, size, jnp.float32),
                    jax.ShapeDtypeStruct((lines, states), jnp.bfloat16)
                    if last
                    else share_of(count, size, jnp.bfloat16),
                ),
                in_specs=[VMEM] * len(operands),
                out_specs=(VMEM, VMEM),
            )(*operands)
            received = swap(send, "term", step)
        parts += [keep, received]

    kept, received, *second = parts
    done = call(
        add_last_kernel,
        "add_last_share",
        10**10,
        1,
        8 * MIB,
        out_shape=jax.ShapeDtypeStruct((trials, sizes[0], rows, states), jnp.bfloat16),
        in_specs=[VMEM, VMEM],
        out_specs=VMEM,
    )(kept, received)
    products, rayleigh = call(
        finish_kernel,
        "finish",
        1,
        1,
        8 * MIB,
        out_shape=(
            jax.ShapeDtypeStruct((trials, pairs, rows, states), jnp.bfloat16),
            jax.ShapeDtypeStruct((trials, trials), jnp.float32),
        ),
        in_specs=[VMEM] * 4,
        out_specs=(VMEM, VMEM),
    )(done, *second, tile)
    return (products[:, None], rayleigh)


def solution(mesh):
    in_specs = (
        P(None, "sec", None, None, None),
        P("term", "sec", None, None),
        P("term", "sec", None, None),
        P("term", None),
    )
    out_specs = (P(None, "sec", None, "term", None), P())
    return jax.shard_map(local, mesh=mesh, in_specs=in_specs, out_specs=out_specs, check_vma=False)
```

```python
import functools

import jax
import jax.numpy as jnp
from jax import lax
from jax.experimental import pallas as pl
from jax.experimental.pallas import tpu as pltpu
from jax.sharding import PartitionSpec as P

MIB = 1 << 20
TILE = (8, 128)
VMEM = pl.BlockSpec(memory_space=pltpu.VMEM)
SMEM = pl.BlockSpec(memory_space=pltpu.SMEM)
HBM = pl.BlockSpec(memory_space=pltpu.HBM)


def swap(value, axis, mask, count=None):
    masks = [mask, mask] if count is None else [turned(mask, parity, count) for parity in range(2)]
    places = range(lax.axis_size(axis))
    return lax.ppermute(value, axis, [(place, place ^ masks[place & 1]) for place in places])


def turned(mask, parity, count):
    bits = count.bit_length() - 1
    if not parity:
        return mask
    return sum(1 << (bits - bit) for bit in range(1, bits) if mask >> bit & 1) | mask & 1


def gather_sectors(own, sectors, after):
    held = {0: own}
    for mask in range(2, sectors, 2):
        step = 1 << (mask.bit_length() - 1)
        sent = after(own) if mask == 4 else held[mask ^ step]
        held[mask] = swap(sent, "sec", step, sectors)
    return [block for mine in held.values() for block in (mine, swap(mine, "sec", 1))]


def place_rows(values):
    row = lax.broadcasted_iota(jnp.int32, TILE, 0)
    tile = jnp.zeros(TILE, jnp.float32)
    for position, value in values:
        tile = jnp.where(row == position, value, tile)
    return tile


def total(value):
    return jnp.sum(jnp.sum(value, axis=0, keepdims=True), axis=1, keepdims=True)


def inner_kernel(square_scale, vectors, left, right_hbm, inner, squares, right, sem):
    fetch = pltpu.make_async_copy(right_hbm, right, sem)
    fetch.start()
    terms, states = left.shape[0], left.shape[1]
    stacked = left[...].reshape(terms * states, states)
    sums = []
    for trial in range(vectors.shape[0]):
        square = jnp.zeros((8, states), jnp.float32)
        for pair in range(vectors.shape[1]):
            block = vectors[trial, pair]
            product = jnp.dot(stacked, block, preferred_element_type=jnp.float32)
            for term in range(terms):
                part = product[term * states : (term + 1) * states].astype(jnp.bfloat16)
                inner[trial, pair, :, term * states : (term + 1) * states] = part
            wide = block.astype(jnp.float32)
            square += jnp.sum((wide * wide).reshape(-1, 8, states), axis=0)
        sums.append(total(square) * square_scale)
    trials = len(sums)
    squares[...] = place_rows([(trials * trials + k, value) for k, value in enumerate(sums)])
    fetch.wait()


def place_blocks(sectors, pieces, rights):
    odd = lax.axis_index("sec") & 1
    for mask in range(0, sectors, 2):
        even_place, odd_place = turned(mask, 0, sectors), turned(mask, 1, sectors)
        rights[jnp.where(odd == 1, odd_place, even_place)] = pieces[mask][...]
        rights[jnp.where(odd == 1, even_place, odd_place) ^ 1] = pieces[mask + 1][...]


def share_masks(shares, backwards):
    if not backwards:
        return list(range(shares))
    bits = shares.bit_length() - 1
    return [sum(1 << (bits - 1 - bit) for bit in range(bits) if k >> bit & 1) for k in range(shares)]


def sum_kernel(sectors, first, offsets, vectors, inner, before, *rest):
    if first == 0:
        *pieces, keep, send, tile, rights, partial = rest
        place_blocks(sectors, pieces, rights)
    else:
        rights, keep, send, tile, partial = rest
    trials, _, states, _ = inner.shape
    terms = rights.shape[1]
    shares = 2 * keep.shape[0]
    rows = states // shares
    sector = lax.axis_index("sec")
    place = lax.axis_index("term")
    grams = [jnp.zeros((8, states), jnp.float32) for _ in range(trials * trials)]
    for local_pair in range(keep.shape[2]):
        pair = first + local_pair
        blocks = []
        for term in range(terms):
            wanted = (sector + offsets[term, pair]) & (sectors - 1)
            blocks.append(rights[sector ^ wanted, term])
        result = jnp.dot(
            inner[:, pair].reshape(trials * states, terms * states),
            jnp.concatenate(blocks, axis=0),
            preferred_element_type=jnp.float32,
        )
        partial[...] = result.reshape(trials, states, states)
        for j in range(trials):
            product = partial[j]
            for i in range(trials):
                spread = vectors[i, pair].astype(jnp.float32) * product
                grams[i * trials + j] += jnp.sum(spread.reshape(-1, 8, states), axis=0)
        for k, mask in enumerate(share_masks(shares, first > 0)):
            start = pl.multiple_of((place ^ mask) * rows, rows)
            share = partial[:, pl.ds(start, rows)]
            if k & 1:
                send[k // 2, :, local_pair] = share.astype(jnp.bfloat16)
            else:
                keep[k // 2, :, local_pair] = share
    tile[...] = before[...] + place_rows([(k, total(value)) for k, value in enumerate(grams)])


def halve_last_kernel(kept, received, tile, keep, send):
    keep[0] = kept[0] + received[0].astype(jnp.float32)
    both = kept[1] + received[1].astype(jnp.float32)
    lines = send.shape[0] - 2 * TILE[0]
    send[:lines] = both.astype(jnp.bfloat16).reshape(lines, send.shape[1])
    left, parts = tile[...], []
    for _ in range(3):
        parts.append(left.astype(jnp.bfloat16).astype(jnp.float32))
        left = left - parts[-1]
    block = jnp.concatenate(
        [
            jnp.concatenate([parts[0], parts[1]], axis=0),
            jnp.concatenate([parts[2], jnp.zeros_like(left)], axis=0),
        ],
        axis=1,
    )
    send[lines:] = block.astype(jnp.bfloat16)


def halve_kernel(kept, received, keep, send):
    for k in range(kept.shape[0]):
        both = kept[k] + received[k].astype(jnp.float32)
        if k & 1:
            send[k // 2] = both.astype(jnp.bfloat16)
        else:
            keep[k // 2] = both


def ridden_tile(received):
    height, width = TILE
    block = received[received.shape[0] - 2 * height :].astype(jnp.float32)
    return block[:height, :width] + block[height:, :width] + block[:height, width:]


def last_rows(kept, received):
    lines = received.shape[0] - 2 * TILE[0]
    both = received[:lines].astype(jnp.float32).reshape(kept.shape[1:])
    return (kept[0] + both).astype(jnp.bfloat16)


def add_last_kernel(kept, received, tile, corner, rows, sums):
    rows[...] = last_rows(kept, received)
    sums[...] = tile[...] + ridden_tile(received) + corner[...]


def finish_kernel(done, tile, kept, received, products, rayleigh):
    first = done.shape[1]
    products[:, :first] = done[...]
    products[:, first:] = last_rows(kept, received)

    tile = tile[...] + ridden_tile(received)
    trials = rayleigh.shape[0]
    row = lax.broadcasted_iota(jnp.int32, rayleigh.shape, 0)
    column = lax.broadcasted_iota(jnp.int32, rayleigh.shape, 1)

    def entry(position):
        return tile[position : position + 1, :trials]

    result = jnp.zeros(rayleigh.shape, jnp.float32)
    for i in range(trials):
        for j in range(trials):
            squares = entry(trials * trials + i) * entry(trials * trials + j)
            value = entry(i * trials + j) / jnp.sqrt(squares)
            result = jnp.where((row == i) & (column == j), value, result)
    rayleigh[...] = result


def in_hbm(value):
    return pltpu.with_memory_space_constraint(value, pltpu.HBM)


def add_places(tile, axis, masks):
    parts = [tile] + [swap(tile, axis, mask) for mask in masks]
    return sum(parts[1:], parts[0])


def steps_of(count, low):
    steps = []
    while 1 << low < count:
        unit = 1 << low
        steps.append([unit, 2 * unit, 3 * unit] if 2 * unit < count else [unit])
        low += 2
    return steps


def call(kernel, name, flops, moved, limit, **kwargs):
    return pl.pallas_call(
        kernel,
        name=name,
        cost_estimate=pl.CostEstimate(flops=flops, bytes_accessed=moved, transcendentals=0),
        compiler_params=pltpu.CompilerParams(vmem_limit_bytes=limit),
        **kwargs,
    )


def local(vectors, left_ops, right_ops, offsets):
    sectors = lax.axis_size("sec")
    shares = lax.axis_size("term")
    trials, _, pairs, states, _ = vectors.shape
    terms = left_ops.shape[0]
    vectors, left, right = vectors[:, 0], left_ops[:, 0], right_ops[:, 0]
    rows = states // shares

    inner, tile, own = call(
        functools.partial(inner_kernel, 1.0 / shares),
        "inner_products",
        2 * terms * trials * pairs * states**3,
        5 * MIB,
        12 * MIB,
        out_shape=(
            jax.ShapeDtypeStruct((trials, pairs, states, terms * states), jnp.bfloat16),
            jax.ShapeDtypeStruct(TILE, jnp.float32),
            jax.ShapeDtypeStruct(right.shape, jnp.bfloat16),
        ),
        in_specs=[VMEM, VMEM, HBM],
        out_specs=(VMEM, VMEM, VMEM),
        scratch_shapes=[pltpu.SemaphoreType.DMA],
    )(vectors, left, in_hbm(right))

    def behind_inner(block):
        return lax.optimization_barrier((block, inner))[0]

    gathered = gather_sectors(right, sectors, behind_inner)
    gathered[0] = own

    def share_of(count, size, dtype):
        return jax.ShapeDtypeStruct((count, trials, size, rows, states), dtype)

    rights_shape = (sectors, terms, states, states)
    sizes = [pairs // 2, pairs - pairs // 2]
    sums, rights, first = [], None, 0
    for size in sizes:
        outs = [
            share_of(shares // 2, size, jnp.float32),
            share_of(shares // 2, size, jnp.bfloat16),
            jax.ShapeDtypeStruct(TILE, jnp.float32),
        ]
        blocks = gathered if first == 0 else [rights]
        if first == 0:
            outs.append(jax.ShapeDtypeStruct(rights_shape, jnp.bfloat16))
        keep, send, tile, *placed = call(
            functools.partial(sum_kernel, sectors, first),
            "sum_over_terms",
            2 * terms * trials * size * states**3,
            4 * MIB,
            12 * MIB,
            out_shape=outs,
            in_specs=[SMEM, VMEM, VMEM, VMEM] + [VMEM] * len(blocks),
            out_specs=[VMEM] * len(outs),
            scratch_shapes=[pltpu.VMEM((trials, states, states), jnp.float32)],
        )(in_hbm(offsets), vectors, inner, tile, *blocks)
        rights = placed[0] if placed else rights
        first += size
        sums.append((keep, send))

    bits = [1 << bit for bit in range(shares.bit_length() - 1)]
    orders = [bits, bits[::-1]]
    arrived = [swap(send, "term", order[0]) for (_, send), order in zip(sums, orders)]
    for masks in [[1]] + steps_of(sectors, 1):
        tile = add_places(tile, "sec", masks)
    for bit in bits[1:-1]:
        tile = add_places(tile, "term", [bit])
    corner = swap(tile, "term", bits[0] | bits[-1])

    parts = []
    for size, (keep, _), received, order in zip(sizes, sums, arrived, orders):
        for step in order[1:]:
            count = keep.shape[0] // 2
            last = count == 1
            operands = (keep, received, tile) if last else (keep, received)
            lines = trials * size * rows + 2 * TILE[0]
            keep, send = call(
                halve_last_kernel if last else halve_kernel,
                "halve_rows",
                1,
                1,
                8 * MIB,
                out_shape=(
                    share_of(count, size, jnp.float32),
                    jax.ShapeDtypeStruct((lines, states), jnp.bfloat16)
                    if last
                    else share_of(count, size, jnp.bfloat16),
                ),
                in_specs=[VMEM] * len(operands),
                out_specs=(VMEM, VMEM),
            )(*operands)
            received = swap(send, "term", step)
        parts += [keep, received]

    kept, received, *second = parts
    done, tile = call(
        add_last_kernel,
        "add_last_share",
        1,
        1,
        8 * MIB,
        out_shape=(
            jax.ShapeDtypeStruct((trials, sizes[0], rows, states), jnp.bfloat16),
            jax.ShapeDtypeStruct(TILE, jnp.float32),
        ),
        in_specs=[VMEM] * 4,
        out_specs=(VMEM, VMEM),
    )(kept, received, tile, corner)
    products, rayleigh = call(
        finish_kernel,
        "finish",
        1,
        1,
        8 * MIB,
        out_shape=(
            jax.ShapeDtypeStruct((trials, pairs, rows, states), jnp.bfloat16),
            jax.ShapeDtypeStruct((trials, trials), jnp.float32),
        ),
        in_specs=[VMEM] * 4,
        out_specs=(VMEM, VMEM),
    )(done, tile, *second)
    return (products[:, None], rayleigh)


def solution(mesh):
    in_specs = (
        P(None, "sec", None, None, None),
        P("term", "sec", None, None),
        P("term", "sec", None, None),
        P("term", None),
    )
    out_specs = (P(None, "sec", None, "term", None), P())
    return jax.shard_map(local, mesh=mesh, in_specs=in_specs, out_specs=out_specs, check_vma=False)
```

```python
import functools

import jax
import jax.numpy as jnp
from jax import lax
from jax.experimental import pallas as pl
from jax.experimental.pallas import tpu as pltpu
from jax.sharding import PartitionSpec as P

MIB = 1 << 20
TILE = (8, 128)
VMEM = pl.BlockSpec(memory_space=pltpu.VMEM)
SMEM = pl.BlockSpec(memory_space=pltpu.SMEM)
HBM = pl.BlockSpec(memory_space=pltpu.HBM)


def swap(value, axis, mask, count=None):
    masks = [mask, mask] if count is None else [turned(mask, parity, count) for parity in range(2)]
    places = range(lax.axis_size(axis))
    return lax.ppermute(value, axis, [(place, place ^ masks[place & 1]) for place in places])


def turned(mask, parity, count):
    bits = count.bit_length() - 1
    if not parity:
        return mask
    return sum(1 << (bits - bit) for bit in range(1, bits) if mask >> bit & 1) | mask & 1


def gather_sectors(own, sectors, after):
    held = {0: own}
    for mask in range(2, sectors, 2):
        step = 1 << (mask.bit_length() - 1)
        sent = after(own) if mask == 4 else held[mask ^ step]
        held[mask] = swap(sent, "sec", step, sectors)
    return [block for mine in held.values() for block in (mine, swap(mine, "sec", 1))]


def place_rows(values):
    row = lax.broadcasted_iota(jnp.int32, TILE, 0)
    tile = jnp.zeros(TILE, jnp.float32)
    for position, value in values:
        tile = jnp.where(row == position, value, tile)
    return tile


def total(value):
    return jnp.sum(jnp.sum(value, axis=0, keepdims=True), axis=1, keepdims=True)


def load_kernel(source, target, sems):
    parts = sems.shape[0] // source.shape[0]
    size = source.shape[1] // parts
    copies = []
    for term in range(source.shape[0]):
        for part in range(parts):
            rows = pl.ds(part * size, size)
            sem = sems.at[term * parts + part]
            copies.append(pltpu.make_async_copy(source.at[term, rows], target.at[term, rows], sem))
    for copy in copies:
        copy.start()
    for copy in copies:
        copy.wait()


def inner_kernel(square_scale, vectors, left, inner, squares):
    terms, states = left.shape[0], left.shape[1]
    stacked = left[...].reshape(terms * states, states)
    sums = []
    for trial in range(vectors.shape[0]):
        square = jnp.zeros((8, states), jnp.float32)
        for pair in range(vectors.shape[1]):
            block = vectors[trial, pair]
            product = jnp.dot(stacked, block, preferred_element_type=jnp.float32)
            for term in range(terms):
                part = product[term * states : (term + 1) * states].astype(jnp.bfloat16)
                inner[trial, pair, :, term * states : (term + 1) * states] = part
            wide = block.astype(jnp.float32)
            square += jnp.sum((wide * wide).reshape(-1, 8, states), axis=0)
        sums.append(total(square) * square_scale)
    trials = len(sums)
    squares[...] = place_rows([(trials * trials + k, value) for k, value in enumerate(sums)])


def place_blocks(sectors, pieces, rights):
    odd = lax.axis_index("sec") & 1
    for mask in range(0, sectors, 2):
        even_place, odd_place = turned(mask, 0, sectors), turned(mask, 1, sectors)
        rights[jnp.where(odd == 1, odd_place, even_place)] = pieces[mask][...]
        rights[jnp.where(odd == 1, even_place, odd_place) ^ 1] = pieces[mask + 1][...]


def sum_kernel(sectors, first, offsets, vectors, inner, before, *rest):
    if first == 0:
        *pieces, keep, send, tile, rights, partial = rest
        place_blocks(sectors, pieces, rights)
    else:
        rights, keep, send, tile, partial = rest
    trials, _, states, _ = inner.shape
    terms = rights.shape[1]
    shares = 2 * keep.shape[0]
    rows = states // shares
    sector = lax.axis_index("sec")
    place = lax.axis_index("term")
    grams = [jnp.zeros((8, states), jnp.float32) for _ in range(trials * trials)]
    for local_pair in range(keep.shape[2]):
        pair = first + local_pair
        blocks = []
        for term in range(terms):
            wanted = (sector + offsets[term, pair]) & (sectors - 1)
            blocks.append(rights[sector ^ wanted, term])
        result = jnp.dot(
            inner[:, pair].reshape(trials * states, terms * states),
            jnp.concatenate(blocks, axis=0),
            preferred_element_type=jnp.float32,
        )
        partial[...] = result.reshape(trials, states, states)
        for j in range(trials):
            product = partial[j]
            for i in range(trials):
                spread = vectors[i, pair].astype(jnp.float32) * product
                grams[i * trials + j] += jnp.sum(spread.reshape(-1, 8, states), axis=0)
        for mask in range(shares):
            start = pl.multiple_of((place ^ mask) * rows, rows)
            share = partial[:, pl.ds(start, rows)]
            if mask & 1:
                send[mask // 2, :, local_pair] = share.astype(jnp.bfloat16)
            else:
                keep[mask // 2, :, local_pair] = share
    tile[...] = before[...] + place_rows([(k, total(value)) for k, value in enumerate(grams)])


def halve_last_kernel(kept, received, tile, keep, send):
    keep[0] = kept[0] + received[0].astype(jnp.float32)
    both = kept[1] + received[1].astype(jnp.float32)
    lines = send.shape[0] - 2 * TILE[0]
    send[:lines] = both.astype(jnp.bfloat16).reshape(lines, send.shape[1])
    left, parts = tile[...], []
    for _ in range(3):
        parts.append(left.astype(jnp.bfloat16).astype(jnp.float32))
        left = left - parts[-1]
    block = jnp.concatenate(
        [
            jnp.concatenate([parts[0], parts[1]], axis=0),
            jnp.concatenate([parts[2], jnp.zeros_like(left)], axis=0),
        ],
        axis=1,
    )
    send[lines:] = block.astype(jnp.bfloat16)


def halve_kernel(kept, received, keep, send):
    for k in range(kept.shape[0]):
        both = kept[k] + received[k].astype(jnp.float32)
        if k & 1:
            send[k // 2] = both.astype(jnp.bfloat16)
        else:
            keep[k // 2] = both


def ridden_tile(received):
    height, width = TILE
    block = received[received.shape[0] - 2 * height :].astype(jnp.float32)
    return block[:height, :width] + block[height:, :width] + block[:height, width:]


def add_last_kernel(kept, received, result):
    result[...] = (kept[0] + received[0].astype(jnp.float32)).astype(jnp.bfloat16)


def finish_kernel(*refs):
    *done, kept, received, tile, products, rayleigh = refs
    first = 0
    for part in done:
        products[:, first : first + part.shape[1]] = part[...]
        first += part.shape[1]
    lines = received.shape[0] - 2 * TILE[0]
    both = received[:lines].astype(jnp.float32).reshape(kept.shape[1:])
    products[:, first:] = (kept[0] + both).astype(jnp.bfloat16)

    tile = tile[...] + ridden_tile(received)
    trials = rayleigh.shape[0]
    row = lax.broadcasted_iota(jnp.int32, rayleigh.shape, 0)
    column = lax.broadcasted_iota(jnp.int32, rayleigh.shape, 1)

    def entry(position):
        return tile[position : position + 1, :trials]

    result = jnp.zeros(rayleigh.shape, jnp.float32)
    for i in range(trials):
        for j in range(trials):
            squares = entry(trials * trials + i) * entry(trials * trials + j)
            value = entry(i * trials + j) / jnp.sqrt(squares)
            result = jnp.where((row == i) & (column == j), value, result)
    rayleigh[...] = result


def in_hbm(value):
    return pltpu.with_memory_space_constraint(value, pltpu.HBM)


def add_places(tile, axis, masks):
    parts = [tile] + [swap(tile, axis, mask) for mask in masks]
    return sum(parts[1:], parts[0])


def steps_of(count, low):
    steps = []
    while 1 << low < count:
        unit = 1 << low
        steps.append([unit, 2 * unit, 3 * unit] if 2 * unit < count else [unit])
        low += 2
    return steps


def call(kernel, name, flops, moved, limit, **kwargs):
    return pl.pallas_call(
        kernel,
        name=name,
        cost_estimate=pl.CostEstimate(flops=flops, bytes_accessed=moved, transcendentals=0),
        compiler_params=pltpu.CompilerParams(vmem_limit_bytes=limit),
        **kwargs,
    )


def local(vectors, left_ops, right_ops, offsets):
    sectors = lax.axis_size("sec")
    shares = lax.axis_size("term")
    trials, _, pairs, states, _ = vectors.shape
    terms = left_ops.shape[0]
    vectors, left, right = vectors[:, 0], left_ops[:, 0], right_ops[:, 0]
    rows = states // shares

    right = call(
        load_kernel,
        "load_right",
        1,
        1,
        4 * MIB,
        out_shape=jax.ShapeDtypeStruct(right.shape, jnp.bfloat16),
        in_specs=[HBM],
        out_specs=VMEM,
        scratch_shapes=[pltpu.SemaphoreType.DMA((2 * terms,))],
    )(in_hbm(right))

    inner, tile = call(
        functools.partial(inner_kernel, 1.0 / shares),
        "inner_products",
        2 * terms * trials * pairs * states**3,
        5 * MIB,
        12 * MIB,
        out_shape=(
            jax.ShapeDtypeStruct((trials, pairs, states, terms * states), jnp.bfloat16),
            jax.ShapeDtypeStruct(TILE, jnp.float32),
        ),
        in_specs=[VMEM, VMEM],
        out_specs=(VMEM, VMEM),
    )(vectors, left)

    def behind_inner(block):
        return lax.optimization_barrier((block, inner))[0]

    gathered = gather_sectors(right, sectors, behind_inner)

    def share_of(count, size, dtype):
        return jax.ShapeDtypeStruct((count, trials, size, rows, states), dtype)

    rights_shape = (sectors, terms, states, states)
    sizes = [pairs // 2, pairs - pairs // 2]
    sums, rights, first = [], None, 0
    for size in sizes:
        outs = [
            share_of(shares // 2, size, jnp.float32),
            share_of(shares // 2, size, jnp.bfloat16),
            jax.ShapeDtypeStruct(TILE, jnp.float32),
        ]
        blocks = gathered if first == 0 else [rights]
        if first == 0:
            outs.append(jax.ShapeDtypeStruct(rights_shape, jnp.bfloat16))
        keep, send, tile, *placed = call(
            functools.partial(sum_kernel, sectors, first),
            "sum_over_terms",
            2 * terms * trials * size * states**3,
            4 * MIB,
            12 * MIB,
            out_shape=outs,
            in_specs=[SMEM, VMEM, VMEM, VMEM] + [VMEM] * len(blocks),
            out_specs=[VMEM] * len(outs),
            scratch_shapes=[pltpu.VMEM((trials, states, states), jnp.float32)],
        )(in_hbm(offsets), vectors, inner, tile, *blocks)
        rights = placed[0] if placed else rights
        first += size
        sums.append((keep, swap(send, "term", 1)))

    for masks in [[1]] + steps_of(sectors, 1):
        tile = add_places(tile, "sec", masks)

    step = 1
    while 2 * step < shares:
        tile = add_places(tile, "term", [step])
        step *= 2

    parts = []
    for chunk, size in enumerate(sizes):
        keep, received = sums[chunk]
        step = 1
        while 2 * step < shares:
            step *= 2
            count = shares // (2 * step)
            last = count == 1 and chunk == len(sizes) - 1
            operands = (keep, received, tile) if last else (keep, received)
            lines = trials * size * rows + 2 * TILE[0]
            keep, send = call(
                halve_last_kernel if last else halve_kernel,
                "halve_rows",
                1,
                1,
                8 * MIB,
                out_shape=(
                    share_of(count, size, jnp.float32),
                    jax.ShapeDtypeStruct((lines, states), jnp.bfloat16)
                    if last
                    else share_of(count, size, jnp.bfloat16),
                ),
                in_specs=[VMEM] * len(operands),
                out_specs=(VMEM, VMEM),
            )(*operands)
            received = swap(send, "term", step)
        parts += [keep, received]

    done = []
    for chunk, size in enumerate(sizes[:-1]):
        done.append(
            call(
                add_last_kernel,
                "add_last_share",
                10**10,
                1,
                8 * MIB,
                out_shape=jax.ShapeDtypeStruct((trials, size, rows, states), jnp.bfloat16),
                in_specs=[VMEM, VMEM],
                out_specs=VMEM,
            )(*parts[2 * chunk : 2 * chunk + 2])
        )
    products, rayleigh = call(
        finish_kernel,
        "finish",
        1,
        1,
        8 * MIB,
        out_shape=(
            jax.ShapeDtypeStruct((trials, pairs, rows, states), jnp.bfloat16),
            jax.ShapeDtypeStruct((trials, trials), jnp.float32),
        ),
        in_specs=[VMEM] * (len(done) + 3),
        out_specs=(VMEM, VMEM),
    )(*done, *parts[-2:], tile)
    return (products[:, None], rayleigh)


def solution(mesh):
    in_specs = (
        P(None, "sec", None, None, None),
        P("term", "sec", None, None),
        P("term", "sec", None, None),
        P("term", None),
    )
    out_specs = (P(None, "sec", None, "term", None), P())
    return jax.shard_map(local, mesh=mesh, in_specs=in_specs, out_specs=out_specs, check_vma=False)
```

```python
import functools

import jax
import jax.numpy as jnp
from jax import lax
from jax.experimental import pallas as pl
from jax.experimental.pallas import tpu as pltpu
from jax.sharding import PartitionSpec as P

MIB = 1 << 20
TILE = (8, 128)
VMEM = pl.BlockSpec(memory_space=pltpu.VMEM)
SMEM = pl.BlockSpec(memory_space=pltpu.SMEM)
HBM = pl.BlockSpec(memory_space=pltpu.HBM)


def swap(value, axis, mask, count=None):
    masks = [mask, mask] if count is None else [turned(mask, parity, count) for parity in range(2)]
    places = range(lax.axis_size(axis))
    return lax.ppermute(value, axis, [(place, place ^ masks[place & 1]) for place in places])


def turned(mask, parity, count):
    bits = count.bit_length() - 1
    if parity:
        return mask
    return sum(1 << (bits - bit) for bit in range(1, bits) if mask >> bit & 1) | mask & 1


def gather_sectors(own, sectors, after):
    held = {0: own}
    for mask in range(2, sectors, 2):
        step = 1 << (mask.bit_length() - 1)
        sent = after(own) if mask == 4 else held[mask ^ step]
        held[mask] = swap(sent, "sec", step, sectors)
    return [block for mine in held.values() for block in (mine, swap(mine, "sec", 1))]


def place_rows(values):
    row = lax.broadcasted_iota(jnp.int32, TILE, 0)
    tile = jnp.zeros(TILE, jnp.float32)
    for position, value in values:
        tile = jnp.where(row == position, value, tile)
    return tile


def total(value):
    return jnp.sum(jnp.sum(value, axis=0, keepdims=True), axis=1, keepdims=True)


def inner_kernel(square_scale, vectors, left, right_hbm, inner, squares, right, sem):
    fetch = pltpu.make_async_copy(right_hbm, right, sem)
    fetch.start()
    terms, states = left.shape[0], left.shape[1]
    stacked = left[...].reshape(terms * states, states)
    sums = []
    for trial in range(vectors.shape[0]):
        square = jnp.zeros((8, states), jnp.float32)
        for pair in range(vectors.shape[1]):
            block = vectors[trial, pair]
            product = jnp.dot(stacked, block, preferred_element_type=jnp.float32)
            for term in range(terms):
                part = product[term * states : (term + 1) * states].astype(jnp.bfloat16)
                inner[trial, pair, :, term * states : (term + 1) * states] = part
            wide = block.astype(jnp.float32)
            square += jnp.sum((wide * wide).reshape(-1, 8, states), axis=0)
        sums.append(total(square) * square_scale)
    trials = len(sums)
    squares[...] = place_rows([(trials * trials + k, value) for k, value in enumerate(sums)])
    fetch.wait()


def place_blocks(sectors, pieces, rights):
    odd = lax.axis_index("sec") & 1
    for mask in range(0, sectors, 2):
        even_place, odd_place = turned(mask, 0, sectors), turned(mask, 1, sectors)
        rights[jnp.where(odd == 1, odd_place, even_place)] = pieces[mask][...]
        rights[jnp.where(odd == 1, even_place, odd_place) ^ 1] = pieces[mask + 1][...]


def sum_kernel(sectors, first, offsets, vectors, inner, before, *rest):
    if first == 0:
        *pieces, keep, send, tile, rights, partial = rest
        place_blocks(sectors, pieces, rights)
    else:
        rights, keep, send, tile, partial = rest
    trials, _, states, _ = inner.shape
    terms = rights.shape[1]
    shares = 2 * keep.shape[0]
    rows = states // shares
    sector = lax.axis_index("sec")
    place = lax.axis_index("term")
    grams = [jnp.zeros((8, states), jnp.float32) for _ in range(trials * trials)]
    for local_pair in range(keep.shape[2]):
        pair = first + local_pair
        blocks = []
        for term in range(terms):
            wanted = (sector + offsets[term, pair]) & (sectors - 1)
            blocks.append(rights[sector ^ wanted, term])
        result = jnp.dot(
            inner[:, pair].reshape(trials * states, terms * states),
            jnp.concatenate(blocks, axis=0),
            preferred_element_type=jnp.float32,
        )
        partial[...] = result.reshape(trials, states, states)
        for j in range(trials):
            product = partial[j]
            for i in range(trials):
                spread = vectors[i, pair].astype(jnp.float32) * product
                grams[i * trials + j] += jnp.sum(spread.reshape(-1, 8, states), axis=0)
        for mask in range(shares):
            start = pl.multiple_of((place ^ mask) * rows, rows)
            share = partial[:, pl.ds(start, rows)]
            if mask & 1:
                send[mask // 2, :, local_pair] = share.astype(jnp.bfloat16)
            else:
                keep[mask // 2, :, local_pair] = share
    tile[...] = before[...] + place_rows([(k, total(value)) for k, value in enumerate(grams)])


def halve_last_kernel(kept, received, tile, keep, send):
    keep[0] = kept[0] + received[0].astype(jnp.float32)
    both = kept[1] + received[1].astype(jnp.float32)
    lines = send.shape[0] - 2 * TILE[0]
    send[:lines] = both.astype(jnp.bfloat16).reshape(lines, send.shape[1])
    left, parts = tile[...], []
    for _ in range(3):
        parts.append(left.astype(jnp.bfloat16).astype(jnp.float32))
        left = left - parts[-1]
    block = jnp.concatenate(
        [
            jnp.concatenate([parts[0], parts[1]], axis=0),
            jnp.concatenate([parts[2], jnp.zeros_like(left)], axis=0),
        ],
        axis=1,
    )
    send[lines:] = block.astype(jnp.bfloat16)


def halve_kernel(kept, received, keep, send):
    for k in range(kept.shape[0]):
        both = kept[k] + received[k].astype(jnp.float32)
        if k & 1:
            send[k // 2] = both.astype(jnp.bfloat16)
        else:
            keep[k // 2] = both


def ridden_tile(received):
    height, width = TILE
    block = received[received.shape[0] - 2 * height :].astype(jnp.float32)
    return block[:height, :width] + block[height:, :width] + block[:height, width:]


def add_last_kernel(kept, received, result):
    result[...] = (kept[0] + received[0].astype(jnp.float32)).astype(jnp.bfloat16)


def finish_kernel(*refs):
    *done, kept, received, tile, products, rayleigh = refs
    first = 0
    for part in done:
        products[:, first : first + part.shape[1]] = part[...]
        first += part.shape[1]
    lines = received.shape[0] - 2 * TILE[0]
    both = received[:lines].astype(jnp.float32).reshape(kept.shape[1:])
    products[:, first:] = (kept[0] + both).astype(jnp.bfloat16)

    tile = tile[...] + ridden_tile(received)
    trials = rayleigh.shape[0]
    row = lax.broadcasted_iota(jnp.int32, rayleigh.shape, 0)
    column = lax.broadcasted_iota(jnp.int32, rayleigh.shape, 1)

    def entry(position):
        return tile[position : position + 1, :trials]

    result = jnp.zeros(rayleigh.shape, jnp.float32)
    for i in range(trials):
        for j in range(trials):
            squares = entry(trials * trials + i) * entry(trials * trials + j)
            value = entry(i * trials + j) / jnp.sqrt(squares)
            result = jnp.where((row == i) & (column == j), value, result)
    rayleigh[...] = result


def in_hbm(value):
    return pltpu.with_memory_space_constraint(value, pltpu.HBM)


def add_places(tile, axis, masks):
    parts = [tile] + [swap(tile, axis, mask) for mask in masks]
    return sum(parts[1:], parts[0])


def steps_of(count, low):
    steps = []
    while 1 << low < count:
        unit = 1 << low
        steps.append([unit, 2 * unit, 3 * unit] if 2 * unit < count else [unit])
        low += 2
    return steps


def call(kernel, name, flops, moved, limit, **kwargs):
    return pl.pallas_call(
        kernel,
        name=name,
        cost_estimate=pl.CostEstimate(flops=flops, bytes_accessed=moved, transcendentals=0),
        compiler_params=pltpu.CompilerParams(vmem_limit_bytes=limit),
        **kwargs,
    )


def local(vectors, left_ops, right_ops, offsets):
    sectors = lax.axis_size("sec")
    shares = lax.axis_size("term")
    trials, _, pairs, states, _ = vectors.shape
    terms = left_ops.shape[0]
    vectors, left, right = vectors[:, 0], left_ops[:, 0], right_ops[:, 0]
    rows = states // shares

    inner, tile, own = call(
        functools.partial(inner_kernel, 1.0 / shares),
        "inner_products",
        2 * terms * trials * pairs * states**3,
        5 * MIB,
        12 * MIB,
        out_shape=(
            jax.ShapeDtypeStruct((trials, pairs, states, terms * states), jnp.bfloat16),
            jax.ShapeDtypeStruct(TILE, jnp.float32),
            jax.ShapeDtypeStruct(right.shape, jnp.bfloat16),
        ),
        in_specs=[VMEM, VMEM, HBM],
        out_specs=(VMEM, VMEM, VMEM),
        scratch_shapes=[pltpu.SemaphoreType.DMA],
    )(vectors, left, in_hbm(right))

    def behind_inner(block):
        return lax.optimization_barrier((block, inner))[0]

    gathered = gather_sectors(right, sectors, behind_inner)
    gathered[0] = own

    def share_of(count, size, dtype):
        return jax.ShapeDtypeStruct((count, trials, size, rows, states), dtype)

    rights_shape = (sectors, terms, states, states)
    sizes = [pairs // 2, pairs - pairs // 2]
    sums, rights, first = [], None, 0
    for size in sizes:
        outs = [
            share_of(shares // 2, size, jnp.float32),
            share_of(shares // 2, size, jnp.bfloat16),
            jax.ShapeDtypeStruct(TILE, jnp.float32),
        ]
        blocks = gathered if first == 0 else [rights]
        if first == 0:
            outs.append(jax.ShapeDtypeStruct(rights_shape, jnp.bfloat16))
        keep, send, tile, *placed = call(
            functools.partial(sum_kernel, sectors, first),
            "sum_over_terms",
            2 * terms * trials * size * states**3,
            4 * MIB,
            12 * MIB,
            out_shape=outs,
            in_specs=[SMEM, VMEM, VMEM, VMEM] + [VMEM] * len(blocks),
            out_specs=[VMEM] * len(outs),
            scratch_shapes=[pltpu.VMEM((trials, states, states), jnp.float32)],
        )(in_hbm(offsets), vectors, inner, tile, *blocks)
        rights = placed[0] if placed else rights
        first += size
        sums.append((keep, swap(send, "term", 1)))

    for masks in [[1]] + steps_of(sectors, 1):
        tile = add_places(tile, "sec", masks)

    step = 1
    while 2 * step < shares:
        tile = add_places(tile, "term", [step])
        step *= 2

    parts = []
    for chunk, size in enumerate(sizes):
        keep, received = sums[chunk]
        step = 1
        while 2 * step < shares:
            step *= 2
            count = shares // (2 * step)
            last = count == 1 and chunk == len(sizes) - 1
            operands = (keep, received, tile) if last else (keep, received)
            lines = trials * size * rows + 2 * TILE[0]
            keep, send = call(
                halve_last_kernel if last else halve_kernel,
                "halve_rows",
                1,
                1,
                8 * MIB,
                out_shape=(
                    share_of(count, size, jnp.float32),
                    jax.ShapeDtypeStruct((lines, states), jnp.bfloat16)
                    if last
                    else share_of(count, size, jnp.bfloat16),
                ),
                in_specs=[VMEM] * len(operands),
                out_specs=(VMEM, VMEM),
            )(*operands)
            received = swap(send, "term", step)
        parts += [keep, received]

    done = []
    for chunk, size in enumerate(sizes[:-1]):
        done.append(
            call(
                add_last_kernel,
                "add_last_share",
                10**10,
                1,
                8 * MIB,
                out_shape=jax.ShapeDtypeStruct((trials, size, rows, states), jnp.bfloat16),
                in_specs=[VMEM, VMEM],
                out_specs=VMEM,
            )(*parts[2 * chunk : 2 * chunk + 2])
        )
    products, rayleigh = call(
        finish_kernel,
        "finish",
        1,
        1,
        8 * MIB,
        out_shape=(
            jax.ShapeDtypeStruct((trials, pairs, rows, states), jnp.bfloat16),
            jax.ShapeDtypeStruct((trials, trials), jnp.float32),
        ),
        in_specs=[VMEM] * (len(done) + 3),
        out_specs=(VMEM, VMEM),
    )(*done, *parts[-2:], tile)
    return (products[:, None], rayleigh)


def solution(mesh):
    in_specs = (
        P(None, "sec", None, None, None),
        P("term", "sec", None, None),
        P("term", "sec", None, None),
        P("term", None),
    )
    out_specs = (P(None, "sec", None, "term", None), P())
    return jax.shard_map(local, mesh=mesh, in_specs=in_specs, out_specs=out_specs, check_vma=False)
```

```python
import functools

import jax
import jax.numpy as jnp
from jax import lax
from jax.experimental import pallas as pl
from jax.experimental.pallas import tpu as pltpu
from jax.sharding import PartitionSpec as P

MIB = 1 << 20
TILE = (8, 128)
VMEM = pl.BlockSpec(memory_space=pltpu.VMEM)
SMEM = pl.BlockSpec(memory_space=pltpu.SMEM)
HBM = pl.BlockSpec(memory_space=pltpu.HBM)


def swap(value, axis, mask, count=None):
    masks = [mask, mask] if count is None else [turned(mask, parity, count) for parity in range(2)]
    places = range(lax.axis_size(axis))
    return lax.ppermute(value, axis, [(place, place ^ masks[place & 1]) for place in places])


def turned(mask, parity, count):
    bits = count.bit_length() - 1
    if parity:
        return mask
    return sum(1 << (bits - bit) for bit in range(1, bits) if mask >> bit & 1) | mask & 1


def gather_sectors(own, sectors, after):
    held = {0: own}
    for mask in range(2, sectors, 2):
        step = 1 << (mask.bit_length() - 1)
        sent = after(own) if mask == 4 else held[mask ^ step]
        held[mask] = swap(sent, "sec", step, sectors)
    return [block for mine in held.values() for block in (mine, swap(mine, "sec", 1))]


def place_rows(values):
    row = lax.broadcasted_iota(jnp.int32, TILE, 0)
    tile = jnp.zeros(TILE, jnp.float32)
    for position, value in values:
        tile = jnp.where(row == position, value, tile)
    return tile


def total(value):
    return jnp.sum(jnp.sum(value, axis=0, keepdims=True), axis=1, keepdims=True)


def inner_kernel(square_scale, vectors, left, right_hbm, inner, squares, right, sem):
    fetch = pltpu.make_async_copy(right_hbm, right, sem)
    fetch.start()
    terms, states = left.shape[0], left.shape[1]
    stacked = left[...].reshape(terms * states, states)
    sums = []
    for trial in range(vectors.shape[0]):
        square = jnp.zeros((8, states), jnp.float32)
        for pair in range(vectors.shape[1]):
            block = vectors[trial, pair]
            product = jnp.dot(stacked, block, preferred_element_type=jnp.float32)
            for term in range(terms):
                part = product[term * states : (term + 1) * states].astype(jnp.bfloat16)
                inner[trial, pair, :, term * states : (term + 1) * states] = part
            wide = block.astype(jnp.float32)
            square += jnp.sum((wide * wide).reshape(-1, 8, states), axis=0)
        sums.append(total(square) * square_scale)
    trials = len(sums)
    squares[...] = place_rows([(trials * trials + k, value) for k, value in enumerate(sums)])
    fetch.wait()


def place_blocks(sectors, pieces, rights):
    odd = lax.axis_index("sec") & 1
    for mask in range(0, sectors, 2):
        even_place, odd_place = turned(mask, 0, sectors), turned(mask, 1, sectors)
        rights[jnp.where(odd == 1, odd_place, even_place)] = pieces[mask][...]
        if mask + 1 < len(pieces):
            rights[jnp.where(odd == 1, even_place, odd_place) ^ 1] = pieces[mask + 1][...]
    rights[sectors - 1] = jnp.zeros(rights.shape[1:], rights.dtype)


def needed_mask(sectors, offsets, term, pair):
    sector = lax.axis_index("sec")
    return sector ^ ((sector + offsets[term, pair]) & (sectors - 1))


def times_right(inner, term, pair, block):
    trials, _, states, _ = inner.shape
    lines = inner[:, pair, :, term * states : (term + 1) * states]
    product = jnp.dot(
        lines.reshape(trials * states, states), block, preferred_element_type=jnp.float32
    )
    return product.reshape(trials, states, states)


def sum_terms(sectors, pair, offsets, inner, rights):
    result = None
    for term in range(rights.shape[1]):
        mask = needed_mask(sectors, offsets, term, pair)
        added = times_right(inner, term, pair, rights[mask, term])
        result = added if result is None else result + added
    return result


def add_gram(vectors, pair, values, grams):
    trials, states = vectors.shape[0], vectors.shape[-1]
    for j in range(trials):
        for i in range(trials):
            spread = vectors[i, pair].astype(jnp.float32) * values[j]
            grams[i * trials + j] += jnp.sum(spread.reshape(-1, 8, states), axis=0)


def write_tile(before, grams, tile):
    count = grams.shape[0]
    tile[...] = before[...] + place_rows([(k, total(grams[k])) for k in range(count)])


def write_shares(whole, slot, keep, send):
    shares = 2 * keep.shape[0]
    rows = whole.shape[1] // shares
    place = lax.axis_index("term")
    for mask in range(shares):
        start = pl.multiple_of((place ^ mask) * rows, rows)
        share = whole[:, pl.ds(start, rows)]
        if mask & 1:
            send[mask // 2, :, slot] = share.astype(jnp.bfloat16)
        else:
            keep[mask // 2, :, slot] = share


def early_kernel(sectors, offsets, vectors, inner, before, *rest):
    *pieces, partial, tile, rights, grams = rest
    place_blocks(sectors, pieces, rights)
    grams[...] = jnp.zeros_like(grams)
    for pair in range(partial.shape[0]):
        partial[pair] = sum_terms(sectors, pair, offsets, inner, rights)
        add_gram(vectors, pair, partial[pair], grams)
    write_tile(before, grams, tile)


def late_kernel(sectors, offsets, vectors, inner, before, partial, last, *rest):
    keep, send, tile, whole, grams = rest
    grams[...] = jnp.zeros_like(grams)
    for pair in range(partial.shape[0]):
        whole[...] = partial[pair]
        for term in range(last.shape[0]):

            @pl.when(needed_mask(sectors, offsets, term, pair) == sectors - 1)
            def _():
                added = times_right(inner, term, pair, last[term])
                whole[...] += added
                add_gram(vectors, pair, added, grams)

        write_shares(whole, pair, keep, send)
    write_tile(before, grams, tile)


def second_kernel(sectors, first, offsets, vectors, inner, before, rights, last, *rest):
    keep, send, tile, whole, grams = rest
    grams[...] = jnp.zeros_like(grams)
    for slot in range(keep.shape[2]):
        pair = first + slot
        whole[slot] = sum_terms(sectors, pair, offsets, inner, rights)
        for term in range(last.shape[0]):

            @pl.when(needed_mask(sectors, offsets, term, pair) == sectors - 1)
            def _():
                whole[slot] += times_right(inner, term, pair, last[term])

    for slot in range(keep.shape[2]):
        add_gram(vectors, first + slot, whole[slot], grams)
        write_shares(whole.at[slot], slot, keep, send)
    write_tile(before, grams, tile)


def halve_last_kernel(kept, received, tile, keep, send):
    keep[0] = kept[0] + received[0].astype(jnp.float32)
    both = kept[1] + received[1].astype(jnp.float32)
    lines = send.shape[0] - 2 * TILE[0]
    send[:lines] = both.astype(jnp.bfloat16).reshape(lines, send.shape[1])
    left, parts = tile[...], []
    for _ in range(3):
        parts.append(left.astype(jnp.bfloat16).astype(jnp.float32))
        left = left - parts[-1]
    block = jnp.concatenate(
        [
            jnp.concatenate([parts[0], parts[1]], axis=0),
            jnp.concatenate([parts[2], jnp.zeros_like(left)], axis=0),
        ],
        axis=1,
    )
    send[lines:] = block.astype(jnp.bfloat16)


def halve_kernel(kept, received, keep, send):
    for k in range(kept.shape[0]):
        both = kept[k] + received[k].astype(jnp.float32)
        if k & 1:
            send[k // 2] = both.astype(jnp.bfloat16)
        else:
            keep[k // 2] = both


def ridden_tile(received):
    height, width = TILE
    block = received[received.shape[0] - 2 * height :].astype(jnp.float32)
    return block[:height, :width] + block[height:, :width] + block[:height, width:]


def add_last_kernel(kept, received, result):
    result[...] = (kept[0] + received[0].astype(jnp.float32)).astype(jnp.bfloat16)


def finish_kernel(*refs):
    *done, kept, received, tile, products, rayleigh = refs
    first = 0
    for part in done:
        products[:, first : first + part.shape[1]] = part[...]
        first += part.shape[1]
    lines = received.shape[0] - 2 * TILE[0]
    both = received[:lines].astype(jnp.float32).reshape(kept.shape[1:])
    products[:, first:] = (kept[0] + both).astype(jnp.bfloat16)

    tile = tile[...] + ridden_tile(received)
    trials = rayleigh.shape[0]
    row = lax.broadcasted_iota(jnp.int32, rayleigh.shape, 0)
    column = lax.broadcasted_iota(jnp.int32, rayleigh.shape, 1)

    def entry(position):
        return tile[position : position + 1, :trials]

    result = jnp.zeros(rayleigh.shape, jnp.float32)
    for i in range(trials):
        for j in range(trials):
            squares = entry(trials * trials + i) * entry(trials * trials + j)
            value = entry(i * trials + j) / jnp.sqrt(squares)
            result = jnp.where((row == i) & (column == j), value, result)
    rayleigh[...] = result


def in_hbm(value):
    return pltpu.with_memory_space_constraint(value, pltpu.HBM)


def add_places(tile, axis, masks):
    parts = [tile] + [swap(tile, axis, mask) for mask in masks]
    return sum(parts[1:], parts[0])


def steps_of(count, low):
    steps = []
    while 1 << low < count:
        unit = 1 << low
        steps.append([unit, 2 * unit, 3 * unit] if 2 * unit < count else [unit])
        low += 2
    return steps


def call(kernel, name, flops, moved, limit, **kwargs):
    return pl.pallas_call(
        kernel,
        name=name,
        cost_estimate=pl.CostEstimate(flops=flops, bytes_accessed=moved, transcendentals=0),
        compiler_params=pltpu.CompilerParams(vmem_limit_bytes=limit),
        **kwargs,
    )


def local(vectors, left_ops, right_ops, offsets):
    sectors = lax.axis_size("sec")
    shares = lax.axis_size("term")
    trials, _, pairs, states, _ = vectors.shape
    terms = left_ops.shape[0]
    vectors, left, right = vectors[:, 0], left_ops[:, 0], right_ops[:, 0]
    rows = states // shares

    inner, tile, own = call(
        functools.partial(inner_kernel, 1.0 / shares),
        "inner_products",
        2 * terms * trials * pairs * states**3,
        5 * MIB,
        12 * MIB,
        out_shape=(
            jax.ShapeDtypeStruct((trials, pairs, states, terms * states), jnp.bfloat16),
            jax.ShapeDtypeStruct(TILE, jnp.float32),
            jax.ShapeDtypeStruct(right.shape, jnp.bfloat16),
        ),
        in_specs=[VMEM, VMEM, HBM],
        out_specs=(VMEM, VMEM, VMEM),
        scratch_shapes=[pltpu.SemaphoreType.DMA],
    )(vectors, left, in_hbm(right))

    def behind_inner(block):
        return lax.optimization_barrier((block, inner))[0]

    gathered = gather_sectors(right, sectors, behind_inner)
    gathered[0] = own

    def share_of(count, size, dtype):
        return jax.ShapeDtypeStruct((count, trials, size, rows, states), dtype)

    tile_shape = jax.ShapeDtypeStruct(TILE, jnp.float32)
    rights_shape = jax.ShapeDtypeStruct((sectors, terms, states, states), jnp.bfloat16)
    sizes = [pairs // 2, pairs - pairs // 2]
    grams = pltpu.VMEM((trials * trials, 8, states), jnp.float32)
    *early, last = gathered
    partial, tile, rights = call(
        functools.partial(early_kernel, sectors),
        "early_products",
        2 * terms * trials * sizes[0] * states**3,
        4 * MIB,
        12 * MIB,
        out_shape=(
            jax.ShapeDtypeStruct((sizes[0], trials, states, states), jnp.float32),
            tile_shape,
            rights_shape,
        ),
        in_specs=[SMEM, VMEM, VMEM, VMEM] + [VMEM] * len(early),
        out_specs=(VMEM, VMEM, VMEM),
        scratch_shapes=[grams],
    )(in_hbm(offsets), vectors, inner, tile, *early)

    def sums_of(kernel, name, flops, size, scratch, *operands):
        return call(
            kernel,
            name,
            flops,
            MIB,
            12 * MIB,
            out_shape=(
                share_of(shares // 2, size, jnp.float32),
                share_of(shares // 2, size, jnp.bfloat16),
                tile_shape,
            ),
            in_specs=[SMEM] + [VMEM] * len(operands),
            out_specs=(VMEM, VMEM, VMEM),
            scratch_shapes=[pltpu.VMEM((*scratch, states, states), jnp.float32), grams],
        )(in_hbm(offsets), *operands)

    keep, send, tile = sums_of(
        functools.partial(late_kernel, sectors),
        "late_products",
        terms * trials * sizes[0] * states**3 // 4,
        sizes[0],
        (trials,),
        vectors,
        inner,
        tile,
        partial,
        last,
    )
    sums = [(keep, swap(send, "term", 1))]
    keep, send, tile = sums_of(
        functools.partial(second_kernel, sectors, sizes[0]),
        "second_products",
        2 * terms * trials * sizes[1] * states**3,
        sizes[1],
        (sizes[1], trials),
        vectors,
        inner,
        tile,
        rights,
        last,
    )
    sums.append((keep, swap(send, "term", 1)))

    for masks in [[1]] + steps_of(sectors, 1):
        tile = add_places(tile, "sec", masks)

    step = 1
    while 2 * step < shares:
        tile = add_places(tile, "term", [step])
        step *= 2

    parts = []
    for chunk, size in enumerate(sizes):
        keep, received = sums[chunk]
        step = 1
        while 2 * step < shares:
            step *= 2
            count = shares // (2 * step)
            last = count == 1 and chunk == len(sizes) - 1
            operands = (keep, received, tile) if last else (keep, received)
            lines = trials * size * rows + 2 * TILE[0]
            keep, send = call(
                halve_last_kernel if last else halve_kernel,
                "halve_rows",
                1,
                1,
                8 * MIB,
                out_shape=(
                    share_of(count, size, jnp.float32),
                    jax.ShapeDtypeStruct((lines, states), jnp.bfloat16)
                    if last
                    else share_of(count, size, jnp.bfloat16),
                ),
                in_specs=[VMEM] * len(operands),
                out_specs=(VMEM, VMEM),
            )(*operands)
            received = swap(send, "term", step)
        parts += [keep, received]

    done = []
    for chunk, size in enumerate(sizes[:-1]):
        done.append(
            call(
                add_last_kernel,
                "add_last_share",
                10**10,
                1,
                8 * MIB,
                out_shape=jax.ShapeDtypeStruct((trials, size, rows, states), jnp.bfloat16),
                in_specs=[VMEM, VMEM],
                out_specs=VMEM,
            )(*parts[2 * chunk : 2 * chunk + 2])
        )
    products, rayleigh = call(
        finish_kernel,
        "finish",
        1,
        1,
        8 * MIB,
        out_shape=(
            jax.ShapeDtypeStruct((trials, pairs, rows, states), jnp.bfloat16),
            jax.ShapeDtypeStruct((trials, trials), jnp.float32),
        ),
        in_specs=[VMEM] * (len(done) + 3),
        out_specs=(VMEM, VMEM),
    )(*done, *parts[-2:], tile)
    return (products[:, None], rayleigh)


def solution(mesh):
    in_specs = (
        P(None, "sec", None, None, None),
        P("term", "sec", None, None),
        P("term", "sec", None, None),
        P("term", None),
    )
    out_specs = (P(None, "sec", None, "term", None), P())
    return jax.shard_map(local, mesh=mesh, in_specs=in_specs, out_specs=out_specs, check_vma=False)
```

```python
import functools

import jax
import jax.numpy as jnp
from jax import lax
from jax.experimental import pallas as pl
from jax.experimental.pallas import tpu as pltpu
from jax.sharding import PartitionSpec as P

MIB = 1 << 20
TILE = (8, 128)
VMEM = pl.BlockSpec(memory_space=pltpu.VMEM)
SMEM = pl.BlockSpec(memory_space=pltpu.SMEM)
HBM = pl.BlockSpec(memory_space=pltpu.HBM)


def swap(value, axis, mask, count=None):
    masks = [mask, mask] if count is None else [turned(mask, parity, count) for parity in range(2)]
    places = range(lax.axis_size(axis))
    return lax.ppermute(value, axis, [(place, place ^ masks[place & 1]) for place in places])


def turned(mask, parity, count):
    bits = count.bit_length() - 1
    if parity:
        return mask
    return sum(1 << (bits - bit) for bit in range(1, bits) if mask >> bit & 1) | mask & 1


def gather_sectors(own, sectors, after):
    held = {0: own}
    for mask in range(2, sectors, 2):
        step = 1 << (mask.bit_length() - 1)
        sent = after(own) if mask == 4 else held[mask ^ step]
        held[mask] = swap(sent, "sec", step, sectors)
    return [block for mine in held.values() for block in (mine, swap(mine, "sec", 1))]


def place_rows(values):
    row = lax.broadcasted_iota(jnp.int32, TILE, 0)
    tile = jnp.zeros(TILE, jnp.float32)
    for position, value in values:
        tile = jnp.where(row == position, value, tile)
    return tile


def total(value):
    return jnp.sum(jnp.sum(value, axis=0, keepdims=True), axis=1, keepdims=True)


def inner_kernel(square_scale, vectors, left, right_hbm, inner, squares, right, sem):
    fetch = pltpu.make_async_copy(right_hbm, right, sem)
    fetch.start()
    terms, states = left.shape[0], left.shape[1]
    stacked = left[...].reshape(terms * states, states)
    sums = []
    for trial in range(vectors.shape[0]):
        square = jnp.zeros((8, states), jnp.float32)
        for pair in range(vectors.shape[1]):
            block = vectors[trial, pair]
            product = jnp.dot(stacked, block, preferred_element_type=jnp.float32)
            for term in range(terms):
                part = product[term * states : (term + 1) * states].astype(jnp.bfloat16)
                inner[trial, pair, :, term * states : (term + 1) * states] = part
            wide = block.astype(jnp.float32)
            square += jnp.sum((wide * wide).reshape(-1, 8, states), axis=0)
        sums.append(total(square) * square_scale)
    trials = len(sums)
    squares[...] = place_rows([(trials * trials + k, value) for k, value in enumerate(sums)])
    fetch.wait()


def place_blocks(sectors, pieces, rights):
    odd = lax.axis_index("sec") & 1
    for mask in range(0, sectors, 2):
        even_place, odd_place = turned(mask, 0, sectors), turned(mask, 1, sectors)
        rights[jnp.where(odd == 1, odd_place, even_place)] = pieces[mask][...]
        if mask + 1 < len(pieces):
            rights[jnp.where(odd == 1, even_place, odd_place) ^ 1] = pieces[mask + 1][...]
    rights[sectors - 1] = jnp.zeros(rights.shape[1:], rights.dtype)


def needed_mask(sectors, offsets, term, pair):
    sector = lax.axis_index("sec")
    return sector ^ ((sector + offsets[term, pair]) & (sectors - 1))


def times_right(inner, term, pair, block):
    trials, _, states, _ = inner.shape
    lines = inner[:, pair, :, term * states : (term + 1) * states]
    product = jnp.dot(
        lines.reshape(trials * states, states), block, preferred_element_type=jnp.float32
    )
    return product.reshape(trials, states, states)


def sum_terms(sectors, pair, offsets, inner, rights):
    result = None
    for term in range(rights.shape[1]):
        mask = needed_mask(sectors, offsets, term, pair)
        added = times_right(inner, term, pair, rights[mask, term])
        result = added if result is None else result + added
    return result


def add_gram(vectors, pair, values, grams):
    trials, states = vectors.shape[0], vectors.shape[-1]
    for j in range(trials):
        for i in range(trials):
            spread = vectors[i, pair].astype(jnp.float32) * values[j]
            grams[i * trials + j] += jnp.sum(spread.reshape(-1, 8, states), axis=0)


def write_tile(before, grams, tile):
    count = grams.shape[0]
    tile[...] = before[...] + place_rows([(k, total(grams[k])) for k in range(count)])


def share_masks(shares, backwards):
    bits = shares.bit_length() - 1
    places = range(bits)
    if backwards:
        return [sum((k >> bit & 1) << (bits - 1 - bit) for bit in places) for k in range(shares)]
    return list(range(shares))


def write_shares(whole, backwards, slot, keep, send):
    shares = 2 * keep.shape[0]
    rows = whole.shape[1] // shares
    place = lax.axis_index("term")
    for k, mask in enumerate(share_masks(shares, backwards)):
        start = pl.multiple_of((place ^ mask) * rows, rows)
        share = whole[:, pl.ds(start, rows)]
        if k & 1:
            send[k // 2, :, slot] = share.astype(jnp.bfloat16)
        else:
            keep[k // 2, :, slot] = share


def early_kernel(sectors, offsets, vectors, inner, before, *rest):
    *pieces, partial, tile, rights, grams = rest
    place_blocks(sectors, pieces, rights)
    grams[...] = jnp.zeros_like(grams)
    for pair in range(partial.shape[0]):
        partial[pair] = sum_terms(sectors, pair, offsets, inner, rights)
        add_gram(vectors, pair, partial[pair], grams)
    write_tile(before, grams, tile)


def late_kernel(sectors, offsets, vectors, inner, before, partial, last, *rest):
    keep, send, tile, whole, grams = rest
    grams[...] = jnp.zeros_like(grams)
    for pair in range(partial.shape[0]):
        whole[...] = partial[pair]
        for term in range(last.shape[0]):

            @pl.when(needed_mask(sectors, offsets, term, pair) == sectors - 1)
            def _():
                added = times_right(inner, term, pair, last[term])
                whole[...] += added
                add_gram(vectors, pair, added, grams)

        write_shares(whole, False, pair, keep, send)
    write_tile(before, grams, tile)


def second_kernel(sectors, first, offsets, vectors, inner, before, rights, last, *rest):
    keep, send, tile, whole, grams = rest
    grams[...] = jnp.zeros_like(grams)
    for slot in range(keep.shape[2]):
        pair = first + slot
        whole[slot] = sum_terms(sectors, pair, offsets, inner, rights)
        for term in range(last.shape[0]):

            @pl.when(needed_mask(sectors, offsets, term, pair) == sectors - 1)
            def _():
                whole[slot] += times_right(inner, term, pair, last[term])

    for slot in range(keep.shape[2]):
        add_gram(vectors, first + slot, whole[slot], grams)
        write_shares(whole.at[slot], True, slot, keep, send)
    write_tile(before, grams, tile)


def halve_last_kernel(kept, received, tile, keep, send):
    keep[0] = kept[0] + received[0].astype(jnp.float32)
    both = kept[1] + received[1].astype(jnp.float32)
    lines = send.shape[0] - 2 * TILE[0]
    send[:lines] = both.astype(jnp.bfloat16).reshape(lines, send.shape[1])
    left, parts = tile[...], []
    for _ in range(3):
        parts.append(left.astype(jnp.bfloat16).astype(jnp.float32))
        left = left - parts[-1]
    block = jnp.concatenate(
        [
            jnp.concatenate([parts[0], parts[1]], axis=0),
            jnp.concatenate([parts[2], jnp.zeros_like(left)], axis=0),
        ],
        axis=1,
    )
    send[lines:] = block.astype(jnp.bfloat16)


def halve_kernel(kept, received, keep, send):
    for k in range(kept.shape[0]):
        both = kept[k] + received[k].astype(jnp.float32)
        if k & 1:
            send[k // 2] = both.astype(jnp.bfloat16)
        else:
            keep[k // 2] = both


def ridden_tile(received):
    height, width = TILE
    block = received[received.shape[0] - 2 * height :].astype(jnp.float32)
    return block[:height, :width] + block[height:, :width] + block[:height, width:]


def last_rows(kept, received):
    lines = received.shape[0] - 2 * TILE[0]
    both = received[:lines].astype(jnp.float32).reshape(kept.shape[1:])
    return (kept[0] + both).astype(jnp.bfloat16)


def add_last_kernel(kept, received, tile, corner, rows, sums):
    rows[...] = last_rows(kept, received)
    sums[...] = tile[...] + ridden_tile(received) + corner[...]


def finish_kernel(kept, received, rows, tile, products, rayleigh):
    first = kept.shape[2]
    products[:, :first] = last_rows(kept, received)
    products[:, first:] = rows[...]

    tile = tile[...] + ridden_tile(received)
    trials = rayleigh.shape[0]
    row = lax.broadcasted_iota(jnp.int32, rayleigh.shape, 0)
    column = lax.broadcasted_iota(jnp.int32, rayleigh.shape, 1)

    def entry(position):
        return tile[position : position + 1, :trials]

    result = jnp.zeros(rayleigh.shape, jnp.float32)
    for i in range(trials):
        for j in range(trials):
            squares = entry(trials * trials + i) * entry(trials * trials + j)
            value = entry(i * trials + j) / jnp.sqrt(squares)
            result = jnp.where((row == i) & (column == j), value, result)
    rayleigh[...] = result


def in_hbm(value):
    return pltpu.with_memory_space_constraint(value, pltpu.HBM)


def add_places(tile, axis, masks):
    parts = [tile] + [swap(tile, axis, mask) for mask in masks]
    return sum(parts[1:], parts[0])


def steps_of(count, low):
    steps = []
    while 1 << low < count:
        unit = 1 << low
        steps.append([unit, 2 * unit, 3 * unit] if 2 * unit < count else [unit])
        low += 2
    return steps


def call(kernel, name, flops, moved, limit, **kwargs):
    return pl.pallas_call(
        kernel,
        name=name,
        cost_estimate=pl.CostEstimate(flops=flops, bytes_accessed=moved, transcendentals=0),
        compiler_params=pltpu.CompilerParams(vmem_limit_bytes=limit),
        **kwargs,
    )


def local(vectors, left_ops, right_ops, offsets):
    sectors = lax.axis_size("sec")
    shares = lax.axis_size("term")
    trials, _, pairs, states, _ = vectors.shape
    terms = left_ops.shape[0]
    vectors, left, right = vectors[:, 0], left_ops[:, 0], right_ops[:, 0]
    rows = states // shares

    inner, tile, own = call(
        functools.partial(inner_kernel, 1.0 / shares),
        "inner_products",
        2 * terms * trials * pairs * states**3,
        5 * MIB,
        12 * MIB,
        out_shape=(
            jax.ShapeDtypeStruct((trials, pairs, states, terms * states), jnp.bfloat16),
            jax.ShapeDtypeStruct(TILE, jnp.float32),
            jax.ShapeDtypeStruct(right.shape, jnp.bfloat16),
        ),
        in_specs=[VMEM, VMEM, HBM],
        out_specs=(VMEM, VMEM, VMEM),
        scratch_shapes=[pltpu.SemaphoreType.DMA],
    )(vectors, left, in_hbm(right))

    def behind_inner(block):
        return lax.optimization_barrier((block, inner))[0]

    gathered = gather_sectors(right, sectors, behind_inner)
    gathered[0] = own

    def share_of(count, size, dtype):
        return jax.ShapeDtypeStruct((count, trials, size, rows, states), dtype)

    tile_shape = jax.ShapeDtypeStruct(TILE, jnp.float32)
    rights_shape = jax.ShapeDtypeStruct((sectors, terms, states, states), jnp.bfloat16)
    sizes = [pairs - pairs // 4, pairs // 4]
    grams = pltpu.VMEM((trials * trials, 8, states), jnp.float32)
    *early, last = gathered
    partial, tile, rights = call(
        functools.partial(early_kernel, sectors),
        "early_products",
        2 * terms * trials * sizes[0] * states**3,
        4 * MIB,
        12 * MIB,
        out_shape=(
            jax.ShapeDtypeStruct((sizes[0], trials, states, states), jnp.float32),
            tile_shape,
            rights_shape,
        ),
        in_specs=[SMEM, VMEM, VMEM, VMEM] + [VMEM] * len(early),
        out_specs=(VMEM, VMEM, VMEM),
        scratch_shapes=[grams],
    )(in_hbm(offsets), vectors, inner, tile, *early)

    def sums_of(kernel, name, flops, size, scratch, *operands):
        return call(
            kernel,
            name,
            flops,
            MIB,
            12 * MIB,
            out_shape=(
                share_of(shares // 2, size, jnp.float32),
                share_of(shares // 2, size, jnp.bfloat16),
                tile_shape,
            ),
            in_specs=[SMEM] + [VMEM] * len(operands),
            out_specs=(VMEM, VMEM, VMEM),
            scratch_shapes=[pltpu.VMEM((*scratch, states, states), jnp.float32), grams],
        )(in_hbm(offsets), *operands)

    keep, send, tile = sums_of(
        functools.partial(late_kernel, sectors),
        "late_products",
        terms * trials * sizes[0] * states**3 // 4,
        sizes[0],
        (trials,),
        vectors,
        inner,
        tile,
        partial,
        last,
    )
    bits = [1 << bit for bit in range(shares.bit_length() - 1)]
    orders = [bits, bits[::-1]]
    sums = [(keep, swap(send, "term", bits[0]))]
    keep, send, tile = sums_of(
        functools.partial(second_kernel, sectors, sizes[0]),
        "second_products",
        2 * terms * trials * sizes[1] * states**3,
        sizes[1],
        (sizes[1], trials),
        vectors,
        inner,
        tile,
        rights,
        last,
    )
    sums.append((keep, swap(send, "term", bits[-1])))

    for masks in [[1]] + steps_of(sectors, 1):
        tile = add_places(tile, "sec", masks)

    for bit in bits[1:-1]:
        tile = add_places(tile, "term", [bit])
    corner = swap(tile, "term", bits[0] | bits[-1])

    parts = []
    for size, (keep, received), order in zip(sizes, sums, orders):
        for step in order[1:]:
            count = keep.shape[0] // 2
            last_step = count == 1
            operands = (keep, received, tile) if last_step else (keep, received)
            lines = trials * size * rows + 2 * TILE[0]
            keep, send = call(
                halve_last_kernel if last_step else halve_kernel,
                "halve_rows",
                1,
                1,
                8 * MIB,
                out_shape=(
                    share_of(count, size, jnp.float32),
                    jax.ShapeDtypeStruct((lines, states), jnp.bfloat16)
                    if last_step
                    else share_of(count, size, jnp.bfloat16),
                ),
                in_specs=[VMEM] * len(operands),
                out_specs=(VMEM, VMEM),
            )(*operands)
            received = swap(send, "term", step)
        parts += [keep, received]

    rows_done, tile = call(
        add_last_kernel,
        "add_last_share",
        1,
        1,
        8 * MIB,
        out_shape=(
            jax.ShapeDtypeStruct((trials, sizes[1], rows, states), jnp.bfloat16),
            tile_shape,
        ),
        in_specs=[VMEM] * 4,
        out_specs=(VMEM, VMEM),
    )(*parts[2:], tile, corner)
    products, rayleigh = call(
        finish_kernel,
        "finish",
        1,
        1,
        8 * MIB,
        out_shape=(
            jax.ShapeDtypeStruct((trials, pairs, rows, states), jnp.bfloat16),
            jax.ShapeDtypeStruct((trials, trials), jnp.float32),
        ),
        in_specs=[VMEM] * 4,
        out_specs=(VMEM, VMEM),
    )(*parts[:2], rows_done, tile)
    return (products[:, None], rayleigh)


def solution(mesh):
    in_specs = (
        P(None, "sec", None, None, None),
        P("term", "sec", None, None),
        P("term", "sec", None, None),
        P("term", None),
    )
    out_specs = (P(None, "sec", None, "term", None), P())
    return jax.shard_map(local, mesh=mesh, in_specs=in_specs, out_specs=out_specs, check_vma=False)
```

```python
import functools

import jax
import jax.numpy as jnp
from jax import lax
from jax.experimental import pallas as pl
from jax.experimental.pallas import tpu as pltpu
from jax.sharding import PartitionSpec as P

MIB = 1 << 20
TILE = (8, 128)
VMEM = pl.BlockSpec(memory_space=pltpu.VMEM)
SMEM = pl.BlockSpec(memory_space=pltpu.SMEM)
HBM = pl.BlockSpec(memory_space=pltpu.HBM)


def swap(value, axis, mask, count=None):
    masks = [mask, mask] if count is None else [turned(mask, parity, count) for parity in range(2)]
    places = range(lax.axis_size(axis))
    return lax.ppermute(value, axis, [(place, place ^ masks[place & 1]) for place in places])


def turned(mask, parity, count):
    bits = count.bit_length() - 1
    if parity:
        return mask
    return sum(1 << (bits - bit) for bit in range(1, bits) if mask >> bit & 1) | mask & 1


def gather_sectors(own, sectors, after):
    held = {0: own}
    for mask in range(2, sectors, 2):
        step = 1 << (mask.bit_length() - 1)
        sent = after(own) if mask == 4 else held[mask ^ step]
        held[mask] = swap(sent, "sec", step, sectors)
    return [block for mine in held.values() for block in (mine, swap(mine, "sec", 1))]


def place_rows(values):
    row = lax.broadcasted_iota(jnp.int32, TILE, 0)
    tile = jnp.zeros(TILE, jnp.float32)
    for position, value in values:
        tile = jnp.where(row == position, value, tile)
    return tile


def total(value):
    return jnp.sum(jnp.sum(value, axis=0, keepdims=True), axis=1, keepdims=True)


def inner_kernel(
    square_scale, vectors, left, right_hbm, offsets_hbm, inner, squares, right, offsets, sems
):
    fetches = [
        pltpu.make_async_copy(offsets_hbm, offsets, sems.at[0]),
        pltpu.make_async_copy(right_hbm, right, sems.at[1]),
    ]
    for fetch in fetches:
        fetch.start()
    terms, states = left.shape[0], left.shape[1]
    stacked = left[...].reshape(terms * states, states)
    sums = []
    for trial in range(vectors.shape[0]):
        square = jnp.zeros((8, states), jnp.float32)
        for pair in range(vectors.shape[1]):
            block = vectors[trial, pair]
            product = jnp.dot(stacked, block, preferred_element_type=jnp.float32)
            for term in range(terms):
                part = product[term * states : (term + 1) * states].astype(jnp.bfloat16)
                inner[trial, pair, :, term * states : (term + 1) * states] = part
            wide = block.astype(jnp.float32)
            square += jnp.sum((wide * wide).reshape(-1, 8, states), axis=0)
        sums.append(total(square) * square_scale)
    trials = len(sums)
    squares[...] = place_rows([(trials * trials + k, value) for k, value in enumerate(sums)])
    for fetch in fetches:
        fetch.wait()


def place_blocks(sectors, pieces, rights):
    odd = lax.axis_index("sec") & 1
    for mask in range(0, sectors, 2):
        even_place, odd_place = turned(mask, 0, sectors), turned(mask, 1, sectors)
        rights[jnp.where(odd == 1, odd_place, even_place)] = pieces[mask][...]
        if mask + 1 < len(pieces):
            rights[jnp.where(odd == 1, even_place, odd_place) ^ 1] = pieces[mask + 1][...]
    rights[sectors - 1] = jnp.zeros(rights.shape[1:], rights.dtype)


def needed_mask(sectors, offsets, term, pair):
    sector = lax.axis_index("sec")
    return sector ^ ((sector + offsets[term, pair]) & (sectors - 1))


def times_right(inner, term, pair, block):
    trials, _, states, _ = inner.shape
    lines = inner[:, pair, :, term * states : (term + 1) * states]
    product = jnp.dot(
        lines.reshape(trials * states, states), block, preferred_element_type=jnp.float32
    )
    return product.reshape(trials, states, states)


def sum_terms(sectors, pair, offsets, inner, rights):
    result = None
    for term in range(rights.shape[1]):
        mask = needed_mask(sectors, offsets, term, pair)
        added = times_right(inner, term, pair, rights[mask, term])
        result = added if result is None else result + added
    return result


def add_gram(vectors, pair, values, grams):
    trials, states = vectors.shape[0], vectors.shape[-1]
    for j in range(trials):
        for i in range(trials):
            spread = vectors[i, pair].astype(jnp.float32) * values[j]
            grams[i * trials + j] += jnp.sum(spread.reshape(-1, 8, states), axis=0)


def write_tile(before, grams, tile):
    count = grams.shape[0]
    tile[...] = before[...] + place_rows([(k, total(grams[k])) for k in range(count)])


def write_shares(whole, slot, keep, send):
    shares = 2 * keep.shape[0]
    rows = whole.shape[1] // shares
    place = lax.axis_index("term")
    for mask in range(shares):
        start = pl.multiple_of((place ^ mask) * rows, rows)
        share = whole[:, pl.ds(start, rows)]
        if mask & 1:
            send[mask // 2, :, slot] = share.astype(jnp.bfloat16)
        else:
            keep[mask // 2, :, slot] = share


def early_kernel(sectors, offsets, vectors, inner, before, *rest):
    *pieces, partial, tile, rights, grams = rest
    place_blocks(sectors, pieces, rights)
    grams[...] = jnp.zeros_like(grams)
    for pair in range(partial.shape[0]):
        partial[pair] = sum_terms(sectors, pair, offsets, inner, rights)
        add_gram(vectors, pair, partial[pair], grams)
    write_tile(before, grams, tile)


def late_kernel(sectors, offsets, vectors, inner, before, partial, last, *rest):
    keep, send, tile, whole, grams = rest
    grams[...] = jnp.zeros_like(grams)
    for pair in range(partial.shape[0]):
        lacks = [
            needed_mask(sectors, offsets, term, pair) == sectors - 1
            for term in range(last.shape[0])
        ]
        lacking = functools.reduce(jnp.logical_or, lacks)
        write_shares(partial.at[pair], pair, keep, send)

        @pl.when(lacking)
        def _():
            whole[...] = partial[pair]
            for term, lack in enumerate(lacks):

                @pl.when(lack)
                def _():
                    added = times_right(inner, term, pair, last[term])
                    whole[...] += added
                    add_gram(vectors, pair, added, grams)

            write_shares(whole, pair, keep, send)

    write_tile(before, grams, tile)


def second_kernel(sectors, first, offsets, vectors, inner, before, rights, last, *rest):
    keep, send, tile, whole, grams = rest
    grams[...] = jnp.zeros_like(grams)
    for slot in range(keep.shape[2]):
        pair = first + slot
        whole[slot] = sum_terms(sectors, pair, offsets, inner, rights)
        for term in range(last.shape[0]):

            @pl.when(needed_mask(sectors, offsets, term, pair) == sectors - 1)
            def _():
                whole[slot] += times_right(inner, term, pair, last[term])

    for slot in range(keep.shape[2]):
        add_gram(vectors, first + slot, whole[slot], grams)
        write_shares(whole.at[slot], slot, keep, send)
    write_tile(before, grams, tile)


def halve_last_kernel(kept, received, tile, keep, send):
    keep[0] = kept[0] + received[0].astype(jnp.float32)
    both = kept[1] + received[1].astype(jnp.float32)
    lines = send.shape[0] - 2 * TILE[0]
    send[:lines] = both.astype(jnp.bfloat16).reshape(lines, send.shape[1])
    left, parts = tile[...], []
    for _ in range(3):
        parts.append(left.astype(jnp.bfloat16).astype(jnp.float32))
        left = left - parts[-1]
    block = jnp.concatenate(
        [
            jnp.concatenate([parts[0], parts[1]], axis=0),
            jnp.concatenate([parts[2], jnp.zeros_like(left)], axis=0),
        ],
        axis=1,
    )
    send[lines:] = block.astype(jnp.bfloat16)


def halve_kernel(kept, received, keep, send):
    for k in range(kept.shape[0]):
        both = kept[k] + received[k].astype(jnp.float32)
        if k & 1:
            send[k // 2] = both.astype(jnp.bfloat16)
        else:
            keep[k // 2] = both


def ridden_tile(received):
    height, width = TILE
    block = received[received.shape[0] - 2 * height :].astype(jnp.float32)
    return block[:height, :width] + block[height:, :width] + block[:height, width:]


def add_last_kernel(kept, received, result):
    result[...] = (kept[0] + received[0].astype(jnp.float32)).astype(jnp.bfloat16)


def finish_kernel(*refs):
    *done, kept, received, tile, products, rayleigh = refs
    first = 0
    for part in done:
        products[:, first : first + part.shape[1]] = part[...]
        first += part.shape[1]
    lines = received.shape[0] - 2 * TILE[0]
    both = received[:lines].astype(jnp.float32).reshape(kept.shape[1:])
    products[:, first:] = (kept[0] + both).astype(jnp.bfloat16)

    tile = tile[...] + ridden_tile(received)
    trials = rayleigh.shape[0]
    row = lax.broadcasted_iota(jnp.int32, rayleigh.shape, 0)
    column = lax.broadcasted_iota(jnp.int32, rayleigh.shape, 1)

    def entry(position):
        return tile[position : position + 1, :trials]

    result = jnp.zeros(rayleigh.shape, jnp.float32)
    for i in range(trials):
        for j in range(trials):
            squares = entry(trials * trials + i) * entry(trials * trials + j)
            value = entry(i * trials + j) / jnp.sqrt(squares)
            result = jnp.where((row == i) & (column == j), value, result)
    rayleigh[...] = result


def in_hbm(value):
    return pltpu.with_memory_space_constraint(value, pltpu.HBM)


def add_places(tile, axis, masks):
    parts = [tile] + [swap(tile, axis, mask) for mask in masks]
    return sum(parts[1:], parts[0])


def steps_of(count, low):
    steps = []
    while 1 << low < count:
        unit = 1 << low
        steps.append([unit, 2 * unit, 3 * unit] if 2 * unit < count else [unit])
        low += 2
    return steps


def call(kernel, name, flops, moved, limit, **kwargs):
    return pl.pallas_call(
        kernel,
        name=name,
        cost_estimate=pl.CostEstimate(flops=flops, bytes_accessed=moved, transcendentals=0),
        compiler_params=pltpu.CompilerParams(vmem_limit_bytes=limit),
        **kwargs,
    )


def local(vectors, left_ops, right_ops, offsets):
    sectors = lax.axis_size("sec")
    shares = lax.axis_size("term")
    trials, _, pairs, states, _ = vectors.shape
    terms = left_ops.shape[0]
    vectors, left, right = vectors[:, 0], left_ops[:, 0], right_ops[:, 0]
    rows = states // shares

    inner, tile, own, offsets = call(
        functools.partial(inner_kernel, 1.0 / shares),
        "inner_products",
        2 * terms * trials * pairs * states**3,
        5 * MIB,
        12 * MIB,
        out_shape=(
            jax.ShapeDtypeStruct((trials, pairs, states, terms * states), jnp.bfloat16),
            jax.ShapeDtypeStruct(TILE, jnp.float32),
            jax.ShapeDtypeStruct(right.shape, jnp.bfloat16),
            jax.ShapeDtypeStruct(offsets.shape, offsets.dtype),
        ),
        in_specs=[VMEM, VMEM, HBM, HBM],
        out_specs=(VMEM, VMEM, VMEM, VMEM),
        scratch_shapes=[pltpu.SemaphoreType.DMA((2,))],
    )(vectors, left, in_hbm(right), in_hbm(offsets))

    def behind_inner(block):
        return lax.optimization_barrier((block, inner))[0]

    gathered = gather_sectors(right, sectors, behind_inner)
    gathered[0] = own

    def share_of(count, size, dtype):
        return jax.ShapeDtypeStruct((count, trials, size, rows, states), dtype)

    tile_shape = jax.ShapeDtypeStruct(TILE, jnp.float32)
    rights_shape = jax.ShapeDtypeStruct((sectors, terms, states, states), jnp.bfloat16)
    sizes = [pairs // 2, pairs - pairs // 2]
    grams = pltpu.VMEM((trials * trials, 8, states), jnp.float32)
    *early, last = gathered
    partial, tile, rights = call(
        functools.partial(early_kernel, sectors),
        "early_products",
        2 * terms * trials * sizes[0] * states**3,
        4 * MIB,
        12 * MIB,
        out_shape=(
            jax.ShapeDtypeStruct((sizes[0], trials, states, states), jnp.float32),
            tile_shape,
            rights_shape,
        ),
        in_specs=[SMEM, VMEM, VMEM, VMEM] + [VMEM] * len(early),
        out_specs=(VMEM, VMEM, VMEM),
        scratch_shapes=[grams],
    )(offsets, vectors, inner, tile, *early)

    def sums_of(kernel, name, flops, size, scratch, *operands):
        return call(
            kernel,
            name,
            flops,
            MIB,
            12 * MIB,
            out_shape=(
                share_of(shares // 2, size, jnp.float32),
                share_of(shares // 2, size, jnp.bfloat16),
                tile_shape,
            ),
            in_specs=[SMEM] + [VMEM] * len(operands),
            out_specs=(VMEM, VMEM, VMEM),
            scratch_shapes=[pltpu.VMEM((*scratch, states, states), jnp.float32), grams],
        )(offsets, *operands)

    keep, send, tile = sums_of(
        functools.partial(late_kernel, sectors),
        "late_products",
        terms * trials * sizes[0] * states**3 // 4,
        sizes[0],
        (trials,),
        vectors,
        inner,
        tile,
        partial,
        last,
    )
    sums = [(keep, swap(send, "term", 1))]
    keep, send, tile = sums_of(
        functools.partial(second_kernel, sectors, sizes[0]),
        "second_products",
        2 * terms * trials * sizes[1] * states**3,
        sizes[1],
        (sizes[1], trials),
        vectors,
        inner,
        tile,
        rights,
        last,
    )
    sums.append((keep, swap(send, "term", 1)))

    for masks in [[1]] + steps_of(sectors, 1):
        tile = add_places(tile, "sec", masks)

    step = 1
    while 2 * step < shares:
        tile = add_places(tile, "term", [step])
        step *= 2

    parts = []
    for chunk, size in enumerate(sizes):
        keep, received = sums[chunk]
        step = 1
        while 2 * step < shares:
            step *= 2
            count = shares // (2 * step)
            last = count == 1 and chunk == len(sizes) - 1
            operands = (keep, received, tile) if last else (keep, received)
            lines = trials * size * rows + 2 * TILE[0]
            keep, send = call(
                halve_last_kernel if last else halve_kernel,
                "halve_rows",
                1,
                1,
                8 * MIB,
                out_shape=(
                    share_of(count, size, jnp.float32),
                    jax.ShapeDtypeStruct((lines, states), jnp.bfloat16)
                    if last
                    else share_of(count, size, jnp.bfloat16),
                ),
                in_specs=[VMEM] * len(operands),
                out_specs=(VMEM, VMEM),
            )(*operands)
            received = swap(send, "term", step)
        parts += [keep, received]

    done = []
    for chunk, size in enumerate(sizes[:-1]):
        done.append(
            call(
                add_last_kernel,
                "add_last_share",
                10**10,
                1,
                8 * MIB,
                out_shape=jax.ShapeDtypeStruct((trials, size, rows, states), jnp.bfloat16),
                in_specs=[VMEM, VMEM],
                out_specs=VMEM,
            )(*parts[2 * chunk : 2 * chunk + 2])
        )
    products, rayleigh = call(
        finish_kernel,
        "finish",
        1,
        1,
        8 * MIB,
        out_shape=(
            jax.ShapeDtypeStruct((trials, pairs, rows, states), jnp.bfloat16),
            jax.ShapeDtypeStruct((trials, trials), jnp.float32),
        ),
        in_specs=[VMEM] * (len(done) + 3),
        out_specs=(VMEM, VMEM),
    )(*done, *parts[-2:], tile)
    return (products[:, None], rayleigh)


def solution(mesh):
    in_specs = (
        P(None, "sec", None, None, None),
        P("term", "sec", None, None),
        P("term", "sec", None, None),
        P("term", None),
    )
    out_specs = (P(None, "sec", None, "term", None), P())
    return jax.shard_map(local, mesh=mesh, in_specs=in_specs, out_specs=out_specs, check_vma=False)
```

```python
import functools

import jax
import jax.numpy as jnp
from jax import lax
from jax.experimental import pallas as pl
from jax.experimental.pallas import tpu as pltpu
from jax.sharding import PartitionSpec as P

MIB = 1 << 20
TILE = (8, 128)
VMEM = pl.BlockSpec(memory_space=pltpu.VMEM)
SMEM = pl.BlockSpec(memory_space=pltpu.SMEM)
HBM = pl.BlockSpec(memory_space=pltpu.HBM)


def swap(value, axis, mask, count=None):
    masks = [mask, mask] if count is None else [turned(mask, parity, count) for parity in range(2)]
    places = range(lax.axis_size(axis))
    return lax.ppermute(value, axis, [(place, place ^ masks[place & 1]) for place in places])


def turned(mask, parity, count):
    bits = count.bit_length() - 1
    if parity:
        return mask
    return sum(1 << (bits - bit) for bit in range(1, bits) if mask >> bit & 1) | mask & 1


def gather_sectors(own, sectors, after):
    held = {0: own}
    for mask in range(2, sectors, 2):
        step = 1 << (mask.bit_length() - 1)
        sent = after(own) if mask == 4 else held[mask ^ step]
        held[mask] = swap(sent, "sec", step, sectors)
    return [block for mine in held.values() for block in (mine, swap(mine, "sec", 1))]


def place_rows(values):
    row = lax.broadcasted_iota(jnp.int32, TILE, 0)
    tile = jnp.zeros(TILE, jnp.float32)
    for position, value in values:
        tile = jnp.where(row == position, value, tile)
    return tile


def total(value):
    return jnp.sum(jnp.sum(value, axis=0, keepdims=True), axis=1, keepdims=True)


def inner_kernel(
    square_scale, vectors, left, right_hbm, offsets_hbm, inner, squares, right, offsets, sems
):
    fetches = [
        pltpu.make_async_copy(offsets_hbm, offsets, sems.at[0]),
        pltpu.make_async_copy(right_hbm, right, sems.at[1]),
    ]
    for fetch in fetches:
        fetch.start()
    terms, states = left.shape[0], left.shape[1]
    stacked = left[...].reshape(terms * states, states)
    sums = []
    for trial in range(vectors.shape[0]):
        square = jnp.zeros((8, states), jnp.float32)
        for pair in range(vectors.shape[1]):
            block = vectors[trial, pair]
            product = jnp.dot(stacked, block, preferred_element_type=jnp.float32)
            for term in range(terms):
                part = product[term * states : (term + 1) * states].astype(jnp.bfloat16)
                inner[trial, pair, :, term * states : (term + 1) * states] = part
            wide = block.astype(jnp.float32)
            square += jnp.sum((wide * wide).reshape(-1, 8, states), axis=0)
        sums.append(total(square) * square_scale)
    trials = len(sums)
    squares[...] = place_rows([(trials * trials + k, value) for k, value in enumerate(sums)])
    for fetch in fetches:
        fetch.wait()


def place_blocks(sectors, pieces, rights):
    odd = lax.axis_index("sec") & 1
    for mask in range(0, sectors, 2):
        even_place, odd_place = turned(mask, 0, sectors), turned(mask, 1, sectors)
        rights[jnp.where(odd == 1, odd_place, even_place)] = pieces[mask][...]
        if mask + 1 < len(pieces):
            rights[jnp.where(odd == 1, even_place, odd_place) ^ 1] = pieces[mask + 1][...]
    rights[sectors - 1] = jnp.zeros(rights.shape[1:], rights.dtype)


def needed_mask(sectors, offsets, term, pair):
    sector = lax.axis_index("sec")
    return sector ^ ((sector + offsets[term, pair]) & (sectors - 1))


def times_right(inner, term, pair, block):
    trials, _, states, _ = inner.shape
    lines = inner[:, pair, :, term * states : (term + 1) * states]
    product = jnp.dot(
        lines.reshape(trials * states, states), block, preferred_element_type=jnp.float32
    )
    return product.reshape(trials, states, states)


def sum_terms(sectors, pair, offsets, inner, rights):
    result = None
    for term in range(rights.shape[1]):
        mask = needed_mask(sectors, offsets, term, pair)
        added = times_right(inner, term, pair, rights[mask, term])
        result = added if result is None else result + added
    return result


def add_gram(vectors, pair, values, grams):
    trials, states = vectors.shape[0], vectors.shape[-1]
    for j in range(trials):
        for i in range(trials):
            spread = vectors[i, pair].astype(jnp.float32) * values[j]
            grams[i * trials + j] += jnp.sum(spread.reshape(-1, 8, states), axis=0)


def write_tile(before, grams, tile):
    count = grams.shape[0]
    tile[...] = before[...] + place_rows([(k, total(grams[k])) for k in range(count)])


def share_masks(shares, backwards):
    bits = shares.bit_length() - 1
    places = range(bits)
    if backwards:
        return [sum((k >> bit & 1) << (bits - 1 - bit) for bit in places) for k in range(shares)]
    return list(range(shares))


def write_shares(whole, backwards, slot, keep, send):
    shares = 2 * keep.shape[0]
    rows = whole.shape[1] // shares
    place = lax.axis_index("term")
    for k, mask in enumerate(share_masks(shares, backwards)):
        start = pl.multiple_of((place ^ mask) * rows, rows)
        share = whole[:, pl.ds(start, rows)]
        if k & 1:
            send[k // 2, :, slot] = share.astype(jnp.bfloat16)
        else:
            keep[k // 2, :, slot] = share


def early_kernel(sectors, offsets, vectors, inner, before, *rest):
    *pieces, partial, tile, rights, grams = rest
    place_blocks(sectors, pieces, rights)
    grams[...] = jnp.zeros_like(grams)
    for pair in range(partial.shape[0]):
        partial[pair] = sum_terms(sectors, pair, offsets, inner, rights)
        add_gram(vectors, pair, partial[pair], grams)
    write_tile(before, grams, tile)


def late_kernel(sectors, offsets, vectors, inner, before, partial, last, *rest):
    keep, send, tile, whole, grams = rest
    grams[...] = jnp.zeros_like(grams)
    for pair in range(partial.shape[0]):
        lacks = [
            needed_mask(sectors, offsets, term, pair) == sectors - 1
            for term in range(last.shape[0])
        ]
        lacking = functools.reduce(jnp.logical_or, lacks)
        write_shares(partial.at[pair], False, pair, keep, send)

        @pl.when(lacking)
        def _():
            whole[...] = partial[pair]
            for term, lack in enumerate(lacks):

                @pl.when(lack)
                def _():
                    added = times_right(inner, term, pair, last[term])
                    whole[...] += added
                    add_gram(vectors, pair, added, grams)

            write_shares(whole, False, pair, keep, send)

    write_tile(before, grams, tile)


def second_kernel(sectors, first, offsets, vectors, inner, before, rights, last, *rest):
    keep, send, tile, whole, grams = rest
    grams[...] = jnp.zeros_like(grams)
    for slot in range(keep.shape[2]):
        pair = first + slot
        whole[slot] = sum_terms(sectors, pair, offsets, inner, rights)
        for term in range(last.shape[0]):

            @pl.when(needed_mask(sectors, offsets, term, pair) == sectors - 1)
            def _():
                whole[slot] += times_right(inner, term, pair, last[term])

    for slot in range(keep.shape[2]):
        add_gram(vectors, first + slot, whole[slot], grams)
        write_shares(whole.at[slot], True, slot, keep, send)
    write_tile(before, grams, tile)


def halve_last_kernel(kept, received, tile, keep, send):
    keep[0] = kept[0] + received[0].astype(jnp.float32)
    both = kept[1] + received[1].astype(jnp.float32)
    lines = send.shape[0] - 2 * TILE[0]
    send[:lines] = both.astype(jnp.bfloat16).reshape(lines, send.shape[1])
    left, parts = tile[...], []
    for _ in range(3):
        parts.append(left.astype(jnp.bfloat16).astype(jnp.float32))
        left = left - parts[-1]
    block = jnp.concatenate(
        [
            jnp.concatenate([parts[0], parts[1]], axis=0),
            jnp.concatenate([parts[2], jnp.zeros_like(left)], axis=0),
        ],
        axis=1,
    )
    send[lines:] = block.astype(jnp.bfloat16)


def halve_kernel(kept, received, keep, send):
    for k in range(kept.shape[0]):
        both = kept[k] + received[k].astype(jnp.float32)
        if k & 1:
            send[k // 2] = both.astype(jnp.bfloat16)
        else:
            keep[k // 2] = both


def ridden_tile(received):
    height, width = TILE
    block = received[received.shape[0] - 2 * height :].astype(jnp.float32)
    return block[:height, :width] + block[height:, :width] + block[:height, width:]


def add_last_kernel(kept, received, result):
    result[...] = (kept[0] + received[0].astype(jnp.float32)).astype(jnp.bfloat16)


def finish_kernel(*refs):
    *done, kept, received, tile, products, rayleigh = refs
    first = 0
    for part in done:
        products[:, first : first + part.shape[1]] = part[...]
        first += part.shape[1]
    lines = received.shape[0] - 2 * TILE[0]
    both = received[:lines].astype(jnp.float32).reshape(kept.shape[1:])
    products[:, first:] = (kept[0] + both).astype(jnp.bfloat16)

    tile = tile[...] + ridden_tile(received)
    trials = rayleigh.shape[0]
    row = lax.broadcasted_iota(jnp.int32, rayleigh.shape, 0)
    column = lax.broadcasted_iota(jnp.int32, rayleigh.shape, 1)

    def entry(position):
        return tile[position : position + 1, :trials]

    result = jnp.zeros(rayleigh.shape, jnp.float32)
    for i in range(trials):
        for j in range(trials):
            squares = entry(trials * trials + i) * entry(trials * trials + j)
            value = entry(i * trials + j) / jnp.sqrt(squares)
            result = jnp.where((row == i) & (column == j), value, result)
    rayleigh[...] = result


def in_hbm(value):
    return pltpu.with_memory_space_constraint(value, pltpu.HBM)


def add_places(tile, axis, masks):
    parts = [tile] + [swap(tile, axis, mask) for mask in masks]
    return sum(parts[1:], parts[0])


def steps_of(count, low):
    steps = []
    while 1 << low < count:
        unit = 1 << low
        steps.append([unit, 2 * unit, 3 * unit] if 2 * unit < count else [unit])
        low += 2
    return steps


def call(kernel, name, flops, moved, limit, **kwargs):
    return pl.pallas_call(
        kernel,
        name=name,
        cost_estimate=pl.CostEstimate(flops=flops, bytes_accessed=moved, transcendentals=0),
        compiler_params=pltpu.CompilerParams(vmem_limit_bytes=limit),
        **kwargs,
    )


def local(vectors, left_ops, right_ops, offsets):
    sectors = lax.axis_size("sec")
    shares = lax.axis_size("term")
    trials, _, pairs, states, _ = vectors.shape
    terms = left_ops.shape[0]
    vectors, left, right = vectors[:, 0], left_ops[:, 0], right_ops[:, 0]
    rows = states // shares

    inner, tile, own, offsets = call(
        functools.partial(inner_kernel, 1.0 / shares),
        "inner_products",
        2 * terms * trials * pairs * states**3,
        5 * MIB,
        12 * MIB,
        out_shape=(
            jax.ShapeDtypeStruct((trials, pairs, states, terms * states), jnp.bfloat16),
            jax.ShapeDtypeStruct(TILE, jnp.float32),
            jax.ShapeDtypeStruct(right.shape, jnp.bfloat16),
            jax.ShapeDtypeStruct(offsets.shape, offsets.dtype),
        ),
        in_specs=[VMEM, VMEM, HBM, HBM],
        out_specs=(VMEM, VMEM, VMEM, VMEM),
        scratch_shapes=[pltpu.SemaphoreType.DMA((2,))],
    )(vectors, left, in_hbm(right), in_hbm(offsets))

    def behind_inner(block):
        return lax.optimization_barrier((block, inner))[0]

    gathered = gather_sectors(right, sectors, behind_inner)
    gathered[0] = own

    def share_of(count, size, dtype):
        return jax.ShapeDtypeStruct((count, trials, size, rows, states), dtype)

    tile_shape = jax.ShapeDtypeStruct(TILE, jnp.float32)
    rights_shape = jax.ShapeDtypeStruct((sectors, terms, states, states), jnp.bfloat16)
    sizes = [pairs // 2, pairs - pairs // 2]
    grams = pltpu.VMEM((trials * trials, 8, states), jnp.float32)
    *early, last = gathered
    partial, tile, rights = call(
        functools.partial(early_kernel, sectors),
        "early_products",
        2 * terms * trials * sizes[0] * states**3,
        4 * MIB,
        12 * MIB,
        out_shape=(
            jax.ShapeDtypeStruct((sizes[0], trials, states, states), jnp.float32),
            tile_shape,
            rights_shape,
        ),
        in_specs=[SMEM, VMEM, VMEM, VMEM] + [VMEM] * len(early),
        out_specs=(VMEM, VMEM, VMEM),
        scratch_shapes=[grams],
    )(offsets, vectors, inner, tile, *early)

    def sums_of(kernel, name, flops, size, scratch, *operands):
        return call(
            kernel,
            name,
            flops,
            MIB,
            12 * MIB,
            out_shape=(
                share_of(shares // 2, size, jnp.float32),
                share_of(shares // 2, size, jnp.bfloat16),
                tile_shape,
            ),
            in_specs=[SMEM] + [VMEM] * len(operands),
            out_specs=(VMEM, VMEM, VMEM),
            scratch_shapes=[pltpu.VMEM((*scratch, states, states), jnp.float32), grams],
        )(offsets, *operands)

    keep, send, tile = sums_of(
        functools.partial(late_kernel, sectors),
        "late_products",
        terms * trials * sizes[0] * states**3 // 4,
        sizes[0],
        (trials,),
        vectors,
        inner,
        tile,
        partial,
        last,
    )
    bits = [1 << bit for bit in range(shares.bit_length() - 1)]
    orders = [bits, bits[::-1]]
    sums = [(keep, swap(send, "term", bits[0]))]
    keep, send, tile = sums_of(
        functools.partial(second_kernel, sectors, sizes[0]),
        "second_products",
        2 * terms * trials * sizes[1] * states**3,
        sizes[1],
        (sizes[1], trials),
        vectors,
        inner,
        tile,
        rights,
        last,
    )
    sums.append((keep, swap(send, "term", bits[-1])))

    for masks in [[1]] + steps_of(sectors, 1):
        tile = add_places(tile, "sec", masks)

    keep, received = sums[0]
    received, tile = lax.optimization_barrier((received, tile))
    sums[0] = (keep, received)
    for bit in bits[1:]:
        tile = add_places(tile, "term", [bit])

    parts = []
    for chunk, (size, (keep, received), order) in enumerate(zip(sizes, sums, orders)):
        for step in order[1:]:
            count = keep.shape[0] // 2
            rides = count == 1 and chunk == len(sizes) - 1
            operands = (keep, received, tile) if rides else (keep, received)
            lines = trials * size * rows + 2 * TILE[0]
            keep, send = call(
                halve_last_kernel if rides else halve_kernel,
                "halve_rows",
                1,
                1,
                8 * MIB,
                out_shape=(
                    share_of(count, size, jnp.float32),
                    jax.ShapeDtypeStruct((lines, states), jnp.bfloat16)
                    if rides
                    else share_of(count, size, jnp.bfloat16),
                ),
                in_specs=[VMEM] * len(operands),
                out_specs=(VMEM, VMEM),
            )(*operands)
            received = swap(send, "term", step)
        parts += [keep, received]

    done = []
    for chunk, size in enumerate(sizes[:-1]):
        done.append(
            call(
                add_last_kernel,
                "add_last_share",
                10**8,
                1,
                8 * MIB,
                out_shape=jax.ShapeDtypeStruct((trials, size, rows, states), jnp.bfloat16),
                in_specs=[VMEM, VMEM],
                out_specs=VMEM,
            )(*parts[2 * chunk : 2 * chunk + 2])
        )
    products, rayleigh = call(
        finish_kernel,
        "finish",
        1,
        1,
        8 * MIB,
        out_shape=(
            jax.ShapeDtypeStruct((trials, pairs, rows, states), jnp.bfloat16),
            jax.ShapeDtypeStruct((trials, trials), jnp.float32),
        ),
        in_specs=[VMEM] * (len(done) + 3),
        out_specs=(VMEM, VMEM),
    )(*done, *parts[-2:], tile)
    return (products[:, None], rayleigh)


def solution(mesh):
    in_specs = (
        P(None, "sec", None, None, None),
        P("term", "sec", None, None),
        P("term", "sec", None, None),
        P("term", None),
    )
    out_specs = (P(None, "sec", None, "term", None), P())
    return jax.shard_map(local, mesh=mesh, in_specs=in_specs, out_specs=out_specs, check_vma=False)
```

```python
import functools

import jax
import jax.numpy as jnp
from jax import lax
from jax.experimental import pallas as pl
from jax.experimental.pallas import tpu as pltpu
from jax.sharding import PartitionSpec as P

MIB = 1 << 20
TILE = (8, 128)
VMEM = pl.BlockSpec(memory_space=pltpu.VMEM)
SMEM = pl.BlockSpec(memory_space=pltpu.SMEM)
HBM = pl.BlockSpec(memory_space=pltpu.HBM)


def swap(value, axis, mask, count=None):
    masks = [mask, mask] if count is None else [turned(mask, parity, count) for parity in range(2)]
    places = range(lax.axis_size(axis))
    return lax.ppermute(value, axis, [(place, place ^ masks[place & 1]) for place in places])


def turned(mask, parity, count):
    bits = count.bit_length() - 1
    if parity:
        return mask
    return sum(1 << (bits - bit) for bit in range(1, bits) if mask >> bit & 1) | mask & 1


def gather_sectors(own, sectors, after):
    held = {0: own}
    for mask in range(2, sectors, 2):
        step = 1 << (mask.bit_length() - 1)
        sent = after(own) if mask == 4 else held[mask ^ step]
        held[mask] = swap(sent, "sec", step, sectors)
    return [block for mine in held.values() for block in (mine, swap(mine, "sec", 1))]


def place_rows(values):
    row = lax.broadcasted_iota(jnp.int32, TILE, 0)
    tile = jnp.zeros(TILE, jnp.float32)
    for position, value in values:
        tile = jnp.where(row == position, value, tile)
    return tile


def total(value):
    return jnp.sum(jnp.sum(value, axis=0, keepdims=True), axis=1, keepdims=True)


def inner_kernel(
    square_scale,
    vectors_hbm,
    left_hbm,
    right_hbm,
    offsets_hbm,
    inner,
    squares,
    right,
    offsets,
    vectors,
    left,
    sems,
    block_sems,
):
    fetch_left = pltpu.make_async_copy(left_hbm, left, sems.at[2])
    fetch_left.start()
    pairs = vectors.shape[1]
    fetch_blocks = []
    for trial in range(vectors.shape[0]):
        for pair in range(pairs):
            place = trial * pairs + pair
            fetch = pltpu.make_async_copy(
                vectors_hbm.at[trial, pair], vectors.at[trial, pair], block_sems.at[place]
            )
            fetch.start()
            fetch_blocks.append(fetch)
    fetches = [
        pltpu.make_async_copy(offsets_hbm, offsets, sems.at[0]),
        pltpu.make_async_copy(right_hbm, right, sems.at[1]),
    ]
    for fetch in fetches:
        fetch.start()
    fetch_left.wait()
    terms, states = left.shape[0], left.shape[1]
    stacked = left[...].reshape(terms * states, states)
    sums = []
    for trial in range(vectors.shape[0]):
        square = jnp.zeros((8, states), jnp.float32)
        for pair in range(vectors.shape[1]):
            fetch_blocks[trial * pairs + pair].wait()
            block = vectors[trial, pair]
            product = jnp.dot(stacked, block, preferred_element_type=jnp.float32)
            for term in range(terms):
                part = product[term * states : (term + 1) * states].astype(jnp.bfloat16)
                inner[trial, pair, :, term * states : (term + 1) * states] = part
            wide = block.astype(jnp.float32)
            square += jnp.sum((wide * wide).reshape(-1, 8, states), axis=0)
        sums.append(total(square) * square_scale)
    trials = len(sums)
    squares[...] = place_rows([(trials * trials + k, value) for k, value in enumerate(sums)])
    for fetch in fetches:
        fetch.wait()


def place_blocks(sectors, pieces, rights):
    odd = lax.axis_index("sec") & 1
    for mask in range(0, sectors, 2):
        even_place, odd_place = turned(mask, 0, sectors), turned(mask, 1, sectors)
        rights[jnp.where(odd == 1, odd_place, even_place)] = pieces[mask][...]
        if mask + 1 < len(pieces):
            rights[jnp.where(odd == 1, even_place, odd_place) ^ 1] = pieces[mask + 1][...]
    rights[sectors - 1] = jnp.zeros(rights.shape[1:], rights.dtype)


def needed_mask(sectors, offsets, term, pair):
    sector = lax.axis_index("sec")
    return sector ^ ((sector + offsets[term, pair]) & (sectors - 1))


def times_right(inner, term, pair, block):
    trials, _, states, _ = inner.shape
    lines = inner[:, pair, :, term * states : (term + 1) * states]
    product = jnp.dot(
        lines.reshape(trials * states, states), block, preferred_element_type=jnp.float32
    )
    return product.reshape(trials, states, states)


def sum_terms(sectors, pair, offsets, inner, rights):
    result = None
    for term in range(rights.shape[1]):
        mask = needed_mask(sectors, offsets, term, pair)
        added = times_right(inner, term, pair, rights[mask, term])
        result = added if result is None else result + added
    return result


def add_gram(vectors, pair, values, grams):
    trials, states = vectors.shape[0], vectors.shape[-1]
    for j in range(trials):
        for i in range(trials):
            spread = vectors[i, pair].astype(jnp.float32) * values[j]
            grams[i * trials + j] += jnp.sum(spread.reshape(-1, 8, states), axis=0)


def write_tile(before, grams, tile):
    count = grams.shape[0]
    tile[...] = before[...] + place_rows([(k, total(grams[k])) for k in range(count)])


def write_shares(whole, slot, keep, send):
    shares = 2 * keep.shape[0]
    rows = whole.shape[1] // shares
    place = lax.axis_index("term")
    for mask in range(shares):
        start = pl.multiple_of((place ^ mask) * rows, rows)
        share = whole[:, pl.ds(start, rows)]
        if mask & 1:
            send[mask // 2, :, slot] = share.astype(jnp.bfloat16)
        else:
            keep[mask // 2, :, slot] = share


def early_kernel(sectors, offsets, vectors, inner, before, *rest):
    *pieces, partial, tile, rights, grams = rest
    place_blocks(sectors, pieces, rights)
    grams[...] = jnp.zeros_like(grams)
    for pair in range(partial.shape[0]):
        partial[pair] = sum_terms(sectors, pair, offsets, inner, rights)
        add_gram(vectors, pair, partial[pair], grams)
    write_tile(before, grams, tile)


def late_kernel(sectors, offsets, vectors, inner, before, partial, last, *rest):
    keep, send, tile, whole, grams = rest
    grams[...] = jnp.zeros_like(grams)
    for pair in range(partial.shape[0]):
        lacks = [
            needed_mask(sectors, offsets, term, pair) == sectors - 1
            for term in range(last.shape[0])
        ]
        lacking = functools.reduce(jnp.logical_or, lacks)
        write_shares(partial.at[pair], pair, keep, send)

        @pl.when(lacking)
        def _():
            whole[...] = partial[pair]
            for term, lack in enumerate(lacks):

                @pl.when(lack)
                def _():
                    added = times_right(inner, term, pair, last[term])
                    whole[...] += added
                    add_gram(vectors, pair, added, grams)

            write_shares(whole, pair, keep, send)

    write_tile(before, grams, tile)


def second_kernel(sectors, first, offsets, vectors, inner, before, rights, last, *rest):
    keep, send, tile, whole, grams = rest
    grams[...] = jnp.zeros_like(grams)
    for slot in range(keep.shape[2]):
        pair = first + slot
        whole[slot] = sum_terms(sectors, pair, offsets, inner, rights)
        for term in range(last.shape[0]):

            @pl.when(needed_mask(sectors, offsets, term, pair) == sectors - 1)
            def _():
                whole[slot] += times_right(inner, term, pair, last[term])

    for slot in range(keep.shape[2]):
        add_gram(vectors, first + slot, whole[slot], grams)
        write_shares(whole.at[slot], slot, keep, send)
    write_tile(before, grams, tile)


def halve_last_kernel(kept, received, tile, keep, send):
    keep[0] = kept[0] + received[0].astype(jnp.float32)
    both = kept[1] + received[1].astype(jnp.float32)
    lines = send.shape[0] - 2 * TILE[0]
    send[:lines] = both.astype(jnp.bfloat16).reshape(lines, send.shape[1])
    left, parts = tile[...], []
    for _ in range(3):
        parts.append(left.astype(jnp.bfloat16).astype(jnp.float32))
        left = left - parts[-1]
    block = jnp.concatenate(
        [
            jnp.concatenate([parts[0], parts[1]], axis=0),
            jnp.concatenate([parts[2], jnp.zeros_like(left)], axis=0),
        ],
        axis=1,
    )
    send[lines:] = block.astype(jnp.bfloat16)


def halve_kernel(kept, received, keep, send):
    for k in range(kept.shape[0]):
        both = kept[k] + received[k].astype(jnp.float32)
        if k & 1:
            send[k // 2] = both.astype(jnp.bfloat16)
        else:
            keep[k // 2] = both


def ridden_tile(received):
    height, width = TILE
    block = received[received.shape[0] - 2 * height :].astype(jnp.float32)
    return block[:height, :width] + block[height:, :width] + block[:height, width:]


def add_last_kernel(kept, received, result):
    result[...] = (kept[0] + received[0].astype(jnp.float32)).astype(jnp.bfloat16)


def finish_kernel(*refs):
    *done, kept, received, tile, products, rayleigh = refs
    first = 0
    for part in done:
        products[:, first : first + part.shape[1]] = part[...]
        first += part.shape[1]
    lines = received.shape[0] - 2 * TILE[0]
    both = received[:lines].astype(jnp.float32).reshape(kept.shape[1:])
    products[:, first:] = (kept[0] + both).astype(jnp.bfloat16)

    tile = tile[...] + ridden_tile(received)
    trials = rayleigh.shape[0]
    row = lax.broadcasted_iota(jnp.int32, rayleigh.shape, 0)
    column = lax.broadcasted_iota(jnp.int32, rayleigh.shape, 1)

    def entry(position):
        return tile[position : position + 1, :trials]

    result = jnp.zeros(rayleigh.shape, jnp.float32)
    for i in range(trials):
        for j in range(trials):
            squares = entry(trials * trials + i) * entry(trials * trials + j)
            value = entry(i * trials + j) / jnp.sqrt(squares)
            result = jnp.where((row == i) & (column == j), value, result)
    rayleigh[...] = result


def in_hbm(value):
    return pltpu.with_memory_space_constraint(value, pltpu.HBM)


def add_places(tile, axis, masks):
    parts = [tile] + [swap(tile, axis, mask) for mask in masks]
    return sum(parts[1:], parts[0])


def steps_of(count, low):
    steps = []
    while 1 << low < count:
        unit = 1 << low
        steps.append([unit, 2 * unit, 3 * unit] if 2 * unit < count else [unit])
        low += 2
    return steps


def call(kernel, name, flops, moved, limit, **kwargs):
    return pl.pallas_call(
        kernel,
        name=name,
        cost_estimate=pl.CostEstimate(flops=flops, bytes_accessed=moved, transcendentals=0),
        compiler_params=pltpu.CompilerParams(vmem_limit_bytes=limit),
        **kwargs,
    )


def local(vectors, left_ops, right_ops, offsets):
    sectors = lax.axis_size("sec")
    shares = lax.axis_size("term")
    trials, _, pairs, states, _ = vectors.shape
    terms = left_ops.shape[0]
    vectors, left, right = vectors[:, 0], left_ops[:, 0], right_ops[:, 0]
    rows = states // shares

    inner, tile, own, offsets = call(
        functools.partial(inner_kernel, 1.0 / shares),
        "inner_products",
        2 * terms * trials * pairs * states**3,
        5 * MIB,
        12 * MIB,
        out_shape=(
            jax.ShapeDtypeStruct((trials, pairs, states, terms * states), jnp.bfloat16),
            jax.ShapeDtypeStruct(TILE, jnp.float32),
            jax.ShapeDtypeStruct(right.shape, jnp.bfloat16),
            jax.ShapeDtypeStruct(offsets.shape, offsets.dtype),
        ),
        in_specs=[HBM, HBM, HBM, HBM],
        out_specs=(VMEM, VMEM, VMEM, VMEM),
        scratch_shapes=[
            pltpu.VMEM(vectors.shape, jnp.bfloat16),
            pltpu.VMEM(left.shape, jnp.bfloat16),
            pltpu.SemaphoreType.DMA((3,)),
            pltpu.SemaphoreType.DMA((trials * pairs,)),
        ],
    )(in_hbm(vectors), in_hbm(left), in_hbm(right), in_hbm(offsets))

    def behind_inner(block):
        return lax.optimization_barrier((block, inner))[0]

    gathered = gather_sectors(right, sectors, behind_inner)
    gathered[0] = own

    def share_of(count, size, dtype):
        return jax.ShapeDtypeStruct((count, trials, size, rows, states), dtype)

    tile_shape = jax.ShapeDtypeStruct(TILE, jnp.float32)
    rights_shape = jax.ShapeDtypeStruct((sectors, terms, states, states), jnp.bfloat16)
    sizes = [pairs // 2, pairs - pairs // 2]
    grams = pltpu.VMEM((trials * trials, 8, states), jnp.float32)
    *early, last = gathered
    partial, tile, rights = call(
        functools.partial(early_kernel, sectors),
        "early_products",
        2 * terms * trials * sizes[0] * states**3,
        4 * MIB,
        12 * MIB,
        out_shape=(
            jax.ShapeDtypeStruct((sizes[0], trials, states, states), jnp.float32),
            tile_shape,
            rights_shape,
        ),
        in_specs=[SMEM, VMEM, VMEM, VMEM] + [VMEM] * len(early),
        out_specs=(VMEM, VMEM, VMEM),
        scratch_shapes=[grams],
    )(offsets, vectors, inner, tile, *early)

    def sums_of(kernel, name, flops, size, scratch, *operands):
        return call(
            kernel,
            name,
            flops,
            MIB,
            12 * MIB,
            out_shape=(
                share_of(shares // 2, size, jnp.float32),
                share_of(shares // 2, size, jnp.bfloat16),
                tile_shape,
            ),
            in_specs=[SMEM] + [VMEM] * len(operands),
            out_specs=(VMEM, VMEM, VMEM),
            scratch_shapes=[pltpu.VMEM((*scratch, states, states), jnp.float32), grams],
        )(offsets, *operands)

    keep, send, tile = sums_of(
        functools.partial(late_kernel, sectors),
        "late_products",
        terms * trials * sizes[0] * states**3 // 4,
        sizes[0],
        (trials,),
        vectors,
        inner,
        tile,
        partial,
        last,
    )
    sums = [(keep, swap(send, "term", 1))]
    keep, send, tile = sums_of(
        functools.partial(second_kernel, sectors, sizes[0]),
        "second_products",
        2 * terms * trials * sizes[1] * states**3,
        sizes[1],
        (sizes[1], trials),
        vectors,
        inner,
        tile,
        rights,
        last,
    )
    sums.append((keep, swap(send, "term", 1)))

    for masks in [[1]] + steps_of(sectors, 1):
        tile = add_places(tile, "sec", masks)

    step = 1
    while 2 * step < shares:
        tile = add_places(tile, "term", [step])
        step *= 2

    parts = []
    for chunk, size in enumerate(sizes):
        keep, received = sums[chunk]
        step = 1
        while 2 * step < shares:
            step *= 2
            count = shares // (2 * step)
            last = count == 1 and chunk == len(sizes) - 1
            operands = (keep, received, tile) if last else (keep, received)
            lines = trials * size * rows + 2 * TILE[0]
            keep, send = call(
                halve_last_kernel if last else halve_kernel,
                "halve_rows",
                1,
                1,
                8 * MIB,
                out_shape=(
                    share_of(count, size, jnp.float32),
                    jax.ShapeDtypeStruct((lines, states), jnp.bfloat16)
                    if last
                    else share_of(count, size, jnp.bfloat16),
                ),
                in_specs=[VMEM] * len(operands),
                out_specs=(VMEM, VMEM),
            )(*operands)
            received = swap(send, "term", step)
        parts += [keep, received]

    done = []
    for chunk, size in enumerate(sizes[:-1]):
        done.append(
            call(
                add_last_kernel,
                "add_last_share",
                10**10,
                1,
                8 * MIB,
                out_shape=jax.ShapeDtypeStruct((trials, size, rows, states), jnp.bfloat16),
                in_specs=[VMEM, VMEM],
                out_specs=VMEM,
            )(*parts[2 * chunk : 2 * chunk + 2])
        )
    products, rayleigh = call(
        finish_kernel,
        "finish",
        1,
        1,
        8 * MIB,
        out_shape=(
            jax.ShapeDtypeStruct((trials, pairs, rows, states), jnp.bfloat16),
            jax.ShapeDtypeStruct((trials, trials), jnp.float32),
        ),
        in_specs=[VMEM] * (len(done) + 3),
        out_specs=(VMEM, VMEM),
    )(*done, *parts[-2:], tile)
    return (products[:, None], rayleigh)


def solution(mesh):
    in_specs = (
        P(None, "sec", None, None, None),
        P("term", "sec", None, None),
        P("term", "sec", None, None),
        P("term", None),
    )
    out_specs = (P(None, "sec", None, "term", None), P())
    return jax.shard_map(local, mesh=mesh, in_specs=in_specs, out_specs=out_specs, check_vma=False)
```

```python
import functools

import jax
import jax.numpy as jnp
from jax import lax
from jax.experimental import pallas as pl
from jax.experimental.pallas import tpu as pltpu
from jax.sharding import PartitionSpec as P

MIB = 1 << 20
TILE = (8, 128)
VMEM = pl.BlockSpec(memory_space=pltpu.VMEM)
SMEM = pl.BlockSpec(memory_space=pltpu.SMEM)
HBM = pl.BlockSpec(memory_space=pltpu.HBM)


def swap(value, axis, mask, count=None):
    masks = [mask, mask] if count is None else [turned(mask, parity, count) for parity in range(2)]
    places = range(lax.axis_size(axis))
    return lax.ppermute(value, axis, [(place, place ^ masks[place & 1]) for place in places])


def turned(mask, parity, count):
    bits = count.bit_length() - 1
    if parity:
        return mask
    return sum(1 << (bits - bit) for bit in range(1, bits) if mask >> bit & 1) | mask & 1


def gather_sectors(own, sectors, after):
    held = {0: own}
    for mask in range(2, sectors, 2):
        step = 1 << (mask.bit_length() - 1)
        sent = after(own) if mask == 4 else held[mask ^ step]
        held[mask] = swap(sent, "sec", step, sectors)
    return [block for mine in held.values() for block in (mine, swap(mine, "sec", 1))]


def place_rows(values):
    row = lax.broadcasted_iota(jnp.int32, TILE, 0)
    tile = jnp.zeros(TILE, jnp.float32)
    for position, value in values:
        tile = jnp.where(row == position, value, tile)
    return tile


def total(value):
    return jnp.sum(jnp.sum(value, axis=0, keepdims=True), axis=1, keepdims=True)


def inner_kernel(
    square_scale, vectors, left, right_hbm, offsets_hbm, inner, squares, right, offsets, sems
):
    fetches = [
        pltpu.make_async_copy(offsets_hbm, offsets, sems.at[0]),
        pltpu.make_async_copy(right_hbm, right, sems.at[1]),
    ]
    for fetch in fetches:
        fetch.start()
    terms, states = left.shape[0], left.shape[1]
    stacked = left[...].reshape(terms * states, states)
    sums = []
    for trial in range(vectors.shape[0]):
        square = jnp.zeros((8, states), jnp.float32)
        for pair in range(vectors.shape[1]):
            block = vectors[trial, pair]
            product = jnp.dot(stacked, block, preferred_element_type=jnp.float32)
            for term in range(terms):
                part = product[term * states : (term + 1) * states].astype(jnp.bfloat16)
                inner[trial, pair, :, term * states : (term + 1) * states] = part
            wide = block.astype(jnp.float32)
            square += jnp.sum((wide * wide).reshape(-1, 8, states), axis=0)
        sums.append(total(square) * square_scale)
    trials = len(sums)
    squares[...] = place_rows([(trials * trials + k, value) for k, value in enumerate(sums)])
    for fetch in fetches:
        fetch.wait()


def place_blocks(sectors, pieces, rights):
    odd = lax.axis_index("sec") & 1
    for mask in range(0, sectors, 2):
        even_place, odd_place = turned(mask, 0, sectors), turned(mask, 1, sectors)
        rights[jnp.where(odd == 1, odd_place, even_place)] = pieces[mask][...]
        if mask + 1 < len(pieces):
            rights[jnp.where(odd == 1, even_place, odd_place) ^ 1] = pieces[mask + 1][...]
    rights[sectors - 1] = jnp.zeros(rights.shape[1:], rights.dtype)


def needed_mask(sectors, offsets, term, pair):
    sector = lax.axis_index("sec")
    return sector ^ ((sector + offsets[term, pair]) & (sectors - 1))


def times_right(inner, term, pair, block):
    trials, _, states, _ = inner.shape
    lines = inner[:, pair, :, term * states : (term + 1) * states]
    product = jnp.dot(
        lines.reshape(trials * states, states), block, preferred_element_type=jnp.float32
    )
    return product.reshape(trials, states, states)


def sum_terms(sectors, pair, offsets, inner, rights):
    result = None
    for term in range(rights.shape[1]):
        mask = needed_mask(sectors, offsets, term, pair)
        added = times_right(inner, term, pair, rights[mask, term])
        result = added if result is None else result + added
    return result


def add_gram(vectors, pair, values, grams):
    trials, states = vectors.shape[0], vectors.shape[-1]
    for j in range(trials):
        for i in range(trials):
            spread = vectors[i, pair].astype(jnp.float32) * values[j]
            grams[i * trials + j] += jnp.sum(spread.reshape(-1, 8, states), axis=0)


def write_tile(before, grams, tile):
    count = grams.shape[0]
    tile[...] = before[...] + place_rows([(k, total(grams[k])) for k in range(count)])


def write_shares(whole, slot, keep, send):
    shares = 2 * keep.shape[0]
    rows = whole.shape[1] // shares
    place = lax.axis_index("term")
    for mask in range(shares):
        start = pl.multiple_of((place ^ mask) * rows, rows)
        share = whole[:, pl.ds(start, rows)]
        if mask & 1:
            send[mask // 2, :, slot] = share.astype(jnp.bfloat16)
        else:
            keep[mask // 2, :, slot] = share


def early_kernel(sectors, offsets, vectors, inner, before, *rest):
    *pieces, partial, tile, rights, grams = rest
    place_blocks(sectors, pieces, rights)
    grams[...] = jnp.zeros_like(grams)
    for pair in range(partial.shape[0]):
        partial[pair] = sum_terms(sectors, pair, offsets, inner, rights)
        add_gram(vectors, pair, partial[pair], grams)
    write_tile(before, grams, tile)


def late_kernel(sectors, offsets, vectors, inner, before, partial, last, *rest):
    keep, send, tile, whole, grams = rest
    grams[...] = jnp.zeros_like(grams)
    for pair in range(partial.shape[0]):
        lacks = [
            needed_mask(sectors, offsets, term, pair) == sectors - 1
            for term in range(last.shape[0])
        ]
        lacking = functools.reduce(jnp.logical_or, lacks)
        write_shares(partial.at[pair], pair, keep, send)

        @pl.when(lacking)
        def _():
            whole[...] = partial[pair]
            for term, lack in enumerate(lacks):

                @pl.when(lack)
                def _():
                    added = times_right(inner, term, pair, last[term])
                    whole[...] += added
                    add_gram(vectors, pair, added, grams)

            write_shares(whole, pair, keep, send)

    write_tile(before, grams, tile)


def second_kernel(sectors, first, offsets, vectors, inner, before, rights, last, *rest):
    keep, send, tile, whole, grams = rest
    grams[...] = jnp.zeros_like(grams)
    for slot in range(keep.shape[2]):
        pair = first + slot
        whole[slot] = sum_terms(sectors, pair, offsets, inner, rights)
        for term in range(last.shape[0]):

            @pl.when(needed_mask(sectors, offsets, term, pair) == sectors - 1)
            def _():
                whole[slot] += times_right(inner, term, pair, last[term])

    for slot in range(keep.shape[2]):
        add_gram(vectors, first + slot, whole[slot], grams)
        write_shares(whole.at[slot], slot, keep, send)
    write_tile(before, grams, tile)


def halve_last_kernel(kept, received, tile, keep, send):
    keep[0] = kept[0] + received[0].astype(jnp.float32)
    both = kept[1] + received[1].astype(jnp.float32)
    lines = send.shape[0] - 2 * TILE[0]
    send[:lines] = both.astype(jnp.bfloat16).reshape(lines, send.shape[1])
    left, parts = tile[...], []
    for _ in range(3):
        parts.append(left.astype(jnp.bfloat16).astype(jnp.float32))
        left = left - parts[-1]
    block = jnp.concatenate(
        [
            jnp.concatenate([parts[0], parts[1]], axis=0),
            jnp.concatenate([parts[2], jnp.zeros_like(left)], axis=0),
        ],
        axis=1,
    )
    send[lines:] = block.astype(jnp.bfloat16)


def halve_kernel(kept, received, keep, send):
    for k in range(kept.shape[0]):
        both = kept[k] + received[k].astype(jnp.float32)
        if k & 1:
            send[k // 2] = both.astype(jnp.bfloat16)
        else:
            keep[k // 2] = both


def ridden_tile(received):
    height, width = TILE
    block = received[received.shape[0] - 2 * height :].astype(jnp.float32)
    return block[:height, :width] + block[height:, :width] + block[:height, width:]


def add_last_kernel(kept, received, result):
    result[...] = (kept[0] + received[0].astype(jnp.float32)).astype(jnp.bfloat16)


def finish_kernel(*refs):
    *done, kept, received, tile, products, rayleigh_hbm, rows, rayleigh, sems = refs
    copies, first = [], 0
    for part in [*done, rows]:
        target = products.at[:, pl.ds(first, part.shape[1])]
        copies.append(pltpu.make_async_copy(part, target, sems.at[len(copies)]))
        first += part.shape[1]
    for copy in copies[:-1]:
        copy.start()
    lines = received.shape[0] - 2 * TILE[0]
    both = received[:lines].astype(jnp.float32).reshape(kept.shape[1:])
    rows[...] = (kept[0] + both).astype(jnp.bfloat16)
    copies[-1].start()

    tile = tile[...] + ridden_tile(received)
    trials = rayleigh.shape[0]
    row = lax.broadcasted_iota(jnp.int32, rayleigh.shape, 0)
    column = lax.broadcasted_iota(jnp.int32, rayleigh.shape, 1)

    def entry(position):
        return tile[position : position + 1, :trials]

    result = jnp.zeros(rayleigh.shape, jnp.float32)
    for i in range(trials):
        for j in range(trials):
            squares = entry(trials * trials + i) * entry(trials * trials + j)
            value = entry(i * trials + j) / jnp.sqrt(squares)
            result = jnp.where((row == i) & (column == j), value, result)
    rayleigh[...] = result
    last = pltpu.make_async_copy(rayleigh, rayleigh_hbm, sems.at[len(copies)])
    last.start()
    for copy in [*copies, last]:
        copy.wait()


def in_hbm(value):
    return pltpu.with_memory_space_constraint(value, pltpu.HBM)


def add_places(tile, axis, masks):
    parts = [tile] + [swap(tile, axis, mask) for mask in masks]
    return sum(parts[1:], parts[0])


def steps_of(count, low):
    steps = []
    while 1 << low < count:
        unit = 1 << low
        steps.append([unit, 2 * unit, 3 * unit] if 2 * unit < count else [unit])
        low += 2
    return steps


def call(kernel, name, flops, moved, limit, **kwargs):
    return pl.pallas_call(
        kernel,
        name=name,
        cost_estimate=pl.CostEstimate(flops=flops, bytes_accessed=moved, transcendentals=0),
        compiler_params=pltpu.CompilerParams(vmem_limit_bytes=limit),
        **kwargs,
    )


def local(vectors, left_ops, right_ops, offsets):
    sectors = lax.axis_size("sec")
    shares = lax.axis_size("term")
    trials, _, pairs, states, _ = vectors.shape
    terms = left_ops.shape[0]
    vectors, left, right = vectors[:, 0], left_ops[:, 0], right_ops[:, 0]
    rows = states // shares

    inner, tile, own, offsets = call(
        functools.partial(inner_kernel, 1.0 / shares),
        "inner_products",
        2 * terms * trials * pairs * states**3,
        5 * MIB,
        12 * MIB,
        out_shape=(
            jax.ShapeDtypeStruct((trials, pairs, states, terms * states), jnp.bfloat16),
            jax.ShapeDtypeStruct(TILE, jnp.float32),
            jax.ShapeDtypeStruct(right.shape, jnp.bfloat16),
            jax.ShapeDtypeStruct(offsets.shape, offsets.dtype),
        ),
        in_specs=[VMEM, VMEM, HBM, HBM],
        out_specs=(VMEM, VMEM, VMEM, VMEM),
        scratch_shapes=[pltpu.SemaphoreType.DMA((2,))],
    )(vectors, left, in_hbm(right), in_hbm(offsets))

    def behind_inner(block):
        return lax.optimization_barrier((block, inner))[0]

    gathered = gather_sectors(right, sectors, behind_inner)
    gathered[0] = own

    def share_of(count, size, dtype):
        return jax.ShapeDtypeStruct((count, trials, size, rows, states), dtype)

    tile_shape = jax.ShapeDtypeStruct(TILE, jnp.float32)
    rights_shape = jax.ShapeDtypeStruct((sectors, terms, states, states), jnp.bfloat16)
    sizes = [pairs // 2, pairs - pairs // 2]
    grams = pltpu.VMEM((trials * trials, 8, states), jnp.float32)
    *early, last = gathered
    partial, tile, rights = call(
        functools.partial(early_kernel, sectors),
        "early_products",
        2 * terms * trials * sizes[0] * states**3,
        4 * MIB,
        12 * MIB,
        out_shape=(
            jax.ShapeDtypeStruct((sizes[0], trials, states, states), jnp.float32),
            tile_shape,
            rights_shape,
        ),
        in_specs=[SMEM, VMEM, VMEM, VMEM] + [VMEM] * len(early),
        out_specs=(VMEM, VMEM, VMEM),
        scratch_shapes=[grams],
    )(offsets, vectors, inner, tile, *early)

    def sums_of(kernel, name, flops, size, scratch, *operands):
        return call(
            kernel,
            name,
            flops,
            MIB,
            12 * MIB,
            out_shape=(
                share_of(shares // 2, size, jnp.float32),
                share_of(shares // 2, size, jnp.bfloat16),
                tile_shape,
            ),
            in_specs=[SMEM] + [VMEM] * len(operands),
            out_specs=(VMEM, VMEM, VMEM),
            scratch_shapes=[pltpu.VMEM((*scratch, states, states), jnp.float32), grams],
        )(offsets, *operands)

    keep, send, tile = sums_of(
        functools.partial(late_kernel, sectors),
        "late_products",
        terms * trials * sizes[0] * states**3 // 4,
        sizes[0],
        (trials,),
        vectors,
        inner,
        tile,
        partial,
        last,
    )
    sums = [(keep, swap(send, "term", 1))]
    keep, send, tile = sums_of(
        functools.partial(second_kernel, sectors, sizes[0]),
        "second_products",
        2 * terms * trials * sizes[1] * states**3,
        sizes[1],
        (sizes[1], trials),
        vectors,
        inner,
        tile,
        rights,
        last,
    )
    sums.append((keep, swap(send, "term", 1)))

    for masks in [[1]] + steps_of(sectors, 1):
        tile = add_places(tile, "sec", masks)

    step = 1
    while 2 * step < shares:
        tile = add_places(tile, "term", [step])
        step *= 2

    parts = []
    for chunk, size in enumerate(sizes):
        keep, received = sums[chunk]
        step = 1
        while 2 * step < shares:
            step *= 2
            count = shares // (2 * step)
            last = count == 1 and chunk == len(sizes) - 1
            operands = (keep, received, tile) if last else (keep, received)
            lines = trials * size * rows + 2 * TILE[0]
            keep, send = call(
                halve_last_kernel if last else halve_kernel,
                "halve_rows",
                1,
                1,
                8 * MIB,
                out_shape=(
                    share_of(count, size, jnp.float32),
                    jax.ShapeDtypeStruct((lines, states), jnp.bfloat16)
                    if last
                    else share_of(count, size, jnp.bfloat16),
                ),
                in_specs=[VMEM] * len(operands),
                out_specs=(VMEM, VMEM),
            )(*operands)
            received = swap(send, "term", step)
        parts += [keep, received]

    done = []
    for chunk, size in enumerate(sizes[:-1]):
        done.append(
            call(
                add_last_kernel,
                "add_last_share",
                10**10,
                1,
                8 * MIB,
                out_shape=jax.ShapeDtypeStruct((trials, size, rows, states), jnp.bfloat16),
                in_specs=[VMEM, VMEM],
                out_specs=VMEM,
            )(*parts[2 * chunk : 2 * chunk + 2])
        )
    products, rayleigh = call(
        finish_kernel,
        "finish",
        1,
        1,
        8 * MIB,
        out_shape=(
            jax.ShapeDtypeStruct((trials, pairs, rows, states), jnp.bfloat16),
            jax.ShapeDtypeStruct((trials, trials), jnp.float32),
        ),
        in_specs=[VMEM] * (len(done) + 3),
        out_specs=(HBM, HBM),
        scratch_shapes=[
            pltpu.VMEM((trials, sizes[-1], rows, states), jnp.bfloat16),
            pltpu.VMEM((trials, trials), jnp.float32),
            pltpu.SemaphoreType.DMA((len(sizes) + 1,)),
        ],
    )(*done, *parts[-2:], tile)
    return (products[:, None], rayleigh)


def solution(mesh):
    in_specs = (
        P(None, "sec", None, None, None),
        P("term", "sec", None, None),
        P("term", "sec", None, None),
        P("term", None),
    )
    out_specs = (P(None, "sec", None, "term", None), P())
    return jax.shard_map(local, mesh=mesh, in_specs=in_specs, out_specs=out_specs, check_vma=False)
```

```python
import functools

import jax
import jax.numpy as jnp
from jax import lax
from jax.experimental import pallas as pl
from jax.experimental.pallas import tpu as pltpu
from jax.sharding import PartitionSpec as P

MIB = 1 << 20
TILE = (8, 128)
VMEM = pl.BlockSpec(memory_space=pltpu.VMEM)
SMEM = pl.BlockSpec(memory_space=pltpu.SMEM)
HBM = pl.BlockSpec(memory_space=pltpu.HBM)


def swap(value, axis, mask, count=None):
    masks = [mask, mask] if count is None else [turned(mask, parity, count) for parity in range(2)]
    places = range(lax.axis_size(axis))
    return lax.ppermute(value, axis, [(place, place ^ masks[place & 1]) for place in places])


def turned(mask, parity, count):
    bits = count.bit_length() - 1
    if parity:
        return mask
    return sum(1 << (bits - bit) for bit in range(1, bits) if mask >> bit & 1) | mask & 1


def gather_sectors(own, sectors, after):
    held = {0: own}
    for mask in range(2, sectors, 2):
        step = 1 << (mask.bit_length() - 1)
        sent = after(own) if mask == 4 else held[mask ^ step]
        held[mask] = swap(sent, "sec", step, sectors)
    return [block for mine in held.values() for block in (mine, swap(mine, "sec", 1))]


def place_rows(values):
    row = lax.broadcasted_iota(jnp.int32, TILE, 0)
    tile = jnp.zeros(TILE, jnp.float32)
    for position, value in values:
        tile = jnp.where(row == position, value, tile)
    return tile


def total(value):
    return jnp.sum(jnp.sum(value, axis=0, keepdims=True), axis=1, keepdims=True)


def inner_kernel(
    square_scale, vectors, left, right_hbm, offsets_hbm, inner, squares, right, offsets, sems
):
    fetches = [
        pltpu.make_async_copy(offsets_hbm, offsets, sems.at[0]),
        pltpu.make_async_copy(right_hbm, right, sems.at[1]),
    ]
    for fetch in fetches:
        fetch.start()
    terms, states = left.shape[0], left.shape[1]
    stacked = left[...].reshape(terms * states, states)
    sums = []
    for trial in range(vectors.shape[0]):
        square = jnp.zeros((8, states), jnp.float32)
        for pair in range(vectors.shape[1]):
            block = vectors[trial, pair]
            product = jnp.dot(stacked, block, preferred_element_type=jnp.float32)
            for term in range(terms):
                part = product[term * states : (term + 1) * states].astype(jnp.bfloat16)
                inner[trial, pair, :, term * states : (term + 1) * states] = part
            wide = block.astype(jnp.float32)
            square += jnp.sum((wide * wide).reshape(-1, 8, states), axis=0)
        sums.append(total(square) * square_scale)
    trials = len(sums)
    squares[...] = place_rows([(trials * trials + k, value) for k, value in enumerate(sums)])
    for fetch in fetches:
        fetch.wait()


def place_blocks(sectors, pieces, rights):
    odd = lax.axis_index("sec") & 1
    for mask in range(0, sectors, 2):
        even_place, odd_place = turned(mask, 0, sectors), turned(mask, 1, sectors)
        rights[jnp.where(odd == 1, odd_place, even_place)] = pieces[mask][...]
        if mask + 1 < len(pieces):
            rights[jnp.where(odd == 1, even_place, odd_place) ^ 1] = pieces[mask + 1][...]
    rights[sectors - 1] = jnp.zeros(rights.shape[1:], rights.dtype)


def needed_mask(sectors, offsets, term, pair):
    sector = lax.axis_index("sec")
    return sector ^ ((sector + offsets[term, pair]) & (sectors - 1))


def times_right(inner, term, pair, block):
    trials, _, states, _ = inner.shape
    lines = inner[:, pair, :, term * states : (term + 1) * states]
    product = jnp.dot(
        lines.reshape(trials * states, states), block, preferred_element_type=jnp.float32
    )
    return product.reshape(trials, states, states)


def sum_terms(sectors, pair, offsets, inner, rights):
    result = None
    for term in range(rights.shape[1]):
        mask = needed_mask(sectors, offsets, term, pair)
        added = times_right(inner, term, pair, rights[mask, term])
        result = added if result is None else result + added
    return result


def add_gram(vectors, pair, values, grams):
    trials, states = vectors.shape[0], vectors.shape[-1]
    for j in range(trials):
        for i in range(trials):
            spread = vectors[i, pair].astype(jnp.float32) * values[j]
            grams[i * trials + j] += jnp.sum(spread.reshape(-1, 8, states), axis=0)


def write_tile(before, grams, tile):
    count = grams.shape[0]
    tile[...] = before[...] + place_rows([(k, total(grams[k])) for k in range(count)])


def write_shares(whole, slot, keep, send):
    shares = 2 * keep.shape[0]
    rows = whole.shape[1] // shares
    place = lax.axis_index("term")
    for mask in range(shares):
        start = pl.multiple_of((place ^ mask) * rows, rows)
        share = whole[:, pl.ds(start, rows)]
        if mask & 1:
            send[mask // 2, :, slot] = share.astype(jnp.bfloat16)
        else:
            keep[mask // 2, :, slot] = share


def early_kernel(sectors, offsets, vectors, inner, before, *rest):
    *pieces, partial, tile, rights, grams = rest
    place_blocks(sectors, pieces, rights)
    grams[...] = jnp.zeros_like(grams)
    for pair in range(partial.shape[0]):
        partial[pair] = sum_terms(sectors, pair, offsets, inner, rights)
        add_gram(vectors, pair, partial[pair], grams)
    write_tile(before, grams, tile)


def late_kernel(sectors, offsets, vectors, inner, before, partial, last, *rest):
    keep, send, tile, whole, grams = rest
    grams[...] = jnp.zeros_like(grams)
    for pair in range(partial.shape[0]):
        lacks = [
            needed_mask(sectors, offsets, term, pair) == sectors - 1
            for term in range(last.shape[0])
        ]
        lacking = functools.reduce(jnp.logical_or, lacks)

        @pl.when(jnp.logical_not(lacking))
        def _():
            write_shares(partial.at[pair], pair, keep, send)

        @pl.when(lacking)
        def _():
            whole[...] = partial[pair]
            for term, lack in enumerate(lacks):

                @pl.when(lack)
                def _():
                    added = times_right(inner, term, pair, last[term])
                    whole[...] += added
                    add_gram(vectors, pair, added, grams)

            write_shares(whole, pair, keep, send)

    write_tile(before, grams, tile)


def second_kernel(sectors, first, offsets, vectors, inner, before, rights, last, *rest):
    keep, send, tile, whole, grams = rest
    grams[...] = jnp.zeros_like(grams)
    for slot in range(keep.shape[2]):
        pair = first + slot
        whole[slot] = sum_terms(sectors, pair, offsets, inner, rights)
        for term in range(last.shape[0]):

            @pl.when(needed_mask(sectors, offsets, term, pair) == sectors - 1)
            def _():
                whole[slot] += times_right(inner, term, pair, last[term])

    for slot in range(keep.shape[2]):
        add_gram(vectors, first + slot, whole[slot], grams)
        write_shares(whole.at[slot], slot, keep, send)
    write_tile(before, grams, tile)


def halve_last_kernel(kept, received, tile, keep, send):
    keep[0] = kept[0] + received[0].astype(jnp.float32)
    both = kept[1] + received[1].astype(jnp.float32)
    lines = send.shape[0] - 2 * TILE[0]
    send[:lines] = both.astype(jnp.bfloat16).reshape(lines, send.shape[1])
    left, parts = tile[...], []
    for _ in range(3):
        parts.append(left.astype(jnp.bfloat16).astype(jnp.float32))
        left = left - parts[-1]
    block = jnp.concatenate(
        [
            jnp.concatenate([parts[0], parts[1]], axis=0),
            jnp.concatenate([parts[2], jnp.zeros_like(left)], axis=0),
        ],
        axis=1,
    )
    send[lines:] = block.astype(jnp.bfloat16)


def halve_kernel(kept, received, keep, send):
    for k in range(kept.shape[0]):
        both = kept[k] + received[k].astype(jnp.float32)
        if k & 1:
            send[k // 2] = both.astype(jnp.bfloat16)
        else:
            keep[k // 2] = both


def ridden_tile(received):
    height, width = TILE
    block = received[received.shape[0] - 2 * height :].astype(jnp.float32)
    return block[:height, :width] + block[height:, :width] + block[:height, width:]


def add_last_kernel(kept, received, result):
    result[...] = (kept[0] + received[0].astype(jnp.float32)).astype(jnp.bfloat16)


def finish_kernel(*refs):
    *done, kept, received, tile, products, rayleigh_hbm, rows, rayleigh, sems = refs
    copies, first = [], 0
    for part in [*done, rows]:
        target = products.at[:, pl.ds(first, part.shape[1])]
        copies.append(pltpu.make_async_copy(part, target, sems.at[len(copies)]))
        first += part.shape[1]
    for copy in copies[:-1]:
        copy.start()
    lines = received.shape[0] - 2 * TILE[0]
    both = received[:lines].astype(jnp.float32).reshape(kept.shape[1:])
    rows[...] = (kept[0] + both).astype(jnp.bfloat16)
    copies[-1].start()

    tile = tile[...] + ridden_tile(received)
    trials = rayleigh.shape[0]
    row = lax.broadcasted_iota(jnp.int32, rayleigh.shape, 0)
    column = lax.broadcasted_iota(jnp.int32, rayleigh.shape, 1)

    def entry(position):
        return tile[position : position + 1, :trials]

    result = jnp.zeros(rayleigh.shape, jnp.float32)
    for i in range(trials):
        for j in range(trials):
            squares = entry(trials * trials + i) * entry(trials * trials + j)
            value = entry(i * trials + j) / jnp.sqrt(squares)
            result = jnp.where((row == i) & (column == j), value, result)
    rayleigh[...] = result
    last = pltpu.make_async_copy(rayleigh, rayleigh_hbm, sems.at[len(copies)])
    last.start()
    for copy in [*copies, last]:
        copy.wait()


def in_hbm(value):
    return pltpu.with_memory_space_constraint(value, pltpu.HBM)


def add_places(tile, axis, masks):
    parts = [tile] + [swap(tile, axis, mask) for mask in masks]
    return sum(parts[1:], parts[0])


def steps_of(count, low):
    steps = []
    while 1 << low < count:
        unit = 1 << low
        steps.append([unit, 2 * unit, 3 * unit] if 2 * unit < count else [unit])
        low += 2
    return steps


def call(kernel, name, flops, moved, limit, **kwargs):
    return pl.pallas_call(
        kernel,
        name=name,
        cost_estimate=pl.CostEstimate(flops=flops, bytes_accessed=moved, transcendentals=0),
        compiler_params=pltpu.CompilerParams(vmem_limit_bytes=limit),
        **kwargs,
    )


def local(vectors, left_ops, right_ops, offsets):
    sectors = lax.axis_size("sec")
    shares = lax.axis_size("term")
    trials, _, pairs, states, _ = vectors.shape
    terms = left_ops.shape[0]
    vectors, left, right = vectors[:, 0], left_ops[:, 0], right_ops[:, 0]
    rows = states // shares

    inner, tile, own, offsets = call(
        functools.partial(inner_kernel, 1.0 / shares),
        "inner_products",
        2 * terms * trials * pairs * states**3,
        5 * MIB,
        12 * MIB,
        out_shape=(
            jax.ShapeDtypeStruct((trials, pairs, states, terms * states), jnp.bfloat16),
            jax.ShapeDtypeStruct(TILE, jnp.float32),
            jax.ShapeDtypeStruct(right.shape, jnp.bfloat16),
            jax.ShapeDtypeStruct(offsets.shape, offsets.dtype),
        ),
        in_specs=[VMEM, VMEM, HBM, HBM],
        out_specs=(VMEM, VMEM, VMEM, VMEM),
        scratch_shapes=[pltpu.SemaphoreType.DMA((2,))],
    )(vectors, left, in_hbm(right), in_hbm(offsets))

    def behind_inner(block):
        return lax.optimization_barrier((block, inner))[0]

    gathered = gather_sectors(right, sectors, behind_inner)
    gathered[0] = own

    def share_of(count, size, dtype):
        return jax.ShapeDtypeStruct((count, trials, size, rows, states), dtype)

    tile_shape = jax.ShapeDtypeStruct(TILE, jnp.float32)
    rights_shape = jax.ShapeDtypeStruct((sectors, terms, states, states), jnp.bfloat16)
    sizes = [pairs // 2, pairs - pairs // 2]
    grams = pltpu.VMEM((trials * trials, 8, states), jnp.float32)
    *early, last = gathered
    partial, tile, rights = call(
        functools.partial(early_kernel, sectors),
        "early_products",
        2 * terms * trials * sizes[0] * states**3,
        4 * MIB,
        12 * MIB,
        out_shape=(
            jax.ShapeDtypeStruct((sizes[0], trials, states, states), jnp.float32),
            tile_shape,
            rights_shape,
        ),
        in_specs=[SMEM, VMEM, VMEM, VMEM] + [VMEM] * len(early),
        out_specs=(VMEM, VMEM, VMEM),
        scratch_shapes=[grams],
    )(offsets, vectors, inner, tile, *early)

    def sums_of(kernel, name, flops, size, scratch, *operands):
        return call(
            kernel,
            name,
            flops,
            MIB,
            12 * MIB,
            out_shape=(
                share_of(shares // 2, size, jnp.float32),
                share_of(shares // 2, size, jnp.bfloat16),
                tile_shape,
            ),
            in_specs=[SMEM] + [VMEM] * len(operands),
            out_specs=(VMEM, VMEM, VMEM),
            scratch_shapes=[pltpu.VMEM((*scratch, states, states), jnp.float32), grams],
        )(offsets, *operands)

    keep, send, tile = sums_of(
        functools.partial(late_kernel, sectors),
        "late_products",
        terms * trials * sizes[0] * states**3 // 4,
        sizes[0],
        (trials,),
        vectors,
        inner,
        tile,
        partial,
        last,
    )
    sums = [(keep, swap(send, "term", 1))]
    keep, send, tile = sums_of(
        functools.partial(second_kernel, sectors, sizes[0]),
        "second_products",
        2 * terms * trials * sizes[1] * states**3,
        sizes[1],
        (sizes[1], trials),
        vectors,
        inner,
        tile,
        rights,
        last,
    )
    sums.append((keep, swap(send, "term", 1)))

    for masks in [[1]] + steps_of(sectors, 1):
        tile = add_places(tile, "sec", masks)

    step = 1
    while 2 * step < shares:
        tile = add_places(tile, "term", [step])
        step *= 2

    parts = []
    for chunk, size in enumerate(sizes):
        keep, received = sums[chunk]
        step = 1
        while 2 * step < shares:
            step *= 2
            count = shares // (2 * step)
            last = count == 1 and chunk == len(sizes) - 1
            operands = (keep, received, tile) if last else (keep, received)
            lines = trials * size * rows + 2 * TILE[0]
            keep, send = call(
                halve_last_kernel if last else halve_kernel,
                "halve_rows",
                1,
                1,
                8 * MIB,
                out_shape=(
                    share_of(count, size, jnp.float32),
                    jax.ShapeDtypeStruct((lines, states), jnp.bfloat16)
                    if last
                    else share_of(count, size, jnp.bfloat16),
                ),
                in_specs=[VMEM] * len(operands),
                out_specs=(VMEM, VMEM),
            )(*operands)
            received = swap(send, "term", step)
        parts += [keep, received]

    done = []
    for chunk, size in enumerate(sizes[:-1]):
        done.append(
            call(
                add_last_kernel,
                "add_last_share",
                10**10,
                1,
                8 * MIB,
                out_shape=jax.ShapeDtypeStruct((trials, size, rows, states), jnp.bfloat16),
                in_specs=[VMEM, VMEM],
                out_specs=VMEM,
            )(*parts[2 * chunk : 2 * chunk + 2])
        )
    products, rayleigh = call(
        finish_kernel,
        "finish",
        1,
        1,
        8 * MIB,
        out_shape=(
            jax.ShapeDtypeStruct((trials, pairs, rows, states), jnp.bfloat16),
            jax.ShapeDtypeStruct((trials, trials), jnp.float32),
        ),
        in_specs=[VMEM] * (len(done) + 3),
        out_specs=(HBM, HBM),
        scratch_shapes=[
            pltpu.VMEM((trials, sizes[-1], rows, states), jnp.bfloat16),
            pltpu.VMEM((trials, trials), jnp.float32),
            pltpu.SemaphoreType.DMA((len(sizes) + 1,)),
        ],
    )(*done, *parts[-2:], tile)
    return (products[:, None], rayleigh)


def solution(mesh):
    in_specs = (
        P(None, "sec", None, None, None),
        P("term", "sec", None, None),
        P("term", "sec", None, None),
        P("term", None),
    )
    out_specs = (P(None, "sec", None, "term", None), P())
    return jax.shard_map(local, mesh=mesh, in_specs=in_specs, out_specs=out_specs, check_vma=False)
```

```python
import functools

import jax
import jax.numpy as jnp
from jax import lax
from jax.experimental import pallas as pl
from jax.experimental.pallas import tpu as pltpu
from jax.sharding import PartitionSpec as P

MIB = 1 << 20
TILE = (8, 128)
VMEM = pl.BlockSpec(memory_space=pltpu.VMEM)
SMEM = pl.BlockSpec(memory_space=pltpu.SMEM)
HBM = pl.BlockSpec(memory_space=pltpu.HBM)


def swap(value, axis, mask, count=None):
    masks = [mask, mask] if count is None else [turned(mask, parity, count) for parity in range(2)]
    places = range(lax.axis_size(axis))
    return lax.ppermute(value, axis, [(place, place ^ masks[place & 1]) for place in places])


def turned(mask, parity, count):
    bits = count.bit_length() - 1
    if parity:
        return mask
    return sum(1 << (bits - bit) for bit in range(1, bits) if mask >> bit & 1) | mask & 1


def gather_sectors(own, sectors, after):
    held = {0: own}
    for mask in range(2, sectors, 2):
        step = 1 << (mask.bit_length() - 1)
        sent = after(own) if mask == 4 else held[mask ^ step]
        held[mask] = swap(sent, "sec", step, sectors)
    return [block for mine in held.values() for block in (mine, swap(mine, "sec", 1))]


def place_rows(values):
    row = lax.broadcasted_iota(jnp.int32, TILE, 0)
    tile = jnp.zeros(TILE, jnp.float32)
    for position, value in values:
        tile = jnp.where(row == position, value, tile)
    return tile


def total(value):
    return jnp.sum(jnp.sum(value, axis=0, keepdims=True), axis=1, keepdims=True)


def inner_kernel(
    square_scale, vectors, left, right_hbm, offsets_hbm, inner, squares, right, offsets, sems
):
    fetches = [
        pltpu.make_async_copy(offsets_hbm, offsets, sems.at[0]),
        pltpu.make_async_copy(right_hbm, right, sems.at[1]),
    ]
    for fetch in fetches:
        fetch.start()
    terms, states = left.shape[0], left.shape[1]
    stacked = left[...].reshape(terms * states, states)
    sums = []
    for trial in range(vectors.shape[0]):
        square = jnp.zeros((8, states), jnp.float32)
        for pair in range(vectors.shape[1]):
            block = vectors[trial, pair]
            product = jnp.dot(stacked, block, preferred_element_type=jnp.float32)
            for term in range(terms):
                part = product[term * states : (term + 1) * states].astype(jnp.bfloat16)
                inner[trial, pair, :, term * states : (term + 1) * states] = part
            wide = block.astype(jnp.float32)
            square += jnp.sum((wide * wide).reshape(-1, 8, states), axis=0)
        sums.append(total(square) * square_scale)
    trials = len(sums)
    squares[...] = place_rows([(trials * trials + k, value) for k, value in enumerate(sums)])
    for fetch in fetches:
        fetch.wait()


def place_blocks(sectors, pieces, rights):
    odd = lax.axis_index("sec") & 1
    for mask in range(0, sectors, 2):
        even_place, odd_place = turned(mask, 0, sectors), turned(mask, 1, sectors)
        rights[jnp.where(odd == 1, odd_place, even_place)] = pieces[mask][...]
        if mask + 1 < len(pieces):
            rights[jnp.where(odd == 1, even_place, odd_place) ^ 1] = pieces[mask + 1][...]
    rights[sectors - 1] = jnp.zeros(rights.shape[1:], rights.dtype)


def needed_mask(sectors, offsets, term, pair):
    sector = lax.axis_index("sec")
    return sector ^ ((sector + offsets[term, pair]) & (sectors - 1))


def times_right(inner, term, pair, block):
    trials, _, states, _ = inner.shape
    lines = inner[:, pair, :, term * states : (term + 1) * states]
    product = jnp.dot(
        lines.reshape(trials * states, states), block, preferred_element_type=jnp.float32
    )
    return product.reshape(trials, states, states)


def sum_terms(sectors, pair, offsets, inner, rights):
    result = None
    for term in range(rights.shape[1]):
        mask = needed_mask(sectors, offsets, term, pair)
        added = times_right(inner, term, pair, rights[mask, term])
        result = added if result is None else result + added
    return result


def add_gram(vectors, pair, values, grams):
    trials, states = vectors.shape[0], vectors.shape[-1]
    for j in range(trials):
        for i in range(trials):
            spread = vectors[i, pair].astype(jnp.float32) * values[j]
            grams[i * trials + j] += jnp.sum(spread.reshape(-1, 8, states), axis=0)


def write_tile(before, grams, tile):
    count = grams.shape[0]
    tile[...] = before[...] + place_rows([(k, total(grams[k])) for k in range(count)])


def write_shares(whole, slot, keep, send):
    shares = 2 * keep.shape[0]
    rows = whole.shape[1] // shares
    place = lax.axis_index("term")
    for mask in range(shares):
        start = pl.multiple_of((place ^ mask) * rows, rows)
        share = whole[:, pl.ds(start, rows)]
        if mask & 1:
            send[mask // 2, :, slot] = share.astype(jnp.bfloat16)
        else:
            keep[mask // 2, :, slot] = share


def early_kernel(sectors, offsets, vectors, inner, before, *rest):
    *pieces, partial, tile, rights, grams = rest
    place_blocks(sectors, pieces, rights)
    grams[...] = jnp.zeros_like(grams)
    for pair in range(partial.shape[0]):
        partial[pair] = sum_terms(sectors, pair, offsets, inner, rights)
        add_gram(vectors, pair, partial[pair], grams)
    write_tile(before, grams, tile)


def late_kernel(sectors, offsets, vectors, inner, before, partial, last, *rest):
    keep, send, tile, whole, grams = rest
    grams[...] = jnp.zeros_like(grams)
    for pair in range(partial.shape[0]):
        lacks = [
            needed_mask(sectors, offsets, term, pair) == sectors - 1
            for term in range(last.shape[0])
        ]
        lacking = functools.reduce(jnp.logical_or, lacks)

        @pl.when(jnp.logical_not(lacking))
        def _():
            write_shares(partial.at[pair], pair, keep, send)

        @pl.when(lacking)
        def _():
            whole[...] = partial[pair]
            for term, lack in enumerate(lacks):

                @pl.when(lack)
                def _():
                    added = times_right(inner, term, pair, last[term])
                    whole[...] += added
                    add_gram(vectors, pair, added, grams)

            write_shares(whole, pair, keep, send)

    write_tile(before, grams, tile)


def second_kernel(sectors, first, offsets, vectors, inner, before, rights, last, *rest):
    keep, send, tile, whole, grams = rest
    grams[...] = jnp.zeros_like(grams)
    for slot in range(keep.shape[2]):
        pair = first + slot
        whole[slot] = sum_terms(sectors, pair, offsets, inner, rights)
        for term in range(last.shape[0]):

            @pl.when(needed_mask(sectors, offsets, term, pair) == sectors - 1)
            def _():
                whole[slot] += times_right(inner, term, pair, last[term])

    for slot in range(keep.shape[2]):
        add_gram(vectors, first + slot, whole[slot], grams)
        write_shares(whole.at[slot], slot, keep, send)
    write_tile(before, grams, tile)


def halve_last_kernel(kept, received, tile, keep, send):
    keep[0] = kept[0] + received[0].astype(jnp.float32)
    both = kept[1] + received[1].astype(jnp.float32)
    lines = send.shape[0] - 2 * TILE[0]
    send[:lines] = both.astype(jnp.bfloat16).reshape(lines, send.shape[1])
    left, parts = tile[...], []
    for _ in range(3):
        parts.append(left.astype(jnp.bfloat16).astype(jnp.float32))
        left = left - parts[-1]
    block = jnp.concatenate(
        [
            jnp.concatenate([parts[0], parts[1]], axis=0),
            jnp.concatenate([parts[2], jnp.zeros_like(left)], axis=0),
        ],
        axis=1,
    )
    send[lines:] = block.astype(jnp.bfloat16)


def halve_kernel(kept, received, keep, send):
    for k in range(kept.shape[0]):
        both = kept[k] + received[k].astype(jnp.float32)
        if k & 1:
            send[k // 2] = both.astype(jnp.bfloat16)
        else:
            keep[k // 2] = both


def ridden_tile(received):
    height, width = TILE
    block = received[received.shape[0] - 2 * height :].astype(jnp.float32)
    return block[:height, :width] + block[height:, :width] + block[:height, width:]


def add_last_kernel(kept, received, result):
    result[...] = (kept[0] + received[0].astype(jnp.float32)).astype(jnp.bfloat16)


def finish_kernel(*refs):
    *done, kept, received, tile, near, far, products, rayleigh_hbm, rows, rayleigh, sems = refs
    copies, first = [], 0
    for part in [*done, rows]:
        target = products.at[:, pl.ds(first, part.shape[1])]
        copies.append(pltpu.make_async_copy(part, target, sems.at[len(copies)]))
        first += part.shape[1]
    for copy in copies[:-1]:
        copy.start()
    lines = received.shape[0] - 2 * TILE[0]
    both = received[:lines].astype(jnp.float32).reshape(kept.shape[1:])
    rows[...] = (kept[0] + both).astype(jnp.bfloat16)
    copies[-1].start()

    tile = tile[...] + near[...] + far[...] + ridden_tile(received)
    trials = rayleigh.shape[0]
    row = lax.broadcasted_iota(jnp.int32, rayleigh.shape, 0)
    column = lax.broadcasted_iota(jnp.int32, rayleigh.shape, 1)

    def entry(position):
        return tile[position : position + 1, :trials]

    result = jnp.zeros(rayleigh.shape, jnp.float32)
    for i in range(trials):
        for j in range(trials):
            squares = entry(trials * trials + i) * entry(trials * trials + j)
            value = entry(i * trials + j) / jnp.sqrt(squares)
            result = jnp.where((row == i) & (column == j), value, result)
    rayleigh[...] = result
    last = pltpu.make_async_copy(rayleigh, rayleigh_hbm, sems.at[len(copies)])
    last.start()
    for copy in [*copies, last]:
        copy.wait()


def in_hbm(value):
    return pltpu.with_memory_space_constraint(value, pltpu.HBM)


def add_places(tile, axis, masks):
    parts = [tile] + [swap(tile, axis, mask) for mask in masks]
    return sum(parts[1:], parts[0])


def steps_of(count, low):
    steps = []
    while 1 << low < count:
        unit = 1 << low
        steps.append([unit, 2 * unit, 3 * unit] if 2 * unit < count else [unit])
        low += 2
    return steps


def call(kernel, name, flops, moved, limit, **kwargs):
    return pl.pallas_call(
        kernel,
        name=name,
        cost_estimate=pl.CostEstimate(flops=flops, bytes_accessed=moved, transcendentals=0),
        compiler_params=pltpu.CompilerParams(vmem_limit_bytes=limit),
        **kwargs,
    )


def local(vectors, left_ops, right_ops, offsets):
    sectors = lax.axis_size("sec")
    shares = lax.axis_size("term")
    trials, _, pairs, states, _ = vectors.shape
    terms = left_ops.shape[0]
    vectors, left, right = vectors[:, 0], left_ops[:, 0], right_ops[:, 0]
    rows = states // shares

    inner, tile, own, offsets = call(
        functools.partial(inner_kernel, 1.0 / shares),
        "inner_products",
        2 * terms * trials * pairs * states**3,
        5 * MIB,
        12 * MIB,
        out_shape=(
            jax.ShapeDtypeStruct((trials, pairs, states, terms * states), jnp.bfloat16),
            jax.ShapeDtypeStruct(TILE, jnp.float32),
            jax.ShapeDtypeStruct(right.shape, jnp.bfloat16),
            jax.ShapeDtypeStruct(offsets.shape, offsets.dtype),
        ),
        in_specs=[VMEM, VMEM, HBM, HBM],
        out_specs=(VMEM, VMEM, VMEM, VMEM),
        scratch_shapes=[pltpu.SemaphoreType.DMA((2,))],
    )(vectors, left, in_hbm(right), in_hbm(offsets))

    def behind_inner(block):
        return lax.optimization_barrier((block, inner))[0]

    gathered = gather_sectors(right, sectors, behind_inner)
    gathered[0] = own

    def share_of(count, size, dtype):
        return jax.ShapeDtypeStruct((count, trials, size, rows, states), dtype)

    tile_shape = jax.ShapeDtypeStruct(TILE, jnp.float32)
    rights_shape = jax.ShapeDtypeStruct((sectors, terms, states, states), jnp.bfloat16)
    sizes = [pairs // 2, pairs - pairs // 2]
    grams = pltpu.VMEM((trials * trials, 8, states), jnp.float32)
    *early, last = gathered
    partial, tile, rights = call(
        functools.partial(early_kernel, sectors),
        "early_products",
        2 * terms * trials * sizes[0] * states**3,
        4 * MIB,
        12 * MIB,
        out_shape=(
            jax.ShapeDtypeStruct((sizes[0], trials, states, states), jnp.float32),
            tile_shape,
            rights_shape,
        ),
        in_specs=[SMEM, VMEM, VMEM, VMEM] + [VMEM] * len(early),
        out_specs=(VMEM, VMEM, VMEM),
        scratch_shapes=[grams],
    )(offsets, vectors, inner, tile, *early)

    def sums_of(kernel, name, flops, size, scratch, *operands):
        return call(
            kernel,
            name,
            flops,
            MIB,
            12 * MIB,
            out_shape=(
                share_of(shares // 2, size, jnp.float32),
                share_of(shares // 2, size, jnp.bfloat16),
                tile_shape,
            ),
            in_specs=[SMEM] + [VMEM] * len(operands),
            out_specs=(VMEM, VMEM, VMEM),
            scratch_shapes=[pltpu.VMEM((*scratch, states, states), jnp.float32), grams],
        )(offsets, *operands)

    keep, send, tile = sums_of(
        functools.partial(late_kernel, sectors),
        "late_products",
        terms * trials * sizes[0] * states**3 // 4,
        sizes[0],
        (trials,),
        vectors,
        inner,
        tile,
        partial,
        last,
    )
    sums = [(keep, swap(send, "term", 1))]
    keep, send, tile = sums_of(
        functools.partial(second_kernel, sectors, sizes[0]),
        "second_products",
        2 * terms * trials * sizes[1] * states**3,
        sizes[1],
        (sizes[1], trials),
        vectors,
        inner,
        tile,
        rights,
        last,
    )
    sums.append((keep, swap(send, "term", 1)))

    for masks in [[1]] + steps_of(sectors, 1):
        tile = add_places(tile, "sec", masks)

    step = 2
    while 2 * step < shares:
        tile = add_places(tile, "term", [step])
        step *= 2
    nearby = [swap(tile, "term", 1), swap(tile, "term", 1 | step)]

    parts = []
    for chunk, size in enumerate(sizes):
        keep, received = sums[chunk]
        step = 1
        while 2 * step < shares:
            step *= 2
            count = shares // (2 * step)
            last = count == 1 and chunk == len(sizes) - 1
            operands = (keep, received, tile) if last else (keep, received)
            lines = trials * size * rows + 2 * TILE[0]
            keep, send = call(
                halve_last_kernel if last else halve_kernel,
                "halve_rows",
                1,
                1,
                8 * MIB,
                out_shape=(
                    share_of(count, size, jnp.float32),
                    jax.ShapeDtypeStruct((lines, states), jnp.bfloat16)
                    if last
                    else share_of(count, size, jnp.bfloat16),
                ),
                in_specs=[VMEM] * len(operands),
                out_specs=(VMEM, VMEM),
            )(*operands)
            received = swap(send, "term", step)
        parts += [keep, received]

    done = []
    for chunk, size in enumerate(sizes[:-1]):
        done.append(
            call(
                add_last_kernel,
                "add_last_share",
                10**8,
                1,
                8 * MIB,
                out_shape=jax.ShapeDtypeStruct((trials, size, rows, states), jnp.bfloat16),
                in_specs=[VMEM, VMEM],
                out_specs=VMEM,
            )(*parts[2 * chunk : 2 * chunk + 2])
        )
    products, rayleigh = call(
        finish_kernel,
        "finish",
        1,
        1,
        8 * MIB,
        out_shape=(
            jax.ShapeDtypeStruct((trials, pairs, rows, states), jnp.bfloat16),
            jax.ShapeDtypeStruct((trials, trials), jnp.float32),
        ),
        in_specs=[VMEM] * (len(done) + 5),
        out_specs=(HBM, HBM),
        scratch_shapes=[
            pltpu.VMEM((trials, sizes[-1], rows, states), jnp.bfloat16),
            pltpu.VMEM((trials, trials), jnp.float32),
            pltpu.SemaphoreType.DMA((len(sizes) + 1,)),
        ],
    )(*done, *parts[-2:], tile, *nearby)
    return (products[:, None], rayleigh)


def solution(mesh):
    in_specs = (
        P(None, "sec", None, None, None),
        P("term", "sec", None, None),
        P("term", "sec", None, None),
        P("term", None),
    )
    out_specs = (P(None, "sec", None, "term", None), P())
    return jax.shard_map(local, mesh=mesh, in_specs=in_specs, out_specs=out_specs, check_vma=False)
```

```python
import functools

import jax
import jax.numpy as jnp
from jax import lax
from jax.experimental import pallas as pl
from jax.experimental.pallas import tpu as pltpu
from jax.sharding import PartitionSpec as P

MIB = 1 << 20
TILE = (8, 128)
VMEM = pl.BlockSpec(memory_space=pltpu.VMEM)
SMEM = pl.BlockSpec(memory_space=pltpu.SMEM)
HBM = pl.BlockSpec(memory_space=pltpu.HBM)


def swap(value, axis, mask, count=None):
    masks = [mask, mask] if count is None else [turned(mask, parity, count) for parity in range(2)]
    places = range(lax.axis_size(axis))
    return lax.ppermute(value, axis, [(place, place ^ masks[place & 1]) for place in places])


def turned(mask, parity, count):
    bits = count.bit_length() - 1
    if parity:
        return mask
    return sum(1 << (bits - bit) for bit in range(1, bits) if mask >> bit & 1) | mask & 1


def gather_sectors(own, sectors, after):
    held = {0: own}
    for mask in range(2, sectors, 2):
        step = 1 << (mask.bit_length() - 1)
        sent = after(own) if mask == 4 else held[mask ^ step]
        held[mask] = swap(sent, "sec", step, sectors)
    return [block for mine in held.values() for block in (mine, swap(mine, "sec", 1))]


def place_rows(values):
    row = lax.broadcasted_iota(jnp.int32, TILE, 0)
    tile = jnp.zeros(TILE, jnp.float32)
    for position, value in values:
        tile = jnp.where(row == position, value, tile)
    return tile


def total(value):
    return jnp.sum(jnp.sum(value, axis=0, keepdims=True), axis=1, keepdims=True)


def inner_kernel(
    square_scale, vectors, left, right_hbm, offsets_hbm, inner, squares, right, offsets, sems
):
    fetches = [
        pltpu.make_async_copy(offsets_hbm, offsets, sems.at[0]),
        pltpu.make_async_copy(right_hbm, right, sems.at[1]),
    ]
    for fetch in fetches:
        fetch.start()
    terms, states = left.shape[0], left.shape[1]
    stacked = left[...].reshape(terms * states, states)
    sums = []
    for trial in range(vectors.shape[0]):
        square = jnp.zeros((8, states), jnp.float32)
        for pair in range(vectors.shape[1]):
            block = vectors[trial, pair]
            product = jnp.dot(stacked, block, preferred_element_type=jnp.float32)
            for term in range(terms):
                part = product[term * states : (term + 1) * states].astype(jnp.bfloat16)
                inner[trial, pair, :, term * states : (term + 1) * states] = part
            wide = block.astype(jnp.float32)
            square += jnp.sum((wide * wide).reshape(-1, 8, states), axis=0)
        sums.append(total(square) * square_scale)
    trials = len(sums)
    squares[...] = place_rows([(trials * trials + k, value) for k, value in enumerate(sums)])
    for fetch in fetches:
        fetch.wait()


def place_blocks(sectors, pieces, rights):
    odd = lax.axis_index("sec") & 1
    for mask in range(0, sectors, 2):
        even_place, odd_place = turned(mask, 0, sectors), turned(mask, 1, sectors)
        rights[jnp.where(odd == 1, odd_place, even_place)] = pieces[mask][...]
        if mask + 1 < len(pieces):
            rights[jnp.where(odd == 1, even_place, odd_place) ^ 1] = pieces[mask + 1][...]
    rights[sectors - 1] = jnp.zeros(rights.shape[1:], rights.dtype)


def needed_mask(sectors, offsets, term, pair):
    sector = lax.axis_index("sec")
    return sector ^ ((sector + offsets[term, pair]) & (sectors - 1))


def times_right(inner, term, pair, block):
    trials, _, states, _ = inner.shape
    lines = inner[:, pair, :, term * states : (term + 1) * states]
    product = jnp.dot(
        lines.reshape(trials * states, states), block, preferred_element_type=jnp.float32
    )
    return product.reshape(trials, states, states)


def sum_terms(sectors, pair, offsets, inner, rights):
    result = None
    for term in range(rights.shape[1]):
        mask = needed_mask(sectors, offsets, term, pair)
        added = times_right(inner, term, pair, rights[mask, term])
        result = added if result is None else result + added
    return result


def add_gram(vectors, pair, values, grams):
    trials, states = vectors.shape[0], vectors.shape[-1]
    for j in range(trials):
        for i in range(trials):
            spread = vectors[i, pair].astype(jnp.float32) * values[j]
            grams[i * trials + j] += jnp.sum(spread.reshape(-1, 8, states), axis=0)


def write_tile(before, grams, tile):
    count = grams.shape[0]
    tile[...] = before[...] + place_rows([(k, total(grams[k])) for k in range(count)])


def write_shares(whole, slot, keep, send):
    shares = 2 * keep.shape[0]
    rows = whole.shape[1] // shares
    place = lax.axis_index("term")
    for mask in range(shares):
        start = pl.multiple_of((place ^ mask) * rows, rows)
        share = whole[:, pl.ds(start, rows)]
        if mask & 1:
            send[mask // 2, :, slot] = share.astype(jnp.bfloat16)
        else:
            keep[mask // 2, :, slot] = share


def early_kernel(sectors, offsets, vectors, inner, before, *rest):
    *pieces, partial, tile, rights, grams = rest
    place_blocks(sectors, pieces, rights)
    grams[...] = jnp.zeros_like(grams)
    for pair in range(partial.shape[0]):
        partial[pair] = sum_terms(sectors, pair, offsets, inner, rights)
        add_gram(vectors, pair, partial[pair], grams)
    write_tile(before, grams, tile)


def late_kernel(sectors, offsets, vectors, inner, before, partial, last, *rest):
    keep, send, tile, whole, grams = rest
    grams[...] = jnp.zeros_like(grams)
    for pair in range(partial.shape[0]):
        lacks = [
            needed_mask(sectors, offsets, term, pair) == sectors - 1
            for term in range(last.shape[0])
        ]
        lacking = functools.reduce(jnp.logical_or, lacks)

        @pl.when(jnp.logical_not(lacking))
        def _():
            write_shares(partial.at[pair], pair, keep, send)

        @pl.when(lacking)
        def _():
            whole[...] = partial[pair]
            for term, lack in enumerate(lacks):

                @pl.when(lack)
                def _():
                    added = times_right(inner, term, pair, last[term])
                    whole[...] += added
                    add_gram(vectors, pair, added, grams)

            write_shares(whole, pair, keep, send)

    write_tile(before, grams, tile)


def other_kernel(sectors, first, offsets, vectors, inner, before, rights, last, *rest):
    keep, send, tile, whole, grams = rest
    grams[...] = jnp.zeros_like(grams)
    for slot in range(keep.shape[2]):
        pair = first + slot
        whole[slot] = sum_terms(sectors, pair, offsets, inner, rights)
        for term in range(last.shape[0]):

            @pl.when(needed_mask(sectors, offsets, term, pair) == sectors - 1)
            def _():
                whole[slot] += times_right(inner, term, pair, last[term])

    for slot in range(keep.shape[2]):
        add_gram(vectors, first + slot, whole[slot], grams)
        write_shares(whole.at[slot], slot, keep, send)
    write_tile(before, grams, tile)


def halve_last_kernel(kept, received, tile, keep, send):
    keep[0] = kept[0] + received[0].astype(jnp.float32)
    both = kept[1] + received[1].astype(jnp.float32)
    lines = send.shape[0] - 2 * TILE[0]
    send[:lines] = both.astype(jnp.bfloat16).reshape(lines, send.shape[1])
    left, parts = tile[...], []
    for _ in range(3):
        parts.append(left.astype(jnp.bfloat16).astype(jnp.float32))
        left = left - parts[-1]
    block = jnp.concatenate(
        [
            jnp.concatenate([parts[0], parts[1]], axis=0),
            jnp.concatenate([parts[2], jnp.zeros_like(left)], axis=0),
        ],
        axis=1,
    )
    send[lines:] = block.astype(jnp.bfloat16)


def halve_kernel(kept, received, keep, send):
    for k in range(kept.shape[0]):
        both = kept[k] + received[k].astype(jnp.float32)
        if k & 1:
            send[k // 2] = both.astype(jnp.bfloat16)
        else:
            keep[k // 2] = both


def ridden_tile(received):
    height, width = TILE
    block = received[received.shape[0] - 2 * height :].astype(jnp.float32)
    return block[:height, :width] + block[height:, :width] + block[:height, width:]


def add_last_kernel(kept, received, result):
    result[...] = (kept[0] + received[0].astype(jnp.float32)).astype(jnp.bfloat16)


def finish_kernel(*refs):
    *done, kept, received, tile, near, far, products, rayleigh_hbm, rows, rayleigh, sems = refs
    copies, first = [], 0
    for part in [*done, rows]:
        target = products.at[:, pl.ds(first, part.shape[1])]
        copies.append(pltpu.make_async_copy(part, target, sems.at[len(copies)]))
        first += part.shape[1]
    for copy in copies[:-1]:
        copy.start()
    lines = received.shape[0] - 2 * TILE[0]
    both = received[:lines].astype(jnp.float32).reshape(kept.shape[1:])
    rows[...] = (kept[0] + both).astype(jnp.bfloat16)
    copies[-1].start()

    tile = tile[...] + near[...] + far[...] + ridden_tile(received)
    trials = rayleigh.shape[0]
    row = lax.broadcasted_iota(jnp.int32, rayleigh.shape, 0)
    column = lax.broadcasted_iota(jnp.int32, rayleigh.shape, 1)

    def entry(position):
        return tile[position : position + 1, :trials]

    result = jnp.zeros(rayleigh.shape, jnp.float32)
    for i in range(trials):
        for j in range(trials):
            squares = entry(trials * trials + i) * entry(trials * trials + j)
            value = entry(i * trials + j) / jnp.sqrt(squares)
            result = jnp.where((row == i) & (column == j), value, result)
    rayleigh[...] = result
    last = pltpu.make_async_copy(rayleigh, rayleigh_hbm, sems.at[len(copies)])
    last.start()
    for copy in [*copies, last]:
        copy.wait()


def in_hbm(value):
    return pltpu.with_memory_space_constraint(value, pltpu.HBM)


def add_places(tile, axis, masks):
    parts = [tile] + [swap(tile, axis, mask) for mask in masks]
    return sum(parts[1:], parts[0])


def steps_of(count, low):
    steps = []
    while 1 << low < count:
        unit = 1 << low
        steps.append([unit, 2 * unit, 3 * unit] if 2 * unit < count else [unit])
        low += 2
    return steps


def call(kernel, name, flops, moved, limit, **kwargs):
    return pl.pallas_call(
        kernel,
        name=name,
        cost_estimate=pl.CostEstimate(flops=flops, bytes_accessed=moved, transcendentals=0),
        compiler_params=pltpu.CompilerParams(vmem_limit_bytes=limit),
        **kwargs,
    )


def local(vectors, left_ops, right_ops, offsets):
    sectors = lax.axis_size("sec")
    shares = lax.axis_size("term")
    trials, _, pairs, states, _ = vectors.shape
    terms = left_ops.shape[0]
    vectors, left, right = vectors[:, 0], left_ops[:, 0], right_ops[:, 0]
    rows = states // shares

    inner, tile, own, offsets = call(
        functools.partial(inner_kernel, 1.0 / shares),
        "inner_products",
        2 * terms * trials * pairs * states**3,
        5 * MIB,
        12 * MIB,
        out_shape=(
            jax.ShapeDtypeStruct((trials, pairs, states, terms * states), jnp.bfloat16),
            jax.ShapeDtypeStruct(TILE, jnp.float32),
            jax.ShapeDtypeStruct(right.shape, jnp.bfloat16),
            jax.ShapeDtypeStruct(offsets.shape, offsets.dtype),
        ),
        in_specs=[VMEM, VMEM, HBM, HBM],
        out_specs=(VMEM, VMEM, VMEM, VMEM),
        scratch_shapes=[pltpu.SemaphoreType.DMA((2,))],
    )(vectors, left, in_hbm(right), in_hbm(offsets))

    def behind_inner(block):
        return lax.optimization_barrier((block, inner))[0]

    gathered = gather_sectors(right, sectors, behind_inner)
    gathered[0] = own

    def share_of(count, size, dtype):
        return jax.ShapeDtypeStruct((count, trials, size, rows, states), dtype)

    tile_shape = jax.ShapeDtypeStruct(TILE, jnp.float32)
    rights_shape = jax.ShapeDtypeStruct((sectors, terms, states, states), jnp.bfloat16)
    sizes = [pairs - 2 * (pairs // 4), pairs // 4, pairs // 4]
    grams = pltpu.VMEM((trials * trials, 8, states), jnp.float32)
    *early, last = gathered
    partial, tile, rights = call(
        functools.partial(early_kernel, sectors),
        "early_products",
        2 * terms * trials * sizes[0] * states**3,
        4 * MIB,
        12 * MIB,
        out_shape=(
            jax.ShapeDtypeStruct((sizes[0], trials, states, states), jnp.float32),
            tile_shape,
            rights_shape,
        ),
        in_specs=[SMEM, VMEM, VMEM, VMEM] + [VMEM] * len(early),
        out_specs=(VMEM, VMEM, VMEM),
        scratch_shapes=[grams],
    )(offsets, vectors, inner, tile, *early)

    def sums_of(kernel, name, flops, size, scratch, *operands):
        return call(
            kernel,
            name,
            flops,
            MIB,
            12 * MIB,
            out_shape=(
                share_of(shares // 2, size, jnp.float32),
                share_of(shares // 2, size, jnp.bfloat16),
                tile_shape,
            ),
            in_specs=[SMEM] + [VMEM] * len(operands),
            out_specs=(VMEM, VMEM, VMEM),
            scratch_shapes=[pltpu.VMEM((*scratch, states, states), jnp.float32), grams],
        )(offsets, *operands)

    keep, send, tile = sums_of(
        functools.partial(late_kernel, sectors),
        "late_products",
        terms * trials * sizes[0] * states**3 // 4,
        sizes[0],
        (trials,),
        vectors,
        inner,
        tile,
        partial,
        last,
    )
    sums = [(keep, swap(send, "term", 1))]
    first = sizes[0]
    for size in sizes[1:]:
        keep, send, tile = sums_of(
            functools.partial(other_kernel, sectors, first),
            "other_products",
            2 * terms * trials * size * states**3,
            size,
            (size, trials),
            vectors,
            inner,
            tile,
            rights,
            last,
        )
        sums.append((keep, swap(send, "term", 1)))
        first += size

    for masks in [[1]] + steps_of(sectors, 1):
        tile = add_places(tile, "sec", masks)

    step = 2
    while 2 * step < shares:
        tile = add_places(tile, "term", [step])
        step *= 2
    nearby = [swap(tile, "term", 1), swap(tile, "term", 1 | step)]

    parts = []
    for chunk, size in enumerate(sizes):
        keep, received = sums[chunk]
        if chunk:
            received, send = lax.optimization_barrier((received, send))
        step = 1
        while 2 * step < shares:
            step *= 2
            count = shares // (2 * step)
            last = count == 1 and chunk == len(sizes) - 1
            operands = (keep, received, tile) if last else (keep, received)
            lines = trials * size * rows + 2 * TILE[0]
            keep, send = call(
                halve_last_kernel if last else halve_kernel,
                "halve_rows",
                1,
                1,
                8 * MIB,
                out_shape=(
                    share_of(count, size, jnp.float32),
                    jax.ShapeDtypeStruct((lines, states), jnp.bfloat16)
                    if last
                    else share_of(count, size, jnp.bfloat16),
                ),
                in_specs=[VMEM] * len(operands),
                out_specs=(VMEM, VMEM),
            )(*operands)
            received = swap(send, "term", step)
        parts += [keep, received]

    done = []
    for chunk, size in enumerate(sizes[:-1]):
        done.append(
            call(
                add_last_kernel,
                "add_last_share",
                10**8,
                1,
                8 * MIB,
                out_shape=jax.ShapeDtypeStruct((trials, size, rows, states), jnp.bfloat16),
                in_specs=[VMEM, VMEM],
                out_specs=VMEM,
            )(*parts[2 * chunk : 2 * chunk + 2])
        )
    products, rayleigh = call(
        finish_kernel,
        "finish",
        1,
        1,
        8 * MIB,
        out_shape=(
            jax.ShapeDtypeStruct((trials, pairs, rows, states), jnp.bfloat16),
            jax.ShapeDtypeStruct((trials, trials), jnp.float32),
        ),
        in_specs=[VMEM] * (len(done) + 5),
        out_specs=(HBM, HBM),
        scratch_shapes=[
            pltpu.VMEM((trials, sizes[-1], rows, states), jnp.bfloat16),
            pltpu.VMEM((trials, trials), jnp.float32),
            pltpu.SemaphoreType.DMA((len(sizes) + 1,)),
        ],
    )(*done, *parts[-2:], tile, *nearby)
    return (products[:, None], rayleigh)


def solution(mesh):
    in_specs = (
        P(None, "sec", None, None, None),
        P("term", "sec", None, None),
        P("term", "sec", None, None),
        P("term", None),
    )
    out_specs = (P(None, "sec", None, "term", None), P())
    return jax.shard_map(local, mesh=mesh, in_specs=in_specs, out_specs=out_specs, check_vma=False)
```

```python
import functools

import jax
import jax.numpy as jnp
from jax import lax
from jax.experimental import pallas as pl
from jax.experimental.pallas import tpu as pltpu
from jax.sharding import PartitionSpec as P

MIB = 1 << 20
TILE = (8, 128)
VMEM = pl.BlockSpec(memory_space=pltpu.VMEM)
SMEM = pl.BlockSpec(memory_space=pltpu.SMEM)
HBM = pl.BlockSpec(memory_space=pltpu.HBM)


def swap(value, axis, mask, count=None):
    masks = [mask, mask] if count is None else [turned(mask, parity, count) for parity in range(2)]
    places = range(lax.axis_size(axis))
    return lax.ppermute(value, axis, [(place, place ^ masks[place & 1]) for place in places])


def turned(mask, parity, count):
    bits = count.bit_length() - 1
    if parity:
        return mask
    return sum(1 << (bits - bit) for bit in range(1, bits) if mask >> bit & 1) | mask & 1


def gather_sectors(own, sectors, after):
    held = {0: own}
    for mask in range(2, sectors, 2):
        step = 1 << (mask.bit_length() - 1)
        sent = after(own) if mask == 4 else held[mask ^ step]
        held[mask] = swap(sent, "sec", step, sectors)
    return [block for mine in held.values() for block in (mine, swap(mine, "sec", 1))]


def place_rows(values):
    row = lax.broadcasted_iota(jnp.int32, TILE, 0)
    tile = jnp.zeros(TILE, jnp.float32)
    for position, value in values:
        tile = jnp.where(row == position, value, tile)
    return tile


def total(value):
    return jnp.sum(jnp.sum(value, axis=0, keepdims=True), axis=1, keepdims=True)


def inner_kernel(
    square_scale, vectors, left, right_hbm, offsets_hbm, inner, squares, right, offsets, sems
):
    fetches = [
        pltpu.make_async_copy(offsets_hbm, offsets, sems.at[0]),
        pltpu.make_async_copy(right_hbm, right, sems.at[1]),
    ]
    for fetch in fetches:
        fetch.start()
    terms, states = left.shape[0], left.shape[1]
    stacked = left[...].reshape(terms * states, states)
    sums = []
    for trial in range(vectors.shape[0]):
        square = jnp.zeros((8, states), jnp.float32)
        for pair in range(vectors.shape[1]):
            block = vectors[trial, pair]
            product = jnp.dot(stacked, block, preferred_element_type=jnp.float32)
            for term in range(terms):
                part = product[term * states : (term + 1) * states].astype(jnp.bfloat16)
                inner[trial, pair, :, term * states : (term + 1) * states] = part
            wide = block.astype(jnp.float32)
            square += jnp.sum((wide * wide).reshape(-1, 8, states), axis=0)
        sums.append(total(square) * square_scale)
    trials = len(sums)
    squares[...] = place_rows([(trials * trials + k, value) for k, value in enumerate(sums)])
    for fetch in fetches:
        fetch.wait()


def place_blocks(sectors, pieces, rights):
    odd = lax.axis_index("sec") & 1
    for mask in range(0, sectors, 2):
        even_place, odd_place = turned(mask, 0, sectors), turned(mask, 1, sectors)
        rights[jnp.where(odd == 1, odd_place, even_place)] = pieces[mask][...]
        if mask + 1 < len(pieces):
            rights[jnp.where(odd == 1, even_place, odd_place) ^ 1] = pieces[mask + 1][...]
    rights[sectors - 1] = jnp.zeros(rights.shape[1:], rights.dtype)


def needed_mask(sectors, offsets, term, pair):
    sector = lax.axis_index("sec")
    return sector ^ ((sector + offsets[term, pair]) & (sectors - 1))


def times_right(inner, term, pair, block):
    trials, _, states, _ = inner.shape
    lines = inner[:, pair, :, term * states : (term + 1) * states]
    product = jnp.dot(
        lines.reshape(trials * states, states), block, preferred_element_type=jnp.float32
    )
    return product.reshape(trials, states, states)


def sum_terms(sectors, pair, offsets, inner, rights):
    result = None
    for term in range(rights.shape[1]):
        mask = needed_mask(sectors, offsets, term, pair)
        added = times_right(inner, term, pair, rights[mask, term])
        result = added if result is None else result + added
    return result


def add_gram(vectors, pair, values, grams):
    trials, states = vectors.shape[0], vectors.shape[-1]
    for j in range(trials):
        for i in range(trials):
            spread = vectors[i, pair].astype(jnp.float32) * values[j]
            grams[i * trials + j] += jnp.sum(spread.reshape(-1, 8, states), axis=0)


def write_tile(before, grams, tile):
    count = grams.shape[0]
    tile[...] = before[...] + place_rows([(k, total(grams[k])) for k in range(count)])


def write_shares(whole, slot, keep, send):
    shares = 2 * keep.shape[0]
    rows = whole.shape[1] // shares
    place = lax.axis_index("term")
    for mask in range(shares):
        start = pl.multiple_of((place ^ mask) * rows, rows)
        share = whole[:, pl.ds(start, rows)]
        if mask & 1:
            send[mask // 2, :, slot] = share.astype(jnp.bfloat16)
        else:
            keep[mask // 2, :, slot] = share


def early_kernel(sectors, offsets, vectors, inner, before, *rest):
    *pieces, partial, tile, rights, grams = rest
    place_blocks(sectors, pieces, rights)
    grams[...] = jnp.zeros_like(grams)
    for pair in range(partial.shape[0]):
        partial[pair] = sum_terms(sectors, pair, offsets, inner, rights)
        add_gram(vectors, pair, partial[pair], grams)
    write_tile(before, grams, tile)


def late_kernel(sectors, offsets, vectors, inner, before, partial, last, *rest):
    keep, send, tile, whole, grams = rest
    grams[...] = jnp.zeros_like(grams)
    for pair in range(partial.shape[0]):
        lacks = [
            needed_mask(sectors, offsets, term, pair) == sectors - 1
            for term in range(last.shape[0])
        ]
        lacking = functools.reduce(jnp.logical_or, lacks)

        @pl.when(jnp.logical_not(lacking))
        def _():
            write_shares(partial.at[pair], pair, keep, send)

        @pl.when(lacking)
        def _():
            whole[...] = partial[pair]
            for term, lack in enumerate(lacks):

                @pl.when(lack)
                def _():
                    added = times_right(inner, term, pair, last[term])
                    whole[...] += added
                    add_gram(vectors, pair, added, grams)

            write_shares(whole, pair, keep, send)

    write_tile(before, grams, tile)


def other_kernel(sectors, first, offsets, vectors, inner, before, rights, last, *rest):
    keep, send, tile, whole, grams = rest
    grams[...] = jnp.zeros_like(grams)
    for slot in range(keep.shape[2]):
        pair = first + slot
        whole[slot] = sum_terms(sectors, pair, offsets, inner, rights)
        for term in range(last.shape[0]):

            @pl.when(needed_mask(sectors, offsets, term, pair) == sectors - 1)
            def _():
                whole[slot] += times_right(inner, term, pair, last[term])

    for slot in range(keep.shape[2]):
        add_gram(vectors, first + slot, whole[slot], grams)
        write_shares(whole.at[slot], slot, keep, send)
    write_tile(before, grams, tile)


def halve_last_kernel(kept, received, tile, keep, send):
    keep[0] = kept[0] + received[0].astype(jnp.float32)
    both = kept[1] + received[1].astype(jnp.float32)
    lines = send.shape[0] - 2 * TILE[0]
    send[:lines] = both.astype(jnp.bfloat16).reshape(lines, send.shape[1])
    left, parts = tile[...], []
    for _ in range(3):
        parts.append(left.astype(jnp.bfloat16).astype(jnp.float32))
        left = left - parts[-1]
    block = jnp.concatenate(
        [
            jnp.concatenate([parts[0], parts[1]], axis=0),
            jnp.concatenate([parts[2], jnp.zeros_like(left)], axis=0),
        ],
        axis=1,
    )
    send[lines:] = block.astype(jnp.bfloat16)


def halve_kernel(kept, received, keep, send):
    for k in range(kept.shape[0]):
        both = kept[k] + received[k].astype(jnp.float32)
        if k & 1:
            send[k // 2] = both.astype(jnp.bfloat16)
        else:
            keep[k // 2] = both


def ridden_tile(received):
    height, width = TILE
    block = received[received.shape[0] - 2 * height :].astype(jnp.float32)
    return block[:height, :width] + block[height:, :width] + block[:height, width:]


def add_last_kernel(kept, received, result):
    result[...] = (kept[0] + received[0].astype(jnp.float32)).astype(jnp.bfloat16)


def finish_kernel(*refs):
    *done, kept, received, tile, near, far, products, rayleigh_hbm, rows, rayleigh, sems = refs
    copies, first = [], 0
    for part in [*done, rows]:
        target = products.at[:, pl.ds(first, part.shape[1])]
        copies.append(pltpu.make_async_copy(part, target, sems.at[len(copies)]))
        first += part.shape[1]
    for copy in copies[:-1]:
        copy.start()
    lines = received.shape[0] - 2 * TILE[0]
    both = received[:lines].astype(jnp.float32).reshape(kept.shape[1:])
    rows[...] = (kept[0] + both).astype(jnp.bfloat16)
    copies[-1].start()

    tile = tile[...] + near[...] + far[...] + ridden_tile(received)
    trials = rayleigh.shape[0]
    row = lax.broadcasted_iota(jnp.int32, rayleigh.shape, 0)
    column = lax.broadcasted_iota(jnp.int32, rayleigh.shape, 1)

    def entry(position):
        return tile[position : position + 1, :trials]

    result = jnp.zeros(rayleigh.shape, jnp.float32)
    for i in range(trials):
        for j in range(trials):
            squares = entry(trials * trials + i) * entry(trials * trials + j)
            value = entry(i * trials + j) / jnp.sqrt(squares)
            result = jnp.where((row == i) & (column == j), value, result)
    rayleigh[...] = result
    last = pltpu.make_async_copy(rayleigh, rayleigh_hbm, sems.at[len(copies)])
    last.start()
    for copy in [*copies, last]:
        copy.wait()


def in_hbm(value):
    return pltpu.with_memory_space_constraint(value, pltpu.HBM)


def add_places(tile, axis, masks):
    parts = [tile] + [swap(tile, axis, mask) for mask in masks]
    return sum(parts[1:], parts[0])


def call(kernel, name, flops, moved, limit, **kwargs):
    return pl.pallas_call(
        kernel,
        name=name,
        cost_estimate=pl.CostEstimate(flops=flops, bytes_accessed=moved, transcendentals=0),
        compiler_params=pltpu.CompilerParams(vmem_limit_bytes=limit),
        **kwargs,
    )


def local(vectors, left_ops, right_ops, offsets):
    sectors = lax.axis_size("sec")
    shares = lax.axis_size("term")
    trials, _, pairs, states, _ = vectors.shape
    terms = left_ops.shape[0]
    vectors, left, right = vectors[:, 0], left_ops[:, 0], right_ops[:, 0]
    rows = states // shares

    inner, tile, own, offsets = call(
        functools.partial(inner_kernel, 1.0 / shares),
        "inner_products",
        2 * terms * trials * pairs * states**3,
        5 * MIB,
        12 * MIB,
        out_shape=(
            jax.ShapeDtypeStruct((trials, pairs, states, terms * states), jnp.bfloat16),
            jax.ShapeDtypeStruct(TILE, jnp.float32),
            jax.ShapeDtypeStruct(right.shape, jnp.bfloat16),
            jax.ShapeDtypeStruct(offsets.shape, offsets.dtype),
        ),
        in_specs=[VMEM, VMEM, HBM, HBM],
        out_specs=(VMEM, VMEM, VMEM, VMEM),
        scratch_shapes=[pltpu.SemaphoreType.DMA((2,))],
    )(vectors, left, in_hbm(right), in_hbm(offsets))

    def behind_inner(block):
        return lax.optimization_barrier((block, inner))[0]

    gathered = gather_sectors(right, sectors, behind_inner)
    gathered[0] = own

    def share_of(count, size, dtype):
        return jax.ShapeDtypeStruct((count, trials, size, rows, states), dtype)

    tile_shape = jax.ShapeDtypeStruct(TILE, jnp.float32)
    rights_shape = jax.ShapeDtypeStruct((sectors, terms, states, states), jnp.bfloat16)
    sizes = [pairs - 2 * (pairs // 4), pairs // 4, pairs // 4]
    grams = pltpu.VMEM((trials * trials, 8, states), jnp.float32)
    *early, last = gathered
    partial, tile, rights = call(
        functools.partial(early_kernel, sectors),
        "early_products",
        2 * terms * trials * sizes[0] * states**3,
        4 * MIB,
        12 * MIB,
        out_shape=(
            jax.ShapeDtypeStruct((sizes[0], trials, states, states), jnp.float32),
            tile_shape,
            rights_shape,
        ),
        in_specs=[SMEM, VMEM, VMEM, VMEM] + [VMEM] * len(early),
        out_specs=(VMEM, VMEM, VMEM),
        scratch_shapes=[grams],
    )(offsets, vectors, inner, tile, *early)

    def sums_of(kernel, name, flops, size, scratch, *operands):
        return call(
            kernel,
            name,
            flops,
            MIB,
            12 * MIB,
            out_shape=(
                share_of(shares // 2, size, jnp.float32),
                share_of(shares // 2, size, jnp.bfloat16),
                tile_shape,
            ),
            in_specs=[SMEM] + [VMEM] * len(operands),
            out_specs=(VMEM, VMEM, VMEM),
            scratch_shapes=[pltpu.VMEM((*scratch, states, states), jnp.float32), grams],
        )(offsets, *operands)

    keep, send, tile = sums_of(
        functools.partial(late_kernel, sectors),
        "late_products",
        terms * trials * sizes[0] * states**3 // 4,
        sizes[0],
        (trials,),
        vectors,
        inner,
        tile,
        partial,
        last,
    )
    sums = [(keep, swap(send, "term", 1))]
    first = sizes[0]
    for size in sizes[1:]:
        keep, send, tile = sums_of(
            functools.partial(other_kernel, sectors, first),
            "other_products",
            2 * terms * trials * size * states**3,
            size,
            (size, trials),
            vectors,
            inner,
            tile,
            rights,
            last,
        )
        sums.append((keep, swap(send, "term", 1)))
        first += size

    step = 1
    while step < sectors:
        tile = add_places(tile, "sec", [step])
        if step == 2:
            keep, received = sums[0]
            received, tile = lax.optimization_barrier((received, tile))
            sums[0] = (keep, received)
        step *= 2
    step = 2
    while 2 * step < shares:
        tile = add_places(tile, "term", [step])
        step *= 2
    nearby = [swap(tile, "term", 1), swap(tile, "term", 1 | step)]

    parts = []
    for chunk, size in enumerate(sizes):
        keep, received = sums[chunk]
        if chunk:
            received, send = lax.optimization_barrier((received, send))
        step = 1
        while 2 * step < shares:
            step *= 2
            count = shares // (2 * step)
            last = count == 1 and chunk == len(sizes) - 1
            operands = (keep, received, tile) if last else (keep, received)
            lines = trials * size * rows + 2 * TILE[0]
            keep, send = call(
                halve_last_kernel if last else halve_kernel,
                "halve_rows",
                1,
                1,
                8 * MIB,
                out_shape=(
                    share_of(count, size, jnp.float32),
                    jax.ShapeDtypeStruct((lines, states), jnp.bfloat16)
                    if last
                    else share_of(count, size, jnp.bfloat16),
                ),
                in_specs=[VMEM] * len(operands),
                out_specs=(VMEM, VMEM),
            )(*operands)
            received = swap(send, "term", step)
        parts += [keep, received]

    done = []
    for chunk, size in enumerate(sizes[:-1]):
        done.append(
            call(
                add_last_kernel,
                "add_last_share",
                10**8,
                1,
                8 * MIB,
                out_shape=jax.ShapeDtypeStruct((trials, size, rows, states), jnp.bfloat16),
                in_specs=[VMEM, VMEM],
                out_specs=VMEM,
            )(*parts[2 * chunk : 2 * chunk + 2])
        )
    products, rayleigh = call(
        finish_kernel,
        "finish",
        1,
        1,
        8 * MIB,
        out_shape=(
            jax.ShapeDtypeStruct((trials, pairs, rows, states), jnp.bfloat16),
            jax.ShapeDtypeStruct((trials, trials), jnp.float32),
        ),
        in_specs=[VMEM] * (len(done) + 5),
        out_specs=(HBM, HBM),
        scratch_shapes=[
            pltpu.VMEM((trials, sizes[-1], rows, states), jnp.bfloat16),
            pltpu.VMEM((trials, trials), jnp.float32),
            pltpu.SemaphoreType.DMA((len(sizes) + 1,)),
        ],
    )(*done, *parts[-2:], tile, *nearby)
    return (products[:, None], rayleigh)


def solution(mesh):
    in_specs = (
        P(None, "sec", None, None, None),
        P("term", "sec", None, None),
        P("term", "sec", None, None),
        P("term", None),
    )
    out_specs = (P(None, "sec", None, "term", None), P())
    return jax.shard_map(local, mesh=mesh, in_specs=in_specs, out_specs=out_specs, check_vma=False)
```

```python
import functools

import jax
import jax.numpy as jnp
from jax import lax
from jax.experimental import pallas as pl
from jax.experimental.pallas import tpu as pltpu
from jax.sharding import PartitionSpec as P

MIB = 1 << 20
TILE = (8, 128)
VMEM = pl.BlockSpec(memory_space=pltpu.VMEM)
SMEM = pl.BlockSpec(memory_space=pltpu.SMEM)
HBM = pl.BlockSpec(memory_space=pltpu.HBM)


def swap(value, axis, mask, count=None):
    masks = [mask, mask] if count is None else [turned(mask, parity, count) for parity in range(2)]
    places = range(lax.axis_size(axis))
    return lax.ppermute(value, axis, [(place, place ^ masks[place & 1]) for place in places])


def turned(mask, parity, count):
    bits = count.bit_length() - 1
    if parity:
        return mask
    return sum(1 << (bits - bit) for bit in range(1, bits) if mask >> bit & 1) | mask & 1


def gather_sectors(own, sectors, after):
    held = {0: own}
    for mask in range(2, sectors, 2):
        step = 1 << (mask.bit_length() - 1)
        sent = after(own) if mask == 4 else held[mask ^ step]
        held[mask] = swap(sent, "sec", step, sectors)
    return [block for mine in held.values() for block in (mine, swap(mine, "sec", 1))]


def place_rows(values):
    row = lax.broadcasted_iota(jnp.int32, TILE, 0)
    tile = jnp.zeros(TILE, jnp.float32)
    for position, value in values:
        tile = jnp.where(row == position, value, tile)
    return tile


def total(value):
    return jnp.sum(jnp.sum(value, axis=0, keepdims=True), axis=1, keepdims=True)


def inner_kernel(
    square_scale, vectors, left, right_hbm, offsets_hbm, inner, squares, right, offsets, sems
):
    fetches = [
        pltpu.make_async_copy(offsets_hbm, offsets, sems.at[0]),
        pltpu.make_async_copy(right_hbm, right, sems.at[1]),
    ]
    for fetch in fetches:
        fetch.start()
    terms, states = left.shape[0], left.shape[1]
    stacked = left[...].reshape(terms * states, states)
    sums = []
    for trial in range(vectors.shape[0]):
        square = jnp.zeros((8, states), jnp.float32)
        for pair in range(vectors.shape[1]):
            block = vectors[trial, pair]
            product = jnp.dot(stacked, block, preferred_element_type=jnp.float32)
            for term in range(terms):
                part = product[term * states : (term + 1) * states].astype(jnp.bfloat16)
                inner[trial, pair, :, term * states : (term + 1) * states] = part
            wide = block.astype(jnp.float32)
            square += jnp.sum((wide * wide).reshape(-1, 8, states), axis=0)
        sums.append(total(square) * square_scale)
    trials = len(sums)
    squares[...] = place_rows([(trials * trials + k, value) for k, value in enumerate(sums)])
    for fetch in fetches:
        fetch.wait()


def place_blocks(sectors, pieces, rights):
    odd = lax.axis_index("sec") & 1
    for mask in range(0, sectors, 2):
        even_place, odd_place = turned(mask, 0, sectors), turned(mask, 1, sectors)
        rights[jnp.where(odd == 1, odd_place, even_place)] = pieces[mask][...]
        if mask + 1 < len(pieces):
            rights[jnp.where(odd == 1, even_place, odd_place) ^ 1] = pieces[mask + 1][...]
    rights[sectors - 1] = jnp.zeros(rights.shape[1:], rights.dtype)


def needed_mask(sectors, offsets, term, pair):
    sector = lax.axis_index("sec")
    return sector ^ ((sector + offsets[term, pair]) & (sectors - 1))


def times_right(inner, term, pair, block):
    trials, _, states, _ = inner.shape
    lines = inner[:, pair, :, term * states : (term + 1) * states]
    product = jnp.dot(
        lines.reshape(trials * states, states), block, preferred_element_type=jnp.float32
    )
    return product.reshape(trials, states, states)


def sum_terms(sectors, pair, offsets, inner, rights):
    result = None
    for term in range(rights.shape[1]):
        mask = needed_mask(sectors, offsets, term, pair)
        added = times_right(inner, term, pair, rights[mask, term])
        result = added if result is None else result + added
    return result


def add_gram(vectors, pair, values, grams):
    trials, states = vectors.shape[0], vectors.shape[-1]
    for j in range(trials):
        for i in range(trials):
            spread = vectors[i, pair].astype(jnp.float32) * values[j]
            grams[i * trials + j] += jnp.sum(spread.reshape(-1, 8, states), axis=0)


def write_tile(before, grams, tile):
    count = grams.shape[0]
    tile[...] = before[...] + place_rows([(k, total(grams[k])) for k in range(count)])


def write_shares(whole, slot, keep, send):
    shares = 2 * keep.shape[0]
    rows = whole.shape[1] // shares
    place = lax.axis_index("term")
    for mask in range(shares):
        start = pl.multiple_of((place ^ mask) * rows, rows)
        share = whole[:, pl.ds(start, rows)]
        if mask & 1:
            send[mask // 2, :, slot] = share.astype(jnp.bfloat16)
        else:
            keep[mask // 2, :, slot] = share


def early_kernel(sectors, offsets, vectors, inner, before, *rest):
    *pieces, partial, tile, rights, grams = rest
    place_blocks(sectors, pieces, rights)
    grams[...] = jnp.zeros_like(grams)
    for pair in range(partial.shape[0]):
        partial[pair] = sum_terms(sectors, pair, offsets, inner, rights)
        add_gram(vectors, pair, partial[pair], grams)
    write_tile(before, grams, tile)


def late_kernel(sectors, offsets, vectors, inner, before, partial, last, *rest):
    keep, send, tile, whole, grams = rest
    grams[...] = jnp.zeros_like(grams)
    for pair in range(partial.shape[0]):
        lacks = [
            needed_mask(sectors, offsets, term, pair) == sectors - 1
            for term in range(last.shape[0])
        ]
        lacking = functools.reduce(jnp.logical_or, lacks)

        @pl.when(jnp.logical_not(lacking))
        def _():
            write_shares(partial.at[pair], pair, keep, send)

        @pl.when(lacking)
        def _():
            whole[...] = partial[pair]
            for term, lack in enumerate(lacks):

                @pl.when(lack)
                def _():
                    added = times_right(inner, term, pair, last[term])
                    whole[...] += added
                    add_gram(vectors, pair, added, grams)

            write_shares(whole, pair, keep, send)

    write_tile(before, grams, tile)


def other_kernel(sectors, first, offsets, vectors, inner, before, rights, last, *rest):
    keep, send, tile, whole, grams = rest
    grams[...] = jnp.zeros_like(grams)
    for slot in range(keep.shape[2]):
        pair = first + slot
        whole[slot] = sum_terms(sectors, pair, offsets, inner, rights)
        for term in range(last.shape[0]):

            @pl.when(needed_mask(sectors, offsets, term, pair) == sectors - 1)
            def _():
                whole[slot] += times_right(inner, term, pair, last[term])

    for slot in range(keep.shape[2]):
        add_gram(vectors, first + slot, whole[slot], grams)
        write_shares(whole.at[slot], slot, keep, send)
    write_tile(before, grams, tile)


def halve_last_kernel(kept, received, tile, keep, send):
    keep[0] = kept[0] + received[0].astype(jnp.float32)
    both = kept[1] + received[1].astype(jnp.float32)
    lines = send.shape[0] - 2 * TILE[0]
    send[:lines] = both.astype(jnp.bfloat16).reshape(lines, send.shape[1])
    left, parts = tile[...], []
    for _ in range(3):
        parts.append(left.astype(jnp.bfloat16).astype(jnp.float32))
        left = left - parts[-1]
    block = jnp.concatenate(
        [
            jnp.concatenate([parts[0], parts[1]], axis=0),
            jnp.concatenate([parts[2], jnp.zeros_like(left)], axis=0),
        ],
        axis=1,
    )
    send[lines:] = block.astype(jnp.bfloat16)


def halve_kernel(kept, received, keep, send):
    for k in range(kept.shape[0]):
        both = kept[k] + received[k].astype(jnp.float32)
        if k & 1:
            send[k // 2] = both.astype(jnp.bfloat16)
        else:
            keep[k // 2] = both


def ridden_tile(received):
    height, width = TILE
    block = received[received.shape[0] - 2 * height :].astype(jnp.float32)
    return block[:height, :width] + block[height:, :width] + block[:height, width:]


def add_last_kernel(kept, received, result):
    result[...] = (kept[0] + received[0].astype(jnp.float32)).astype(jnp.bfloat16)


def finish_kernel(*refs):
    *done, kept, received, tile, near, far, products, rayleigh_hbm, rows, rayleigh, sems = refs
    copies, first = [], 0
    for part in [*done, rows]:
        target = products.at[:, pl.ds(first, part.shape[1])]
        copies.append(pltpu.make_async_copy(part, target, sems.at[len(copies)]))
        first += part.shape[1]
    for copy in copies[:-1]:
        copy.start()
    lines = received.shape[0] - 2 * TILE[0]
    both = received[:lines].astype(jnp.float32).reshape(kept.shape[1:])
    rows[...] = (kept[0] + both).astype(jnp.bfloat16)
    copies[-1].start()

    tile = tile[...] + near[...] + far[...] + ridden_tile(received)
    trials = rayleigh.shape[0]
    row = lax.broadcasted_iota(jnp.int32, rayleigh.shape, 0)
    column = lax.broadcasted_iota(jnp.int32, rayleigh.shape, 1)

    def entry(position):
        return tile[position : position + 1, :trials]

    result = jnp.zeros(rayleigh.shape, jnp.float32)
    for i in range(trials):
        for j in range(trials):
            squares = entry(trials * trials + i) * entry(trials * trials + j)
            value = entry(i * trials + j) / jnp.sqrt(squares)
            result = jnp.where((row == i) & (column == j), value, result)
    rayleigh[...] = result
    last = pltpu.make_async_copy(rayleigh, rayleigh_hbm, sems.at[len(copies)])
    last.start()
    for copy in [*copies, last]:
        copy.wait()


def in_hbm(value):
    return pltpu.with_memory_space_constraint(value, pltpu.HBM)


def add_places(tile, axis, masks):
    parts = [tile] + [swap(tile, axis, mask) for mask in masks]
    return sum(parts[1:], parts[0])


def call(kernel, name, flops, moved, limit, **kwargs):
    return pl.pallas_call(
        kernel,
        name=name,
        cost_estimate=pl.CostEstimate(flops=flops, bytes_accessed=moved, transcendentals=0),
        compiler_params=pltpu.CompilerParams(vmem_limit_bytes=limit),
        **kwargs,
    )


def local(vectors, left_ops, right_ops, offsets):
    sectors = lax.axis_size("sec")
    shares = lax.axis_size("term")
    trials, _, pairs, states, _ = vectors.shape
    terms = left_ops.shape[0]
    vectors, left, right = vectors[:, 0], left_ops[:, 0], right_ops[:, 0]
    rows = states // shares

    inner, tile, own, offsets = call(
        functools.partial(inner_kernel, 1.0 / shares),
        "inner_products",
        2 * terms * trials * pairs * states**3,
        5 * MIB,
        12 * MIB,
        out_shape=(
            jax.ShapeDtypeStruct((trials, pairs, states, terms * states), jnp.bfloat16),
            jax.ShapeDtypeStruct(TILE, jnp.float32),
            jax.ShapeDtypeStruct(right.shape, jnp.bfloat16),
            jax.ShapeDtypeStruct(offsets.shape, offsets.dtype),
        ),
        in_specs=[VMEM, VMEM, HBM, HBM],
        out_specs=(VMEM, VMEM, VMEM, VMEM),
        scratch_shapes=[pltpu.SemaphoreType.DMA((2,))],
    )(vectors, left, in_hbm(right), in_hbm(offsets))

    def behind_inner(block):
        return lax.optimization_barrier((block, inner))[0]

    gathered = gather_sectors(right, sectors, behind_inner)
    gathered[0] = own

    def share_of(count, size, dtype):
        return jax.ShapeDtypeStruct((count, trials, size, rows, states), dtype)

    tile_shape = jax.ShapeDtypeStruct(TILE, jnp.float32)
    rights_shape = jax.ShapeDtypeStruct((sectors, terms, states, states), jnp.bfloat16)
    sizes = [pairs - 2 * (pairs // 4), pairs // 4, pairs // 4]
    grams = pltpu.VMEM((trials * trials, 8, states), jnp.float32)
    *early, last = gathered
    partial, tile, rights = call(
        functools.partial(early_kernel, sectors),
        "early_products",
        2 * terms * trials * sizes[0] * states**3,
        4 * MIB,
        12 * MIB,
        out_shape=(
            jax.ShapeDtypeStruct((sizes[0], trials, states, states), jnp.float32),
            tile_shape,
            rights_shape,
        ),
        in_specs=[SMEM, VMEM, VMEM, VMEM] + [VMEM] * len(early),
        out_specs=(VMEM, VMEM, VMEM),
        scratch_shapes=[grams],
    )(offsets, vectors, inner, tile, *early)

    def sums_of(kernel, name, flops, size, scratch, *operands):
        return call(
            kernel,
            name,
            flops,
            MIB,
            12 * MIB,
            out_shape=(
                share_of(shares // 2, size, jnp.float32),
                share_of(shares // 2, size, jnp.bfloat16),
                tile_shape,
            ),
            in_specs=[SMEM] + [VMEM] * len(operands),
            out_specs=(VMEM, VMEM, VMEM),
            scratch_shapes=[pltpu.VMEM((*scratch, states, states), jnp.float32), grams],
        )(offsets, *operands)

    keep, send, tile = sums_of(
        functools.partial(late_kernel, sectors),
        "late_products",
        terms * trials * sizes[0] * states**3 // 4,
        sizes[0],
        (trials,),
        vectors,
        inner,
        tile,
        partial,
        last,
    )
    sums = [(keep, swap(send, "term", 1))]
    first = sizes[0]
    for size in sizes[1:]:
        keep, send, tile = sums_of(
            functools.partial(other_kernel, sectors, first),
            "other_products",
            2 * terms * trials * size * states**3,
            size,
            (size, trials),
            vectors,
            inner,
            tile,
            rights,
            last,
        )
        sums.append((keep, swap(send, "term", 1)))
        first += size

    step = 1
    while step < sectors:
        tile = add_places(tile, "sec", [step])
        if step == 2:
            keep, received = sums[0]
            received, tile = lax.optimization_barrier((received, tile))
            sums[0] = (keep, received)
        step *= 2
    step = 2
    while 2 * step < shares:
        tile = add_places(tile, "term", [step])
        step *= 2
    nearby = [swap(tile, "term", 1), swap(tile, "term", 1 | step)]

    parts = []
    for chunk, size in enumerate(sizes):
        keep, received = sums[chunk]
        if chunk:
            received, send = lax.optimization_barrier((received, send))
        step = 1
        while 2 * step < shares:
            step *= 2
            count = shares // (2 * step)
            last = count == 1 and chunk == len(sizes) - 1
            operands = (keep, received, tile) if last else (keep, received)
            lines = trials * size * rows + 2 * TILE[0]
            keep, send = call(
                halve_last_kernel if last else halve_kernel,
                "halve_rows",
                1,
                1,
                8 * MIB,
                out_shape=(
                    share_of(count, size, jnp.float32),
                    jax.ShapeDtypeStruct((lines, states), jnp.bfloat16)
                    if last
                    else share_of(count, size, jnp.bfloat16),
                ),
                in_specs=[VMEM] * len(operands),
                out_specs=(VMEM, VMEM),
            )(*operands)
            received = swap(send, "term", step)
        parts += [keep, received]

    done = []
    for chunk, size in enumerate(sizes[:-1]):
        done.append(
            call(
                add_last_kernel,
                "add_last_share",
                [10**10,1][chunk],
                1,
                8 * MIB,
                out_shape=jax.ShapeDtypeStruct((trials, size, rows, states), jnp.bfloat16),
                in_specs=[VMEM, VMEM],
                out_specs=VMEM,
            )(*parts[2 * chunk : 2 * chunk + 2])
        )
    products, rayleigh = call(
        finish_kernel,
        "finish",
        1,
        1,
        8 * MIB,
        out_shape=(
            jax.ShapeDtypeStruct((trials, pairs, rows, states), jnp.bfloat16),
            jax.ShapeDtypeStruct((trials, trials), jnp.float32),
        ),
        in_specs=[VMEM] * (len(done) + 5),
        out_specs=(HBM, HBM),
        scratch_shapes=[
            pltpu.VMEM((trials, sizes[-1], rows, states), jnp.bfloat16),
            pltpu.VMEM((trials, trials), jnp.float32),
            pltpu.SemaphoreType.DMA((len(sizes) + 1,)),
        ],
    )(*done, *parts[-2:], tile, *nearby)
    return (products[:, None], rayleigh)


def solution(mesh):
    in_specs = (
        P(None, "sec", None, None, None),
        P("term", "sec", None, None),
        P("term", "sec", None, None),
        P("term", None),
    )
    out_specs = (P(None, "sec", None, "term", None), P())
    return jax.shard_map(local, mesh=mesh, in_specs=in_specs, out_specs=out_specs, check_vma=False)
```
